32 devices in a mesh: section: 2 (over core), dp: 16 (over z, y, x).
Axes of the slice: x: 2, y: 2, z: 4, core: 2. Of those that a mesh axis runs over, the one named last changes fastest.
Arguments:
- tokens: bfloat16 [2, 16, 512, 1024], P(None, 'dp'), may hold values from -6 to 6
- segment_ids: int32 [2, 16, 512], P(None, 'dp'), may hold values from 0 to 63, as said below
- row_lengths: int32 [2, 16], P(None, 'dp'), may hold values from 256 to 512, as said below
- w_qkv: bfloat16 [2, 1024, 3072], P('section', 'dp'), may hold values from -0.1875 to 0.1875
- w_out: bfloat16 [2, 1024, 1024], P('section', 'dp'), may hold values from -1 to 1
- w_in: bfloat16 [2, 1024, 4096], P('section', 'dp'), may hold values from -0.1875 to 0.1875
- w_ffn_out: bfloat16 [2, 4096, 1024], P('section', 'dp'), may hold values from -0.09375 to 0.09375
- bias_q: float32 [2, 1024], P('section'), may hold values from -1.75 to 1.75
- bias_v: float32 [2, 1024], P('section'), may hold values from -0.3125 to 0.3125
- bias_out: float32 [2, 1024], P('section'), may hold values from -1.75 to 1.75
- bias_in: float32 [2, 4096], P('section'), may hold values from -1.75 to 1.75
- bias_ffn_out: float32 [2, 1024], P('section'), may hold values from -1.75 to 1.75
- ln_gain: float32 [2, 2, 1024], P('section'), may hold values from 0.25 to 1.75
- ln_shift: float32 [2, 2, 1024], P('section'), may hold values from -1.75 to 1.75
- out_cotangent: bfloat16 [2, 16, 512, 1024], P(None, 'dp'), may hold values from -6 to 6
Outputs:
- layer_out: bfloat16 [2, 2, 16, 512, 1024], P('section', None, 'dp')
- input_grad: bfloat16 [2, 2, 16, 512, 1024], P('section', None, 'dp')
- grad_bias_q: float32 [2, 1024], P('section')
- grad_bias_v: float32 [2, 1024], P('section')
- grad_bias_out: float32 [2, 1024], P('section')
- grad_bias_in: float32 [2, 4096], P('section')
- grad_bias_ffn_out: float32 [2, 1024], P('section')
The draws below stay inside these ranges and needn't reach their ends.
Inputs may be any that keep to these rules, and one draw needn't show every extreme that they name: `segment_ids`: in each row the numbers start at 0 and never fall along the row; a run of equal numbers is one packed item. `row_lengths`: some row of every draw is full.
All inputs are finite; a program needn't handle non-finite values.
Results may differ from the reference program's by a relative error of at most 0.02.
Values may be sent and summed in bfloat16 or wider, within the bound.
A program may use at most 112 MiB of HBM per device.

```python
import math
import jax
import jax.numpy as jnp
from jax import lax

D = 1024
HEADS = 16
HEAD_DIM = 64
FF = 4096
SEQ = 512
MICRO = 2
LAYERS = 2
ROWS = 16


def draw_segment_ids(key, part):
    key = jax.random.fold_in(key, 11)
    rate_key, flag_key = jax.random.split(key)
    rates = jax.random.randint(rate_key, (MICRO, ROWS, 1), 16, 129)
    flags = jax.random.randint(flag_key, (MICRO, ROWS, SEQ), 0, 1 << 20) % rates
    starts = (flags == 0).astype(jnp.int32)
    positions = jnp.arange(SEQ, dtype=jnp.int32)
    regular = (positions % 8 == 0).astype(jnp.int32)
    starts = starts.at[0, 0].set(regular)
    starts = starts.at[:, :, 0].set(0)
    numbers = jnp.cumsum(starts, axis=-1)
    return jnp.minimum(numbers, SEQ // 8 - 1).astype(jnp.int32)


def draw_row_lengths(key, part):
    key = jax.random.fold_in(key, 12)
    lengths = jax.random.randint(key, (MICRO, ROWS), SEQ // 2, SEQ + 1)
    return lengths.at[0, 0].set(SEQ).astype(jnp.int32)


def steps_of(key, dims, cuts, least, high):
    gain, own = 1.0, jax.random.fold_in(key, 6)
    for axis_at, blocks in cuts:
        steps = jnp.exp(jax.random.uniform(jax.random.fold_in(own, axis_at), (blocks,), jnp.float32, least / len(cuts), high / len(cuts)))
        gain = gain * jnp.repeat(steps, dims[axis_at] // blocks).reshape([-1 if axis == axis_at else 1 for axis in range(len(dims))])
    return gain


def scatter_about(stream_key, shape, spread, reach, pieces=(), kind=jnp.bfloat16):
    drawn = spread * jax.random.normal(stream_key, shape, jnp.float32)
    if pieces:
        drawn = drawn * steps_of(stream_key, shape, pieces, -0.22, 0.18)
    return jnp.clip(drawn, -reach, reach).astype(kind)


def setup_inputs(seed: int = 0) -> dict:
    key_list = jax.random.split(jax.random.key(seed), 16)
    tokens = scatter_about(key_list[0], (MICRO, ROWS, SEQ, D), 1.0, 6.0, ((1, 16),))
    segment_ids = draw_segment_ids(jax.random.fold_in(key_list[15], 71), 0)
    row_lengths = draw_row_lengths(jax.random.fold_in(key_list[15], 71), 0)
    w_qkv = scatter_about(key_list[3], (LAYERS, D, 3 * D), D ** -0.5, 0.1875, ((0, 2), (1, 16)))
    w_out = scatter_about(key_list[4], (LAYERS, D, D), (D // 32) ** -0.5, 1.0, ((0, 2), (1, 16)))
    w_in = scatter_about(key_list[5], (LAYERS, D, FF), D ** -0.5, 0.1875, ((0, 2), (1, 16)))
    w_ffn_out = scatter_about(key_list[6], (LAYERS, FF, D), FF ** -0.5, 0.09375, ((0, 2), (1, 16)))
    bias_q = scatter_about(key_list[7], (LAYERS, D), 0.3, 1.75, ((0, 2),), jnp.float32)
    bias_v = scatter_about(key_list[8], (LAYERS, D), 0.05, 0.3125, ((0, 2),), jnp.float32)
    bias_out = scatter_about(key_list[9], (LAYERS, D), 0.3, 1.75, ((0, 2),), jnp.float32)
    bias_in = scatter_about(key_list[10], (LAYERS, FF), 0.3, 1.75, ((0, 2),), jnp.float32)
    bias_ffn_out = scatter_about(key_list[11], (LAYERS, D), 0.3, 1.75, ((0, 2),), jnp.float32)
    ln_gain = jnp.clip(1.0 + 0.15 * jax.random.normal(key_list[12], (LAYERS, 2, D), jnp.float32), 0.25, 1.75)
    ln_shift = scatter_about(key_list[13], (LAYERS, 2, D), 0.3, 1.75, ((0, 2),), jnp.float32)
    out_cotangent = scatter_about(key_list[14], (MICRO, ROWS, SEQ, D), 1.0, 6.0, ((1, 16),))
    return {"tokens": tokens, "segment_ids": segment_ids, "row_lengths": row_lengths, "w_qkv": w_qkv, "w_out": w_out, "w_in": w_in, "w_ffn_out": w_ffn_out, "bias_q": bias_q, "bias_v": bias_v, "bias_out": bias_out, "bias_in": bias_in, "bias_ffn_out": bias_ffn_out, "ln_gain": ln_gain, "ln_shift": ln_shift, "out_cotangent": out_cotangent}


@jax.custom_vjp
def low(v):
    return lax.optimization_barrier(v.astype(jnp.bfloat16)).astype(jnp.float32)

@jax.custom_vjp
def low_back(v):
    return v

def low_keep(v):
    return (low(v), None)

def low_pass(kept, grad):
    return (grad,)

def back_keep(v):
    return (v, None)

def back_low(kept, grad):
    return (low(grad),)
low.defvjp(low_keep, low_pass)
low_back.defvjp(back_keep, back_low)
epsilon = 1e-06
highest = lax.Precision.HIGHEST

def project(inputs, matrix):
    return jnp.einsum('gsd,de->gse', inputs, matrix, precision=highest)

def normalize(residual):
    average = lax.optimization_barrier(jnp.mean(residual, -1, keepdims=True))
    centered = residual - average
    return centered * lax.rsqrt(lax.optimization_barrier(jnp.mean(centered * centered, -1, keepdims=True)) + epsilon)

def pair_mask(segments, lengths):
    positions = jnp.arange(segments.shape[-1], dtype=jnp.int32)
    is_valid = positions[None, :] < lengths[:, None]
    same_item = segments[:, :, None] == segments[:, None, :]
    return same_item & (is_valid[:, :, None] == is_valid[:, None, :])

def layer_apply(inputs, biases, matrices, gain_rows, shifts, allowed):
    bias_query, bias_value, bias_attn, bias_hidden, bias_final = biases
    mat_qkv, mat_attn, mat_hidden, mat_final = matrices
    group_rows, seq_len, model_width = inputs.shape
    projected = project(inputs, mat_qkv) + jnp.concatenate([bias_query, jnp.zeros_like(bias_query), bias_value])
    projected = low(low_back(projected)).reshape(group_rows, seq_len, 3, HEADS, HEAD_DIM)
    queries = projected[:, :, 0]
    key_rows = projected[:, :, 1]
    values = projected[:, :, 2]
    scale_factor = 1.0 / math.sqrt(HEAD_DIM)
    scores = low_back(jnp.einsum('gqhd,gkhd->ghqk', queries, key_rows, precision=highest) * scale_factor)
    scores = jnp.where(allowed[:, None], scores, -1000000000.0)
    attn_probs = jax.nn.softmax(scores, axis=-1)
    context = jnp.einsum('ghqk,gkhd->gqhd', low(attn_probs), values, precision=highest)
    context = low(low_back(context)).reshape(group_rows, seq_len, model_width)
    attn_out = low_back(project(context, mat_attn) + bias_attn)
    hidden = low(low_back(normalize(inputs + attn_out) * gain_rows[0] + shifts[0]))
    pre_gelu = low_back(project(hidden, mat_hidden) + bias_hidden)
    activated = low(jax.nn.gelu(pre_gelu, approximate=False))
    ffn_out = low_back(project(activated, mat_final) + bias_final)
    return normalize(hidden + ffn_out) * gain_rows[1] + shifts[1]

def reference(tokens, segment_ids, row_lengths, w_qkv, w_out, w_in, w_ffn_out, bias_q, bias_v, bias_out, bias_in, bias_ffn_out, ln_gain, ln_shift, out_cotangent):
    floats = jnp.float32
    levels = []
    for level_index in range(2):
        matrices = tuple((matrix[level_index].astype(floats) for matrix in (w_qkv, w_out, w_in, w_ffn_out)))
        biases = tuple((vector[level_index].astype(floats) for vector in (bias_q, bias_v, bias_out, bias_in, bias_ffn_out)))
        levels.append((matrices, biases, ln_gain[level_index].astype(floats), ln_shift[level_index].astype(floats)))
    group_rows = 8
    group_count = MICRO * ROWS // group_rows
    scanned_inputs = (tokens.reshape(group_count, group_rows, SEQ, D), segment_ids.reshape(group_count, group_rows, SEQ), row_lengths.reshape(group_count, group_rows), out_cotangent.reshape(group_count, group_rows, SEQ, D))

    def one_group(totals, scanned):
        block_tokens, block_segments, block_lengths, block_cot = scanned
        allowed = pair_mask(block_segments, block_lengths)

        def lower_layer(layer_in, *biases):
            return layer_apply(layer_in, biases, levels[0][0], levels[0][2], levels[0][3], allowed)

        def upper_layer(layer_in, *biases):
            return layer_apply(layer_in, biases, levels[1][0], levels[1][2], levels[1][3], allowed)
        out_lower, back_lower = jax.vjp(lower_layer, block_tokens.astype(floats), *levels[0][1])
        lower_sent = out_lower.astype(jnp.bfloat16)
        out_upper, back_upper = jax.vjp(upper_layer, lower_sent.astype(floats), *levels[1][1])
        grads_upper = back_upper(block_cot.astype(floats))
        upper_in = grads_upper[0].astype(jnp.bfloat16)
        grads_lower = back_lower(upper_in.astype(floats))
        totals = tuple((tuple((running + update for running, update in zip(earlier, fresh[1:]))) for earlier, fresh in zip(totals, (grads_lower, grads_upper))))
        return (totals, (lower_sent, out_upper.astype(jnp.bfloat16), grads_lower[0].astype(jnp.bfloat16), upper_in))
    start = tuple((tuple((jnp.zeros_like(vector) for vector in levels[level_index][1])) for level_index in range(2)))
    totals, (out_low, out_high, grad_low, grad_high) = lax.scan(one_group, start, scanned_inputs)
    layer_out = jnp.stack([out_low, out_high]).reshape(2, MICRO, ROWS, SEQ, D)
    input_grad = jnp.stack([grad_low, grad_high]).reshape(2, MICRO, ROWS, SEQ, D)
    stacked = tuple((jnp.stack([totals[0][index], totals[1][index]]) for index in range(5)))
    return (layer_out, input_grad, stacked[0], stacked[1], stacked[2], stacked[3], stacked[4])
```

```python
from functools import partial
import math

import jax
import jax.numpy as jnp
from jax import lax
from jax.experimental import pallas as pl
from jax.experimental.pallas import tpu as pltpu
from jax.sharding import PartitionSpec as P

HEAD_DIM = 64
SEQ = 512
epsilon = 1e-06
VMEM_LIMIT = 60 * 2**20

MESH = pl.DeviceIdType.MESH
LANES = 1024
BLOCK = 64
HALF = BLOCK // 2
CUT = 384
STAGES = (0, 1, 2, 3, 4, 6)


LOAD = 7


def link_plan(
    items, wq, wo, wi, wf, own_vec, full, vec, vec_sem, stage, in_sem, place_sem, cross_send, cross_recv, send_sem, recv_sem
):
    sec = lax.axis_index("section")
    chip = lax.axis_index("dp")
    z = chip // 4
    y = (chip // 2) % 2
    x = chip % 2
    dev_x = (sec, z * 4 + y * 2 + 1 - x)
    dev_y = (sec, z * 4 + (1 - y) * 2 + x)
    dev_up = (sec, jnp.minimum(z + 1, 3) * 4 + y * 2 + x)
    dev_down = (sec, jnp.maximum(z - 1, 0) * 4 + y * 2 + x)
    dev_core = (1 - sec, chip)
    per_layer = items // 2

    def own_block(b, row):
        if b < 3:
            return wq.at[0, pl.ds(row, HALF), b * LANES : (b + 1) * LANES]
        if b == 3:
            return wo.at[0, pl.ds(row, HALF), :]
        if b < 8:
            return wi.at[0, pl.ds(row, HALF), (b - 4) * LANES : (b - 3) * LANES]
        return wf.at[0, pl.ds((b - 8) * BLOCK + row, HALF), :]

    mine = pl.multiple_of(sec * HALF, HALF)
    other = pl.multiple_of((1 - sec) * HALF, HALF)

    def to_stage(b):
        return pltpu.make_async_copy(own_block(b, mine), stage.at[b], in_sem.at[b])

    def to_place(b):
        return pltpu.make_async_copy(
            stage.at[b], full.at[sec * per_layer + b, z, y, x, pl.ds(mine, HALF), :], place_sem.at[b]
        )

    def cross(b):
        return pltpu.make_async_remote_copy(
            src_ref=own_block(b, other),
            dst_ref=full.at[sec * per_layer + b, z, y, x, pl.ds(other, HALF), :],
            send_sem=cross_send.at[b],
            recv_sem=cross_recv.at[b],
            device_id=dev_core,
            device_id_type=MESH,
        )

    take_vec = pltpu.make_async_copy(own_vec, vec.at[sec], vec_sem.at[0])
    give_vec = pltpu.make_async_remote_copy(
        src_ref=own_vec,
        dst_ref=vec.at[sec],
        send_sem=vec_sem.at[1],
        recv_sem=vec_sem.at[2],
        device_id=dev_core,
        device_id_type=MESH,
    )

    def begin():
        for b in range(per_layer):
            to_stage(b).start()
        take_vec.start()
        barrier = pltpu.get_barrier_semaphore()
        for device in (dev_x, dev_y, dev_core):
            pl.semaphore_signal(barrier, inc=1, device_id=device, device_id_type=MESH)

        @pl.when(z < 3)
        def _():
            pl.semaphore_signal(barrier, inc=1, device_id=dev_up, device_id_type=MESH)

        @pl.when(z > 0)
        def _():
            pl.semaphore_signal(barrier, inc=1, device_id=dev_down, device_id_type=MESH)

        pl.semaphore_wait(barrier, 3 + jnp.minimum(z, 1) + jnp.minimum(3 - z, 1))
        for b in range(per_layer):
            cross(b).start()
        for b in range(per_layer):
            to_stage(b).wait()
            to_place(b).start()
        give_vec.start()
        take_vec.wait()
        give_vec.wait_send()
        theirs = vec.at[1 - sec]
        pltpu.make_async_remote_copy(
            src_ref=theirs,
            dst_ref=theirs,
            send_sem=vec_sem.at[1],
            recv_sem=vec_sem.at[2],
            device_id=dev_core,
            device_id_type=MESH,
        ).wait_recv()

    def copy(ref, kind, item, device):
        return pltpu.make_async_remote_copy(
            src_ref=ref,
            dst_ref=ref,
            send_sem=send_sem.at[kind],
            recv_sem=recv_sem.at[kind, item],
            device_id=device,
            device_id_type=MESH,
        )

    def views(core):
        rows = slice(core * HALF, (core + 1) * HALF)
        first, last = slice(0, CUT), slice(CUT, LANES)
        if core == 0:
            pair = lambda i, at: full.at[i, at, :, x, rows, last]
            eight_first = lambda i: full.at[i, :, y, :, rows, first]
            eight_last = lambda i: full.at[i, :, :, x, rows, last]
            towards = (dev_x, dev_y)
        else:
            pair = lambda i, at: full.at[i, at, y, :, rows, last]
            eight_first = lambda i: full.at[i, :, :, x, rows, first]
            eight_last = lambda i: full.at[i, :, y, :, rows, last]
            towards = (dev_y, dev_x)
        return (
            towards,
            lambda i, at: full.at[i, at, y, x, rows, first],
            lambda i: full.at[i, :, y, x, rows, first],
            eight_first,
            lambda i, at: full.at[i, at, y, x, rows, last],
            pair,
            eight_last,
            lambda i: full.at[i, :, :, :, rows, :],
        )

    def z_send(base, block, hop, item, at):
        if at < 3 and at - (hop - 1) >= 0:
            copy(block(item, at - (hop - 1)), base + hop - 1, item, dev_up).start()
        if at > 0 and at + (hop - 1) <= 3:
            copy(block(item, at + (hop - 1)), base + 2 + hop, item, dev_down).start()

    def z_recv(base, block, hop, item, at):
        if at - hop >= 0:
            copy(block(item, at - hop), base + hop - 1, item, dev_up).wait_recv()
        if at + hop <= 3:
            copy(block(item, at + hop), base + 2 + hop, item, dev_down).wait_recv()

    def step_at(t, at, core):
        (dev_u, dev_v), own_a, col_a, eight_a, own_d, pair_d, eight_d, whole = views(core)
        turns = [t - offset for offset in STAGES]

        def live(item):
            return (item >= 0) & (item < items)

        item = turns[0]

        @pl.when(live(item))
        def _():
            layer, b = item // per_layer, item % per_layer

            @pl.when(layer == core)
            def _():
                pltpu.make_async_copy(
                    stage.at[b], full.at[item, z, y, x, pl.ds(core * HALF, HALF), :], place_sem.at[b]
                ).wait()

            @pl.when(layer != core)
            def _():
                mine_there = full.at[item, z, y, x, pl.ds(core * HALF, HALF), :]
                pltpu.make_async_remote_copy(
                    src_ref=mine_there,
                    dst_ref=mine_there,
                    send_sem=cross_send.at[b],
                    recv_sem=cross_recv.at[b],
                    device_id=dev_core,
                    device_id_type=MESH,
                ).wait_recv()

            z_send(0, own_a, 1, item, at)
            copy(own_d(item, at), 8, item, dev_v).start()

        item1 = turns[1]

        @pl.when(live(item1))
        def _():
            z_recv(0, own_a, 1, item1, at)
            z_send(0, own_a, 2, item1, at)
            copy(own_d(item1, at), 8, item1, dev_v).wait_recv()
            z_send(9, pair_d, 1, item1, at)

        item2 = turns[2]

        @pl.when(live(item2))
        def _():
            z_recv(0, own_a, 2, item2, at)
            z_send(0, own_a, 3, item2, at)
            z_recv(9, pair_d, 1, item2, at)
            z_send(9, pair_d, 2, item2, at)

        item3 = turns[3]

        @pl.when(live(item3))
        def _():
            z_recv(0, own_a, 3, item3, at)
            copy(col_a(item3), 6, item3, dev_u).start()
            z_recv(9, pair_d, 2, item3, at)
            z_send(9, pair_d, 3, item3, at)

        item4 = turns[4]

        @pl.when(live(item4))
        def _():
            copy(col_a(item4), 6, item4, dev_u).wait_recv()
            copy(eight_a(item4), 7, item4, dev_v).start()
            z_recv(9, pair_d, 3, item4, at)
            copy(eight_d(item4), 15, item4, dev_u).start()

        item5 = turns[5]

        @pl.when(live(item5))
        def _():
            copy(eight_a(item5), 7, item5, dev_v).wait_recv()
            copy(eight_d(item5), 15, item5, dev_u).wait_recv()
            copy(whole(item5), 16, item5, dev_core).start()

    def step(t):
        for at in range(4):
            for core in range(2):

                @pl.when((z == at) & (sec == core))
                def _():
                    step_at(t, at, core)

    def arrived(item):
        for core in range(2):

            @pl.when(sec == core)
            def _():
                copy(views(1 - core)[-1](item), 16, item, dev_core).wait_recv()

    def end():
        for b in range(per_layer):
            cross(b).wait_send()
        for core in range(2):

            @pl.when(sec == core)
            def _():
                _, own_a, col_a, eight_a, own_d, pair_d, eight_d, whole = views(core)
                every = slice(None)

                def sent(ref, kind):
                    copy(ref, kind, 0, dev_core).wait_send()

                sent(whole(every), 16)
                sent(col_a(every), 6)
                sent(eight_a(every), 7)
                sent(eight_d(every), 15)
                sent(own_d(every, 0), 8)
                for hop in (1, 2, 3):
                    for base, block in ((0, own_a), (9, pair_d)):

                        @pl.when((z < 3) & (z - (hop - 1) >= 0))
                        def _():
                            sent(block(every, 0), base + hop - 1)

                        @pl.when((z > 0) & (z + (hop - 1) <= 3))
                        def _():
                            sent(block(every, 0), base + 2 + hop)

    return begin, step, arrived, end


def wide(ref, columns):
    block = ref[:, :, :, :, columns]
    return block.reshape(-1, block.shape[-1])


def dot_nt(left, right):
    return lax.dot_general(left, right, (((1,), (1,)), ((), ())), preferred_element_type=jnp.float32)


def dot_nn(left, right):
    return jnp.dot(left, right, preferred_element_type=jnp.float32)


def pair_bias(codes):
    down = jnp.broadcast_to(codes, (128, codes.shape[1])).T[:, :1]
    return jnp.where(down == codes, 0.0, -1000000000.0)


def lane_half(pair, half):
    lanes = lax.broadcasted_iota(jnp.int32, pair.shape, 1)
    return jnp.where((lanes < HEAD_DIM) == (half == 0), pair, jnp.zeros_like(pair))


TILE = 256


def forward_kernel(items, with_links, *refs):
    if with_links:
        wq, wo, wi, wf = refs[:4]
        refs = refs[4:]
    else:
        given, given_vec = refs[:2]
        refs = refs[2:]
    if with_links:
        own_vec, refs = refs[0], refs[1:]
    tokens, codes = refs[:2]
    refs = refs[2:]
    if with_links:
        full, refs = refs[0], refs[1:]
    else:
        full = given
    qkv_out, prob_out, ctx_out, slope_out, norm_out, inv_out, y_out, vec_out = refs[:8]
    refs = refs[8:]
    (x, vec, m_qkv, m_attn, m_hidden, m_final, qkv, ctx, hid, act, slope, acc, bias, stage_p, stage_n, stage_i) = refs[:16]
    load_sem, x_sem, vec_sem, p_sem, save_sem = refs[16:21]
    refs = refs[21:]
    sec = lax.axis_index("section")
    per_layer = items // 2

    take_x = pltpu.make_async_copy(tokens.at[sec, 0], x, x_sem.at[0])
    take_x.start()
    if with_links:
        begin_links, step_links, arrived, end_links = link_plan(items, wq, wo, wi, wf, own_vec, full, vec, vec_sem, *refs)
        begin_links()
    else:
        take_vec = pltpu.make_async_copy(given_vec, vec, vec_sem.at[0])
        take_vec.start()
        take_vec.wait()
    bias[...] = pair_bias(codes[sec])
    take_x.wait()
    put_vec = pltpu.make_async_copy(vec, vec_out, x_sem.at[1])
    put_vec.start()

    def load(item):
        b = item % per_layer

        def into(b):
            if b < 3:
                return m_qkv.at[:, :, :, :, b * LANES : (b + 1) * LANES]
            if b == 3:
                return m_attn
            if b < 8:
                return m_hidden.at[:, :, :, :, (b - 4) * LANES : (b - 3) * LANES]
            return m_final.at[(b - 8) // 2, :, :, :, ((b - 8) % 2) * BLOCK : ((b - 8) % 2 + 1) * BLOCK, :]

        for k in range(per_layer):

            @pl.when(b == k)
            def _():
                pltpu.make_async_copy(full.at[item], into(k), load_sem.at[k]).start()

    def loaded(b):
        pltpu.make_async_copy(full.at[0], m_attn, load_sem.at[b]).wait()

    def row(layer, index):
        return vec[layer, index : index + 1, :]

    def project(layer, b):
        scale = jnp.where(b == 0, 0.125, 1.0)
        shift = jnp.where(b == 0, row(layer, 0), jnp.where(b == 2, row(layer, 1), 0.0))
        at = pl.multiple_of(b * LANES, LANES)
        for n in range(0, LANES, TILE):
            columns = pl.ds(at + n, TILE)
            out = dot_nn(x[...], wide(m_qkv, columns)) + shift[:, n : n + TILE]
            qkv[:, columns] = (out.astype(jnp.bfloat16).astype(jnp.float32) * scale).astype(jnp.bfloat16)

    def save_p(layer, p):
        slot = p % 2
        return pltpu.make_async_copy(stage_p.at[slot], prob_out.at[layer, p], p_sem.at[slot])

    def attend(layer, first, last):
        def one(p, _):
            @pl.when(p >= 2)
            def _():
                save_p(layer, p).wait()

            at = pl.multiple_of(p * 128, 128)
            q, k, v = (qkv[:, pl.ds(part * LANES + at, 128)] for part in range(3))
            total = None
            for half in range(2):
                scores = dot_nt(lane_half(q, half), k) + bias[...]
                exps = jnp.exp(scores - jnp.max(scores, -1, keepdims=True))
                probs = (exps / jnp.sum(exps, -1, keepdims=True)).astype(jnp.bfloat16)
                stage_p[p % 2, half] = probs
                out = dot_nn(probs, lane_half(v, half))
                total = out if total is None else total + out
            ctx[:, pl.ds(at, 128)] = total.astype(jnp.bfloat16)
            save_p(layer, p).start()
            return 0

        lax.fori_loop(first, last, one, 0)

    def save(which, layer):
        pairs = (
            (qkv, qkv_out.at[layer]),
            (ctx, ctx_out.at[layer]),
            (slope, slope_out.at[layer]),
            (stage_n, norm_out.at[layer, 0]),
            (stage_i, inv_out.at[layer, 0]),
            (stage_n, norm_out.at[layer, 1]),
            (stage_i, inv_out.at[layer, 1]),
            (x, y_out.at[layer]),
        )
        return pltpu.make_async_copy(*pairs[which], save_sem.at[which])

    def normalize(layer, which, put):
        for r in range(0, SEQ, 128):
            rows = slice(r, r + 128)
            residual = acc[rows, :]
            centered = residual - jnp.mean(residual, -1, keepdims=True)
            inverse = lax.rsqrt(jnp.mean(centered * centered, -1, keepdims=True) + epsilon)
            normed = centered * inverse
            stage_n[rows, :] = normed.astype(jnp.bfloat16)
            stage_i[rows, :] = jnp.broadcast_to(inverse, (128, 128))
            put[rows, :] = (normed * row(layer, 8 + which) + row(layer, 10 + which)).astype(jnp.bfloat16)

    def attn_out(layer):
        for n in range(0, LANES, TILE):
            columns = slice(n, n + TILE)
            acc[:, columns] = x[:, columns].astype(jnp.float32) + (
                dot_nn(ctx[...], wide(m_attn, columns)) + row(layer, 2)[:, columns]
            )
        normalize(layer, 0, hid)

    def ffn_in(layer, j):
        shift = vec[layer, pl.ds(3 + j, 1), :]
        at = pl.multiple_of(j * LANES, LANES)
        for n in range(0, LANES, TILE):
            pre = dot_nn(hid[...], wide(m_hidden, pl.ds(at + n, TILE))) + shift[:, n : n + TILE]
            cdf = 0.5 * (1.0 + lax.erf(pre * math.sqrt(0.5)))
            pdf = jnp.exp(pre * pre * -0.5) * (1.0 / math.sqrt(2.0 * math.pi))
            value = (pre * cdf).astype(jnp.bfloat16)
            grade = (cdf + pre * pdf).astype(jnp.bfloat16)
            to = pl.ds(pl.multiple_of(j * 512 + n // 2, 128), 128)
            for half in range(2):
                act[half, :, to] = value[:, half * 128 : (half + 1) * 128]
                slope[half, :, to] = grade[:, half * 128 : (half + 1) * 128]

    def ffn_out(layer, half):
        for n in range(0, LANES, TILE):
            columns = slice(n, n + TILE)
            out = dot_nn(act[half], wide(m_final.at[half], columns))
            if half == 0:
                acc[:, columns] = hid[:, columns].astype(jnp.float32) + (out + row(layer, 7)[:, columns])
            else:
                acc[:, columns] += out

    def compute(c):
        layer, b = c // per_layer, c % per_layer

        @pl.when((b == 0) & (layer == 1))
        def _():
            save(7, 0).wait()

        @pl.when(b <= 2)
        def _():
            loaded(b)
            project(layer, b)

        @pl.when(b == 2)
        def _():
            save(0, layer).start()
            attend(layer, 0, 2)

        @pl.when(b == 3)
        def _():
            loaded(3)
            attend(layer, 2, 5)

        @pl.when(b == 4)
        def _():
            loaded(4)
            attend(layer, 5, 8)

        @pl.when(b == 5)
        def _():
            save(1, layer).start()
            loaded(5)
            attn_out(layer)
            save(3, layer).start()
            save(4, layer).start()

        @pl.when((b >= 5) & (b <= 8))
        def _():
            ffn_in(layer, b - 5)

        @pl.when(b == 6)
        def _():
            loaded(6)
            save_p(layer, 0).wait()
            save_p(layer, 1).wait()
            save(0, layer).wait()
            save(1, layer).wait()

        @pl.when(b == 7)
        def _():
            loaded(7)

        @pl.when(b == 8)
        def _():
            save(2, layer).start()
            loaded(8)

        @pl.when(b == 9)
        def _():
            loaded(9)
            ffn_out(layer, 0)
            save(3, layer).wait()
            save(4, layer).wait()

        @pl.when(b == 10)
        def _():
            loaded(10)
            save(2, layer).wait()

        @pl.when(b == 11)
        def _():
            loaded(11)
            ffn_out(layer, 1)
            normalize(layer, 1, x)
            save(5, layer).start()
            save(6, layer).start()
            save(7, layer).start()
            save(5, layer).wait()
            save(6, layer).wait()

    def step(t, _):
        if with_links:
            step_links(t)
        first = t - LOAD

        @pl.when((first >= 0) & (first < items))
        def _():
            if with_links:
                arrived(first)
            load(first)

        second = t - LOAD - 1

        @pl.when((second >= 0) & (second < items))
        def _():
            compute(second)

        return 0

    lax.fori_loop(0, items + LOAD + 1, step, 0)
    save(7, 1).wait()
    put_vec.wait()
    if with_links:
        end_links()


def forward(tokens, codes, vec, weights):
    items = 24
    with_links = len(weights) == 4
    low, wide_type = jnp.bfloat16, jnp.float32
    in_hbm = pl.BlockSpec(memory_space=pltpu.HBM)
    in_vmem = pl.BlockSpec(memory_space=pltpu.VMEM)
    shape = jax.ShapeDtypeStruct
    full = shape((items, 4, 2, 2, BLOCK, LANES), low)
    saved = (
        shape((2, SEQ, 3 * LANES), low),
        shape((2, 8, 2, SEQ, SEQ), low),
        shape((2, SEQ, LANES), low),
        shape((2, 2, SEQ, 2 * LANES), low),
        shape((2, 2, SEQ, LANES), low),
        shape((2, 2, SEQ, 128), wide_type),
        shape((2, SEQ, LANES), low),
        shape((2, 16, LANES), wide_type),
    )
    scratch = [
        pltpu.VMEM((SEQ, LANES), low),
        pltpu.VMEM((2, 16, LANES), wide_type),
        pltpu.VMEM((4, 2, 2, BLOCK, 3 * LANES), low),
        pltpu.VMEM((4, 2, 2, BLOCK, LANES), low),
        pltpu.VMEM((4, 2, 2, BLOCK, 4 * LANES), low),
        pltpu.VMEM((2, 4, 2, 2, 2 * BLOCK, LANES), low),
        pltpu.VMEM((SEQ, 3 * LANES), low),
        pltpu.VMEM((SEQ, LANES), low),
        pltpu.VMEM((SEQ, LANES), low),
        pltpu.VMEM((2, SEQ, 2 * LANES), low),
        pltpu.VMEM((2, SEQ, 2 * LANES), low),
        pltpu.VMEM((SEQ, LANES), wide_type),
        pltpu.VMEM((SEQ, SEQ), wide_type),
        pltpu.VMEM((2, 2, SEQ, SEQ), low),
        pltpu.VMEM((SEQ, LANES), low),
        pltpu.VMEM((SEQ, 128), wide_type),
        pltpu.SemaphoreType.DMA((12,)),
        pltpu.SemaphoreType.DMA((2,)),
        pltpu.SemaphoreType.DMA((3,)),
        pltpu.SemaphoreType.DMA((2,)),
        pltpu.SemaphoreType.DMA((8,)),
    ]
    if with_links:
        operands = (*weights, vec, tokens, codes)
        specs = [in_hbm] * 6 + [in_vmem]
        outs = (full, *saved)
        scratch += [
            pltpu.VMEM((items // 2, HALF, LANES), low),
            pltpu.SemaphoreType.DMA((items // 2,)),
            pltpu.SemaphoreType.DMA((items // 2,)),
            pltpu.SemaphoreType.DMA((items // 2,)),
            pltpu.SemaphoreType.DMA((items // 2,)),
            pltpu.SemaphoreType.DMA((17,)),
            pltpu.SemaphoreType.DMA((17, items)),
        ]
        params = pltpu.CompilerParams(collective_id=0, has_side_effects=True, vmem_limit_bytes=VMEM_LIMIT)
    else:
        operands = (weights[0], vec, tokens, codes)
        specs = [in_hbm] * 3 + [in_vmem]
        outs = saved
        params = pltpu.CompilerParams(vmem_limit_bytes=VMEM_LIMIT)
    results = pl.pallas_call(
        partial(forward_kernel, items, with_links),
        out_shape=outs,
        in_specs=specs,
        out_specs=tuple([in_hbm] * len(outs)),
        scratch_shapes=scratch,
        compiler_params=params,
    )(*operands)
    return results if with_links else (weights[0], *results)


def backward_kernel(
    cotangent,
    full,
    vec_in,
    qkv_in,
    prob_in,
    ctx_in,
    slope_in,
    norm_in,
    inv_in,
    grad_out,
    sums,
    vec,
    m_qkv,
    m_attn,
    m_hidden,
    m_final,
    qkv,
    ctx,
    slope,
    norms,
    invs,
    probs,
    grad,
    rounded_grad,
    pre_grad,
    proj_grad,
    acc,
    sem,
    m_sem,
    p_sem,
    out_sem,
):
    sec = lax.axis_index("section")

    def start(copies):
        for copy in copies:
            copy.start()

    def wait(copies):
        for copy in copies:
            copy.wait()

    def fetch_final(layer, half):
        return [
            pltpu.make_async_copy(
                full.at[layer * 12 + 8 + 2 * half + g],
                m_final.at[half, :, :, :, g * BLOCK : (g + 1) * BLOCK, :],
                m_sem.at[2 * half + g],
            )
            for g in range(2)
        ]

    def fetch_hidden(layer):
        return [
            pltpu.make_async_copy(
                full.at[layer * 12 + 4 + j], m_hidden.at[:, :, :, :, j * LANES : (j + 1) * LANES], m_sem.at[4 + j]
            )
            for j in range(4)
        ]

    def fetch_attn(layer):
        return [pltpu.make_async_copy(full.at[layer * 12 + 3], m_attn, m_sem.at[8])]

    def fetch_qkv(layer):
        return [
            pltpu.make_async_copy(
                full.at[layer * 12 + j], m_qkv.at[:, :, :, :, j * LANES : (j + 1) * LANES], m_sem.at[9 + j]
            )
            for j in range(3)
        ]

    def fetch_norm(layer, which):
        return [
            pltpu.make_async_copy(norm_in.at[layer, which], norms.at[which], sem.at[2 * which]),
            pltpu.make_async_copy(inv_in.at[layer, which], invs.at[which], sem.at[2 * which + 1]),
        ]

    def fetch_slope(layer, half):
        return [pltpu.make_async_copy(slope_in.at[layer, half], slope.at[half], sem.at[4 + half])]

    def fetch_heads(layer):
        return [
            pltpu.make_async_copy(qkv_in.at[layer], qkv, sem.at[6]),
            pltpu.make_async_copy(ctx_in.at[layer], ctx, sem.at[7]),
        ]

    def fetch_probs(layer, p):
        return [pltpu.make_async_copy(prob_in.at[layer, p], probs.at[p % 2], p_sem.at[p % 2])]

    take_grad = pltpu.make_async_copy(cotangent.at[sec, 0], grad, sem.at[8])
    take_vec = pltpu.make_async_copy(vec_in, vec, sem.at[9])
    take_grad.start()
    start(fetch_norm(1, 1))
    take_vec.start()
    start(fetch_final(1, 0) + fetch_slope(1, 0) + fetch_final(1, 1) + fetch_slope(1, 1) + fetch_hidden(1))
    start(fetch_norm(1, 0) + fetch_attn(1) + fetch_heads(1))
    start(fetch_probs(1, 0) + fetch_probs(1, 1) + fetch_qkv(1))
    take_grad.wait()
    take_vec.wait()

    def put_grad(layer):
        return pltpu.make_async_copy(grad, grad_out.at[layer], out_sem.at[0])

    def column_sum(values):
        return jnp.sum(values.astype(jnp.float32), 0, keepdims=True)

    def norm_back(layer, which, upstream_of):
        gain = vec[layer, 8 + which : 9 + which, :]
        total = jnp.zeros((1, LANES), jnp.float32)
        for r in range(0, SEQ, 128):
            rows = slice(r, r + 128)
            upstream = upstream_of(rows) * gain
            normed = norms[which, rows, :].astype(jnp.float32)
            back = invs[which, rows, 0:1] * (
                upstream
                - jnp.mean(upstream, -1, keepdims=True)
                - normed * jnp.mean(upstream * normed, -1, keepdims=True)
            )
            acc[rows, :] = back
            low = back.astype(jnp.bfloat16)
            rounded_grad[rows, :] = low
            total = total + column_sum(low)
        return total

    def one_layer(s, _):
        layer = 1 - s

        def prefetch(copies):
            @pl.when(s == 0)
            def _():
                start(copies)

        wait(fetch_norm(layer, 1))
        sums[layer, 7:8, :] = norm_back(layer, 1, lambda rows: grad[rows, :].astype(jnp.float32))
        prefetch(fetch_norm(0, 1))
        for half in range(2):
            wait(fetch_final(layer, half) + fetch_slope(layer, half))
            for n in range(0, 2048, TILE):
                chip = n // 128
                block = m_final[half, chip // 4, (chip // 2) % 2].reshape(TILE, LANES)
                back = dot_nt(rounded_grad[...], block) * slope[half, :, n : n + TILE].astype(jnp.float32)
                low = back.astype(jnp.bfloat16)
                total = column_sum(low)
                for k in range(2):
                    at = (chip + k) * 256 + half * 128
                    part = slice(k * 128, (k + 1) * 128)
                    pre_grad[:, at : at + 128] = low[:, part]
                    sums[layer, 3 + at // LANES : 4 + at // LANES, at % LANES : at % LANES + 128] = total[:, part]
            prefetch(fetch_final(0, half) + fetch_slope(0, half))
        wait(fetch_hidden(layer))
        for n in range(0, LANES, TILE):
            block = m_hidden[n // TILE].reshape(TILE, 4 * LANES)
            acc[:, n : n + TILE] += dot_nt(pre_grad[...], block)
        prefetch(fetch_hidden(0))
        wait(fetch_norm(layer, 0))
        sums[layer, 2:3, :] = norm_back(
            layer, 0, lambda rows: acc[rows, :].astype(jnp.bfloat16).astype(jnp.float32)
        )
        prefetch(fetch_norm(0, 0))

        @pl.when(s == 1)
        def _():
            put_grad(1).wait()

        wait(fetch_attn(layer))
        for n in range(0, LANES, TILE):
            block = m_attn[n // TILE].reshape(TILE, LANES)
            grad[:, n : n + TILE] = dot_nt(rounded_grad[...], block).astype(jnp.bfloat16)
        prefetch(fetch_attn(0))
        wait(fetch_heads(layer))

        def one_pair(p, _):
            wait(fetch_probs(layer, p))
            at = pl.multiple_of(p * 128, 128)
            q, k, v = (qkv[:, pl.ds(part * LANES + at, 128)] for part in range(3))
            upper = grad[:, pl.ds(at, 128)]
            product = upper.astype(jnp.float32) * ctx[:, pl.ds(at, 128)].astype(jnp.float32)
            q_t, upper_t = q.T, upper.T
            grad_q = None
            grad_k, grad_v = [], []
            for half in range(2):
                weights = probs[p % 2, half]
                delta = jnp.sum(lane_half(product, half), -1, keepdims=True)
                scores = dot_nt(lane_half(upper, half), v)
                low = (weights.astype(jnp.float32) * (scores - delta)).astype(jnp.bfloat16)
                part = dot_nn(low, lane_half(k, half))
                grad_q = part if grad_q is None else grad_q + part
                here = slice(half * HEAD_DIM, (half + 1) * HEAD_DIM)
                grad_k.append(dot_nn(q_t[here], low))
                grad_v.append(dot_nn(upper_t[here], weights))
            back_q = (grad_q * 0.125).astype(jnp.bfloat16)
            back_v = jnp.concatenate(grad_v, 0).astype(jnp.bfloat16).T
            proj_grad[:, pl.ds(at, 128)] = back_q
            proj_grad[:, pl.ds(LANES + at, 128)] = jnp.concatenate(grad_k, 0).astype(jnp.bfloat16).T
            proj_grad[:, pl.ds(2 * LANES + at, 128)] = back_v
            sums[layer, 0:1, pl.ds(at, 128)] = column_sum(back_q)
            sums[layer, 1:2, pl.ds(at, 128)] = column_sum(back_v)

            @pl.when(p < 6)
            def _():
                start(fetch_probs(layer, p + 2))

            return 0

        lax.fori_loop(0, 8, one_pair, 0)
        prefetch(fetch_heads(0) + fetch_probs(0, 0) + fetch_probs(0, 1))
        wait(fetch_qkv(layer))
        for n in range(0, LANES, TILE):
            block = m_qkv[n // TILE].reshape(TILE, 3 * LANES)
            columns = slice(n, n + TILE)
            grad[:, columns] = (acc[:, columns] + dot_nt(proj_grad[...], block)).astype(jnp.bfloat16)
        prefetch(fetch_qkv(0))
        put_grad(layer).start()
        return 0

    lax.fori_loop(0, 2, one_layer, 0)
    put_grad(0).wait()


def backward(cotangent, full, vec, saved):
    qkv, probs, ctx, slope, norms, invs = saved
    in_hbm = pl.BlockSpec(memory_space=pltpu.HBM)
    in_vmem = pl.BlockSpec(memory_space=pltpu.VMEM)
    low, wide_type = jnp.bfloat16, jnp.float32
    return pl.pallas_call(
        backward_kernel,
        out_shape=(
            jax.ShapeDtypeStruct((2, SEQ, LANES), low),
            jax.ShapeDtypeStruct((2, 8, LANES), wide_type),
        ),
        in_specs=[in_hbm] * 9,
        out_specs=(in_hbm, in_vmem),
        scratch_shapes=[
            pltpu.VMEM((2, 16, LANES), wide_type),
            pltpu.VMEM((4, 2, 2, BLOCK, 3 * LANES), low),
            pltpu.VMEM((4, 2, 2, BLOCK, LANES), low),
            pltpu.VMEM((4, 2, 2, BLOCK, 4 * LANES), low),
            pltpu.VMEM((2, 4, 2, 2, 2 * BLOCK, LANES), low),
            pltpu.VMEM((SEQ, 3 * LANES), low),
            pltpu.VMEM((SEQ, LANES), low),
            pltpu.VMEM((2, SEQ, 2 * LANES), low),
            pltpu.VMEM((2, SEQ, LANES), low),
            pltpu.VMEM((2, SEQ, 128), wide_type),
            pltpu.VMEM((2, 2, SEQ, SEQ), low),
            pltpu.VMEM((SEQ, LANES), low),
            pltpu.VMEM((SEQ, LANES), low),
            pltpu.VMEM((SEQ, 4 * LANES), low),
            pltpu.VMEM((SEQ, 3 * LANES), low),
            pltpu.VMEM((SEQ, LANES), wide_type),
            pltpu.SemaphoreType.DMA((10,)),
            pltpu.SemaphoreType.DMA((12,)),
            pltpu.SemaphoreType.DMA((2,)),
            pltpu.SemaphoreType.DMA((1,)),
        ],
        compiler_params=pltpu.CompilerParams(vmem_limit_bytes=VMEM_LIMIT),
    )(cotangent, full, vec, qkv, probs, ctx, slope, norms, invs)


def gather(w_qkv, w_out, w_in, w_ffn_out):
    matrices = [lax.all_gather(w[0], "dp", axis=0, tiled=True) for w in (w_qkv, w_out, w_in, w_ffn_out)]
    qkv, attn, hidden, final = matrices
    blocks = [qkv[:, b * LANES : (b + 1) * LANES] for b in range(3)] + [attn]
    blocks += [hidden[:, b * LANES : (b + 1) * LANES] for b in range(4)]
    final = final.reshape(16, 4, BLOCK, LANES).transpose(1, 0, 2, 3).reshape(4, 1024, LANES)
    own = jnp.concatenate([jnp.stack(blocks), final])
    return lax.all_gather(own, "section", axis=0, tiled=True).reshape(24, 4, 2, 2, BLOCK, LANES)


def on_device(
    tokens,
    segment_ids,
    row_lengths,
    w_qkv,
    w_out,
    w_in,
    w_ffn_out,
    bias_q,
    bias_v,
    bias_out,
    bias_in,
    bias_ffn_out,
    ln_gain,
    ln_shift,
    out_cotangent,
):
    sec = lax.axis_index("section")
    weights = (w_qkv, w_out, w_in, w_ffn_out)
    vec = jnp.concatenate(
        [bias_q, bias_v, bias_out, bias_in.reshape(4, LANES), bias_ffn_out, ln_gain[0], ln_shift[0], jnp.zeros((4, LANES))]
    )
    if w_qkv.shape[1] != BLOCK:
        weights = (gather(*weights),)
        vec = lax.all_gather(vec, "section", axis=0)
    valid = jnp.arange(SEQ, dtype=jnp.int32) < row_lengths[:, :, None]
    codes = segment_ids * 2 + valid.astype(jnp.int32)
    full, *saved, tops, vec = forward(tokens, codes, vec, weights)
    grads, sums = backward(out_cotangent, full, vec, saved)

    def swap(array):
        return lax.ppermute(array, "section", [(0, 1), (1, 0)])

    def placed(both):
        got = swap(jnp.where(sec == 0, both[1], both[0]))
        placed = jnp.where(sec == 0, jnp.stack([both[0], got]), jnp.stack([got, both[1]]))
        return placed[None, :, None]

    sums = jnp.where(sec == 0, sums[0], sums[1]) + swap(jnp.where(sec == 0, sums[1], sums[0]))
    sums = lax.psum(sums, "dp")
    totals = (sums[0:1], sums[1:2], sums[2:3], sums[3:7].reshape(1, 4 * LANES), sums[7:8])
    return (placed(tops), placed(grads)) + totals


def solution(mesh):
    placed = (
        P(None, "dp", None, None),
        P(None, "dp", None),
        P(None, "dp"),
        P("section", "dp", None),
        P("section", "dp", None),
        P("section", "dp", None),
        P("section", "dp", None),
        P("section", None),
        P("section", None),
        P("section", None),
        P("section", None),
        P("section", None),
        P("section", None, None),
        P("section", None, None),
        P(None, "dp", None, None),
    )
    return jax.shard_map(
        on_device,
        mesh=mesh,
        in_specs=placed,
        out_specs=(
            P("section", None, "dp", None, None),
            P("section", None, "dp", None, None),
            P("section", None),
            P("section", None),
            P("section", None),
            P("section", None),
            P("section", None),
        ),
        check_vma=False,
    )
```

```python
from functools import partial
import math

import jax
import jax.numpy as jnp
from jax import lax
from jax.experimental import pallas as pl
from jax.experimental.pallas import tpu as pltpu
from jax.sharding import PartitionSpec as P

HEAD_DIM = 64
SEQ = 512
PAIRS = 8
epsilon = 1e-06
VMEM_LIMIT = 60 * 2**20
MESH = pl.DeviceIdType.MESH
ITEMS = 24
PER_LAYER = ITEMS // 2
LANES = 1024
BLOCK = 64
HALF = BLOCK // 2
CUT = 384
STAGES = (1, 2, 3, 4, 6)
LOAD = 7
FRONT = 2
TILE = 256


def link_plan(wq, wo, wi, wf, full, vec, stage, in_sem, place_sem, cross_send, cross_recv, send_sem, recv_sem, vec_sem):
    sec = lax.axis_index("section")
    chip = lax.axis_index("dp")
    per_layer, items = PER_LAYER, ITEMS
    z = chip // 4
    y = (chip // 2) % 2
    x = chip % 2
    dev_x = (sec, z * 4 + y * 2 + 1 - x)
    dev_y = (sec, z * 4 + (1 - y) * 2 + x)
    dev_xy = (sec, z * 4 + (1 - y) * 2 + 1 - x)
    dev_up = (sec, jnp.minimum(z + 1, 3) * 4 + y * 2 + x)
    dev_down = (sec, jnp.maximum(z - 1, 0) * 4 + y * 2 + x)
    dev_core = (1 - sec, chip)
    in_plane = (dev_x, dev_y, dev_xy)
    along_z = tuple((sec, ((z + k) % 4) * 4 + y * 2 + x) for k in (1, 2, 3))

    def own_block(b, row):
        if b < 3:
            return wq.at[0, pl.ds(row, HALF), b * LANES : (b + 1) * LANES]
        if b == 3:
            return wo.at[0, pl.ds(row, HALF), :]
        if b < 8:
            return wi.at[0, pl.ds(row, HALF), (b - 4) * LANES : (b - 3) * LANES]
        return wf.at[0, pl.ds((b - 8) * BLOCK + row, HALF), :]

    mine = pl.multiple_of(sec * HALF, HALF)
    other = pl.multiple_of((1 - sec) * HALF, HALF)

    def to_stage(b):
        return pltpu.make_async_copy(own_block(b, mine), stage.at[b], in_sem.at[b])

    def to_place(b):
        return pltpu.make_async_copy(
            stage.at[b], full.at[sec * per_layer + b, z, y, x, pl.ds(mine, HALF), :], place_sem.at[b]
        )

    def cross(b):
        return pltpu.make_async_remote_copy(
            src_ref=own_block(b, other),
            dst_ref=full.at[sec * per_layer + b, z, y, x, pl.ds(other, HALF), :],
            send_sem=cross_send.at[b],
            recv_sem=cross_recv.at[b],
            device_id=dev_core,
            device_id_type=MESH,
        )

    def give_vec(where):
        return pltpu.make_async_remote_copy(
            src_ref=where,
            dst_ref=where,
            send_sem=vec_sem.at[0],
            recv_sem=vec_sem.at[1],
            device_id=dev_core,
            device_id_type=MESH,
        )

    def begin():
        for b in range(per_layer):
            to_stage(b).start()
        barrier = pltpu.get_barrier_semaphore()
        for device in (dev_core, *in_plane, *along_z):
            pl.semaphore_signal(barrier, inc=1, device_id=device, device_id_type=MESH)
        pl.semaphore_wait(barrier, 7)
        for b in range(per_layer):
            cross(b).start()
        give_vec(vec.at[sec]).start()
        for b in range(per_layer):
            to_stage(b).wait()
            to_place(b).start()

    def vec_here():
        give_vec(vec.at[sec]).wait_send()
        give_vec(vec.at[1 - sec]).wait_recv()

    def copy(ref, kind, item, device):
        return pltpu.make_async_remote_copy(
            src_ref=ref,
            dst_ref=ref,
            send_sem=send_sem.at[kind],
            recv_sem=recv_sem.at[kind, item],
            device_id=device,
            device_id_type=MESH,
        )

    def views(core):
        rows = slice(core * HALF, (core + 1) * HALF)
        first, last = slice(0, CUT), slice(CUT, LANES)
        if core == 0:
            pair = lambda i, at: full.at[i, at, :, x, rows, last]
            eight_first = lambda i: full.at[i, :, y, :, rows, first]
            eight_last = lambda i: full.at[i, :, :, x, rows, last]
            towards = (dev_x, dev_y)
        else:
            pair = lambda i, at: full.at[i, at, y, :, rows, last]
            eight_first = lambda i: full.at[i, :, :, x, rows, first]
            eight_last = lambda i: full.at[i, :, y, :, rows, last]
            towards = (dev_y, dev_x)
        return (
            towards,
            lambda i, at: full.at[i, at, y, x, rows, first],
            lambda i: full.at[i, :, y, x, rows, first],
            eight_first,
            lambda i, at: full.at[i, at, y, x, rows, last],
            pair,
            eight_last,
            lambda i: full.at[i, :, :, :, rows, :],
        )

    def z_send(base, block, hop, item, at):
        if at < 3 and at - (hop - 1) >= 0:
            copy(block(item, at - (hop - 1)), base + hop - 1, item, dev_up).start()
        if at > 0 and at + (hop - 1) <= 3:
            copy(block(item, at + (hop - 1)), base + 2 + hop, item, dev_down).start()

    def z_recv(base, block, hop, item, at):
        if at - hop >= 0:
            copy(block(item, at - hop), base + hop - 1, item, dev_up).wait_recv()
        if at + hop <= 3:
            copy(block(item, at + hop), base + 2 + hop, item, dev_down).wait_recv()

    def step_at(t, at, core):
        (dev_u, dev_v), own_a, col_a, eight_a, own_d, pair_d, eight_d, whole = views(core)
        turns = [t - offset for offset in STAGES]

        def live(item):
            return (item >= 0) & (item < items)

        def first_move(item):
            @pl.when(live(item))
            def _():
                layer, b = item // per_layer, item % per_layer

                @pl.when(layer == core)
                def _():
                    pltpu.make_async_copy(
                        stage.at[b], full.at[item, z, y, x, pl.ds(core * HALF, HALF), :], place_sem.at[b]
                    ).wait()

                @pl.when(layer != core)
                def _():
                    mine_there = full.at[item, z, y, x, pl.ds(core * HALF, HALF), :]
                    pltpu.make_async_remote_copy(
                        src_ref=mine_there,
                        dst_ref=mine_there,
                        send_sem=cross_send.at[b],
                        recv_sem=cross_recv.at[b],
                        device_id=dev_core,
                        device_id_type=MESH,
                    ).wait_recv()

                z_send(0, own_a, 1, item, at)
                copy(own_d(item, at), 8, item, dev_v).start()

        for lead in range(FRONT):
            first_move(t * FRONT + lead)

        item1 = turns[0]

        @pl.when(live(item1))
        def _():
            z_recv(0, own_a, 1, item1, at)
            z_send(0, own_a, 2, item1, at)
            copy(own_d(item1, at), 8, item1, dev_v).wait_recv()
            z_send(9, pair_d, 1, item1, at)

        item2 = turns[1]

        @pl.when(live(item2))
        def _():
            z_recv(0, own_a, 2, item2, at)
            z_send(0, own_a, 3, item2, at)
            z_recv(9, pair_d, 1, item2, at)
            z_send(9, pair_d, 2, item2, at)

        item3 = turns[2]

        @pl.when(live(item3))
        def _():
            z_recv(0, own_a, 3, item3, at)
            copy(col_a(item3), 6, item3, dev_u).start()
            z_recv(9, pair_d, 2, item3, at)
            z_send(9, pair_d, 3, item3, at)

        item4 = turns[3]

        @pl.when(live(item4))
        def _():
            copy(col_a(item4), 6, item4, dev_u).wait_recv()
            copy(eight_a(item4), 7, item4, dev_v).start()
            z_recv(9, pair_d, 3, item4, at)
            copy(eight_d(item4), 15, item4, dev_u).start()

        item5 = turns[4]

        @pl.when(live(item5))
        def _():
            copy(eight_a(item5), 7, item5, dev_v).wait_recv()
            copy(eight_d(item5), 15, item5, dev_u).wait_recv()
            copy(whole(item5), 16, item5, dev_core).start()

    def step(t):
        for at in range(4):
            for core in range(2):

                @pl.when((z == at) & (sec == core))
                def _():
                    step_at(t, at, core)

    def arrived(item):
        for core in range(2):

            @pl.when(sec == core)
            def _():
                copy(views(1 - core)[-1](item), 16, item, dev_core).wait_recv()

    def end():
        for b in range(per_layer):
            cross(b).wait_send()
        for core in range(2):

            @pl.when(sec == core)
            def _():
                _, own_a, col_a, eight_a, own_d, pair_d, eight_d, whole = views(core)
                every = slice(None)

                def sent(ref, kind):
                    copy(ref, kind, 0, dev_core).wait_send()

                sent(whole(every), 16)
                sent(col_a(every), 6)
                sent(eight_a(every), 7)
                sent(eight_d(every), 15)
                sent(own_d(every, 0), 8)
                for hop in (1, 2, 3):
                    for base, block in ((0, own_a), (9, pair_d)):

                        @pl.when((z < 3) & (z - (hop - 1) >= 0))
                        def _():
                            sent(block(every, 0), base + hop - 1)

                        @pl.when((z > 0) & (z + (hop - 1) <= 3))
                        def _():
                            sent(block(every, 0), base + 2 + hop)

    return begin, vec_here, step, arrived, end, dev_core, in_plane, along_z


def wide(ref, columns):
    block = ref[:, :, :, :, columns]
    return block.reshape(-1, block.shape[-1])


def dot_nt(left, right):
    return lax.dot_general(left, right, (((1,), (1,)), ((), ())), preferred_element_type=jnp.float32)


def dot_nn(left, right):
    return jnp.dot(left, right, preferred_element_type=jnp.float32)


def pair_bias(codes):
    down = jnp.broadcast_to(codes, (128, codes.shape[1])).T[:, :1]
    return jnp.where(down == codes, 0.0, -1000000000.0)


def lane_half(pair, half):
    lanes = lax.broadcasted_iota(jnp.int32, pair.shape, 1)
    return jnp.where((lanes < HEAD_DIM) == (half == 0), pair, jnp.zeros_like(pair))


def layers_kernel(with_links, *refs):
    if with_links:
        wq, wo, wi, wf, *refs = refs
    else:
        full, *refs = refs
    tokens, cotangent, segments, lengths, *refs = refs
    if with_links:
        parts, refs = refs[:7], refs[7:]
        full, *refs = refs
    else:
        given_vec, *refs = refs
    (y_out, grad_out, sums, prob_save, qkv_save, ctx_save, slope_save, norm_save, inv_save, *refs) = refs
    (x, vec, m_qkv, m_attn, m_hidden, m_final, qkv, ctx, hid, act, slope, acc, bias, probs, norms, invs, *refs) = refs
    (grad, proj_grad, layer_sums, in_sem, load_sem, p_sem, save_sem, m_sem, sem, out_sem, *refs) = refs
    sec = lax.axis_index("section")
    if with_links:
        (stage, got_core, got_plane, got_z, part_core, part_plane, *link_sems) = refs
        *link_sems, ex_send, ex_recv, sum_send, sum_recv = link_sems

    def start(copies):
        for copy in copies:
            copy.start()

    def wait(copies):
        for copy in copies:
            copy.wait()

    take_x = pltpu.make_async_copy(tokens.at[sec, 0], x, in_sem.at[0])
    take_grad = pltpu.make_async_copy(cotangent.at[sec, 0], grad, in_sem.at[1])
    take_x.start()
    take_grad.start()
    if with_links:
        bias_q, bias_v, bias_out, bias_in, bias_ffn_out, ln_gain, ln_shift = parts
        for k, ref in enumerate((bias_q, bias_v, bias_out)):
            vec[sec, k : k + 1, :] = ref[...]
        for k in range(4):
            vec[sec, 3 + k : 4 + k, :] = bias_in[:, k * LANES : (k + 1) * LANES]
        vec[sec, 7:8, :] = bias_ffn_out[...]
        vec[sec, 8:10, :] = ln_gain[0]
        vec[sec, 10:12, :] = ln_shift[0]
        vec[sec, 12:16, :] = jnp.zeros((4, LANES), jnp.float32)
        begin_links, vec_here, step_links, arrived, end_links, dev_core, in_plane, along_z = link_plan(
            wq, wo, wi, wf, full, vec, stage, *link_sems
        )
        begin_links()
    else:
        take_vec = pltpu.make_async_copy(given_vec, vec, in_sem.at[2])
        take_vec.start()
        take_vec.wait()
    valid = lax.broadcasted_iota(jnp.int32, (1, SEQ), 1) < lengths[sec, 0]
    bias[...] = pair_bias(segments[sec] * 2 + valid.astype(jnp.int32))
    take_x.wait()
    if with_links:
        vec_here()

    def row(layer, index):
        return vec[layer, index : index + 1, :]

    def hand_over(which, source, out, layer):
        local = pltpu.make_async_copy(source, out.at[sec], out_sem.at[which])
        if with_links:
            far = pltpu.make_async_remote_copy(
                src_ref=source,
                dst_ref=out.at[sec],
                send_sem=ex_send.at[which],
                recv_sem=ex_recv.at[which],
                device_id=dev_core,
                device_id_type=MESH,
            )
            return local, far
        return (pltpu.make_async_copy(source, out.at[layer], out_sem.at[which]),)

    def hand_start(which, source, out, layer):
        copies = hand_over(which, source, out, layer)
        if with_links:

            @pl.when(layer == sec)
            def _():
                copies[0].start()

            @pl.when(layer != sec)
            def _():
                copies[1].start()

        else:
            copies[0].start()

    def hand_wait(which, source, out, layer):
        copies = hand_over(which, source, out, layer)
        if with_links:

            @pl.when(layer == sec)
            def _():
                copies[0].wait()

            @pl.when(layer != sec)
            def _():
                copies[1].wait_send()

        else:
            copies[0].wait()

    def hand_arrived(which, source, out):
        pltpu.make_async_remote_copy(
            src_ref=source,
            dst_ref=out.at[1 - sec],
            send_sem=ex_send.at[which],
            recv_sem=ex_recv.at[which],
            device_id=dev_core,
            device_id_type=MESH,
        ).wait_recv()

    def load(item):
        b = item % PER_LAYER

        def into(b):
            if b < 3:
                return m_qkv.at[:, :, :, :, b * LANES : (b + 1) * LANES]
            if b == 3:
                return m_attn
            if b < 8:
                return m_hidden.at[:, :, :, :, (b - 4) * LANES : (b - 3) * LANES]
            return m_final.at[(b - 8) // 2, :, :, :, ((b - 8) % 2) * BLOCK : ((b - 8) % 2 + 1) * BLOCK, :]

        for k in range(PER_LAYER):

            @pl.when(b == k)
            def _():
                pltpu.make_async_copy(full.at[item], into(k), load_sem.at[k]).start()

    def loaded(b):
        pltpu.make_async_copy(full.at[0], m_attn, load_sem.at[b]).wait()

    def project(layer, b):
        scale = jnp.where(b == 0, 0.125, 1.0)
        shift = jnp.where(b == 0, row(layer, 0), jnp.where(b == 2, row(layer, 1), 0.0))
        at = pl.multiple_of(b * LANES, LANES)
        for n in range(0, LANES, TILE):
            columns = pl.ds(at + n, TILE)
            out = dot_nn(x[...], wide(m_qkv, columns)) + shift[:, n : n + TILE]
            qkv[:, columns] = (out.astype(jnp.bfloat16).astype(jnp.float32) * scale).astype(jnp.bfloat16)

    def save_p(layer, p):
        slot = p % 2
        return pltpu.make_async_copy(probs.at[slot], prob_save.at[layer, p], p_sem.at[slot])

    def attend(layer, first, last):
        def one(p, _):
            @pl.when(p >= 2)
            def _():
                save_p(layer, p).wait()

            at = pl.multiple_of(p * 128, 128)
            q, k, v = (qkv[:, pl.ds(part * LANES + at, 128)] for part in range(3))
            total = None
            for half in range(2):
                scores = dot_nt(lane_half(q, half), k) + bias[...]
                exps = jnp.exp(scores - jnp.max(scores, -1, keepdims=True))
                share = (exps / jnp.sum(exps, -1, keepdims=True)).astype(jnp.bfloat16)
                probs[p % 2, half] = share
                out = dot_nn(share, lane_half(v, half))
                total = out if total is None else total + out
            ctx[:, pl.ds(at, 128)] = total.astype(jnp.bfloat16)
            save_p(layer, p).start()
            return 0

        lax.fori_loop(first, last, one, 0)

    def save(which):
        pairs = (
            (qkv, qkv_save),
            (ctx, ctx_save),
            (slope, slope_save),
            (norms.at[0], norm_save.at[0]),
            (invs.at[0], inv_save.at[0]),
            (norms.at[1], norm_save.at[1]),
            (invs.at[1], inv_save.at[1]),
        )
        return pltpu.make_async_copy(*pairs[which], save_sem.at[which])

    def normalize(layer, which, put):
        for r in range(0, SEQ, 128):
            rows = slice(r, r + 128)
            residual = acc[rows, :]
            centered = residual - jnp.mean(residual, -1, keepdims=True)
            inverse = lax.rsqrt(jnp.mean(centered * centered, -1, keepdims=True) + epsilon)
            normed = centered * inverse
            norms[which, rows, :] = normed.astype(jnp.bfloat16)
            invs[which, rows, :] = jnp.broadcast_to(inverse, (128, 128))
            put[rows, :] = (normed * row(layer, 8 + which) + row(layer, 10 + which)).astype(jnp.bfloat16)

    def attn_out(layer):
        for n in range(0, LANES, TILE):
            columns = slice(n, n + TILE)
            acc[:, columns] = x[:, columns].astype(jnp.float32) + (
                dot_nn(ctx[...], wide(m_attn, columns)) + row(layer, 2)[:, columns]
            )
        normalize(layer, 0, hid)

    def ffn_in(layer, j):
        shift = vec[layer, pl.ds(3 + j, 1), :]
        at = pl.multiple_of(j * LANES, LANES)
        for n in range(0, LANES, TILE):
            pre = dot_nn(hid[...], wide(m_hidden, pl.ds(at + n, TILE))) + shift[:, n : n + TILE]
            cdf = 0.5 * (1.0 + lax.erf(pre * math.sqrt(0.5)))
            pdf = jnp.exp(pre * pre * -0.5) * (1.0 / math.sqrt(2.0 * math.pi))
            value = (pre * cdf).astype(jnp.bfloat16)
            grade = (cdf + pre * pdf).astype(jnp.bfloat16)
            to = pl.ds(pl.multiple_of(j * 512 + n // 2, 128), 128)
            for half in range(2):
                act[half, :, to] = value[:, half * 128 : (half + 1) * 128]
                slope[half, :, to] = grade[:, half * 128 : (half + 1) * 128]

    def ffn_out(layer, half):
        for n in range(0, LANES, TILE):
            columns = slice(n, n + TILE)
            out = dot_nn(act[half], wide(m_final.at[half], columns))
            if half == 0:
                acc[:, columns] = hid[:, columns].astype(jnp.float32) + (out + row(layer, 7)[:, columns])
            else:
                acc[:, columns] += out

    def compute(c):
        layer, b = c // PER_LAYER, c % PER_LAYER

        def lower(then):
            pl.when(layer == 0)(then)

        @pl.when(b <= 2)
        def _():
            loaded(b)

            @pl.when((b == 0) & (layer == 1))
            def _():
                wait([save(5), save(6)])

            project(layer, b)

        @pl.when(b == 2)
        def _():
            lower(lambda: start([save(0)]))
            attend(layer, 0, 2)

        @pl.when(b == 3)
        def _():
            loaded(3)
            attend(layer, 2, 5)

        @pl.when(b == 4)
        def _():
            loaded(4)
            attend(layer, 5, 8)

        @pl.when(b == 5)
        def _():
            lower(lambda: start([save(1)]))
            loaded(5)
            attn_out(layer)
            lower(lambda: start([save(3), save(4)]))

        @pl.when((b >= 5) & (b <= 8))
        def _():
            ffn_in(layer, b - 5)

        @pl.when(b == 6)
        def _():
            loaded(6)
            wait([save_p(layer, 0), save_p(layer, 1)])
            lower(lambda: wait([save(0), save(1)]))

        @pl.when(b == 7)
        def _():
            loaded(7)

        @pl.when(b == 8)
        def _():
            lower(lambda: start([save(2)]))
            loaded(8)

        @pl.when(b == 9)
        def _():
            loaded(9)

            @pl.when(layer == 1)
            def _():
                hand_wait(0, x, y_out, 0)

            ffn_out(layer, 0)
            lower(lambda: wait([save(3), save(4)]))

        @pl.when(b == 10)
        def _():
            loaded(10)
            lower(lambda: wait([save(2)]))

        @pl.when(b == 11)
        def _():
            loaded(11)
            ffn_out(layer, 1)
            normalize(layer, 1, x)
            lower(lambda: start([save(5), save(6)]))
            hand_start(layer, x, y_out, layer)

    def step(t, _):
        if with_links:
            step_links(t)
        first = t - LOAD

        @pl.when((first >= 0) & (first < ITEMS))
        def _():
            if with_links:
                arrived(first)
            load(first)

        second = t - LOAD - 1

        @pl.when((second >= 0) & (second < ITEMS))
        def _():
            compute(second)

        return 0

    lax.fori_loop(0, ITEMS + LOAD + 1, step, 0)
    def fetch_final(half):
        return [
            pltpu.make_async_copy(
                full.at[8 + 2 * half + g],
                m_final.at[half, :, :, :, g * BLOCK : (g + 1) * BLOCK, :],
                m_sem.at[2 * half + g],
            )
            for g in range(2)
        ]

    def fetch_hidden():
        return [
            pltpu.make_async_copy(
                full.at[4 + j], m_hidden.at[:, :, :, :, j * LANES : (j + 1) * LANES], m_sem.at[4 + j]
            )
            for j in range(4)
        ]

    def fetch_attn():
        return [pltpu.make_async_copy(full.at[3], m_attn, m_sem.at[8])]

    def fetch_qkv():
        return [
            pltpu.make_async_copy(full.at[j], m_qkv.at[:, :, :, :, j * LANES : (j + 1) * LANES], m_sem.at[9 + j])
            for j in range(3)
        ]

    def fetch_norm(which):
        return [
            pltpu.make_async_copy(norm_save.at[which], norms.at[which], sem.at[2 * which]),
            pltpu.make_async_copy(inv_save.at[which], invs.at[which], sem.at[2 * which + 1]),
        ]

    def fetch_slope(half):
        return [pltpu.make_async_copy(slope_save.at[half], slope.at[half], sem.at[4 + half])]

    def fetch_heads():
        return [
            pltpu.make_async_copy(qkv_save, qkv, sem.at[6]),
            pltpu.make_async_copy(ctx_save, ctx, sem.at[7]),
        ]

    def fetch_probs(layer, p):
        return [pltpu.make_async_copy(prob_save.at[layer, p], probs.at[p % 2], p_sem.at[p % 2])]

    start(fetch_probs(1, 0) + fetch_probs(1, 1))
    take_grad.wait()

    def column_sum(values):
        return jnp.sum(values.astype(jnp.float32), 0, keepdims=True)

    def norm_back(layer, which, upstream_of):
        gain = vec[layer, 8 + which : 9 + which, :]
        total = jnp.zeros((1, LANES), jnp.float32)
        for r in range(0, SEQ, 128):
            rows = slice(r, r + 128)
            upstream = upstream_of(rows) * gain
            normed = norms[which, rows, :].astype(jnp.float32)
            back = invs[which, rows, 0:1] * (
                upstream
                - jnp.mean(upstream, -1, keepdims=True)
                - normed * jnp.mean(upstream * normed, -1, keepdims=True)
            )
            acc[rows, :] = back
            low = back.astype(jnp.bfloat16)
            hid[rows, :] = low
            total = total + column_sum(low)
        return total

    def sum_copy(source, target, k, device):
        return pltpu.make_async_remote_copy(
            src_ref=source,
            dst_ref=target,
            send_sem=sum_send.at[k],
            recv_sem=sum_recv.at[k],
            device_id=device,
            device_id_type=MESH,
        )

    def core_sums():
        return [sum_copy(layer_sums.at[1 - sec], got_core, 0, dev_core)]

    def plane_sums():
        return [sum_copy(part_core, got_plane.at[k], 1 + k, device) for k, device in enumerate(in_plane)]

    def z_sums():
        return [sum_copy(part_plane, got_z.at[k], 4 + k, device) for k, device in enumerate(along_z)]

    def begin_sums():
        start(core_sums())

    def then_sums(k):
        if k == 0:
            wait(core_sums())
            part_core[...] = layer_sums[sec] + got_core[...]
            start(plane_sums())
        elif k == 1:
            wait(plane_sums())
            part_plane[...] = part_core[...] + (got_plane[0] + got_plane[1]) + got_plane[2]
            start(z_sums())
        elif k == 3:
            wait(z_sums())
            sums[...] = part_plane[...] + (got_z[0] + got_z[1]) + got_z[2]

    def one_layer(s, _):
        layer = 1 - s

        def prefetch(copies):
            @pl.when(s == 0)
            def _():
                start(copies)

        def fetched(copies):
            @pl.when(s == 1)
            def _():
                wait(copies)

        fetched(fetch_norm(1))
        layer_sums[layer, 7:8, :] = norm_back(layer, 1, lambda rows: grad[rows, :].astype(jnp.float32))
        prefetch(fetch_norm(1))
        for half in range(2):
            fetched(fetch_final(half) + fetch_slope(half))
            for n in range(0, 2048, TILE):
                chip = n // 128
                block = m_final[half, chip // 4, (chip // 2) % 2].reshape(TILE, LANES)
                back = dot_nt(hid[...], block) * slope[half, :, n : n + TILE].astype(jnp.float32)
                low = back.astype(jnp.bfloat16)
                total = column_sum(low)
                for k in range(2):
                    at = (chip + k) * 256 + half * 128
                    part = slice(k * 128, (k + 1) * 128)
                    act[at // 2048, :, at % 2048 : at % 2048 + 128] = low[:, part]
                    layer_sums[layer, 3 + at // LANES : 4 + at // LANES, at % LANES : at % LANES + 128] = total[:, part]
            prefetch(fetch_final(half) + fetch_slope(half))
        fetched(fetch_hidden())
        for n in range(0, LANES, TILE):
            block = m_hidden[n // TILE].reshape(TILE, 4 * LANES)
            acc[:, n : n + TILE] += dot_nt(act[0], block[:, : 2 * LANES]) + dot_nt(act[1], block[:, 2 * LANES :])
        prefetch(fetch_hidden())
        fetched(fetch_norm(0))
        layer_sums[layer, 2:3, :] = norm_back(
            layer, 0, lambda rows: acc[rows, :].astype(jnp.bfloat16).astype(jnp.float32)
        )
        prefetch(fetch_norm(0))

        @pl.when(s == 1)
        def _():
            hand_wait(3, grad, grad_out, 1)

        fetched(fetch_attn())
        for n in range(0, LANES, TILE):
            block = m_attn[n // TILE].reshape(TILE, LANES)
            grad[:, n : n + TILE] = dot_nt(hid[...], block).astype(jnp.bfloat16)
        prefetch(fetch_attn())
        fetched(fetch_heads())

        def one_pair(p, _):
            wait(fetch_probs(layer, p))
            at = pl.multiple_of(p * 128, 128)
            q, k, v = (qkv[:, pl.ds(part * LANES + at, 128)] for part in range(3))
            upper = grad[:, pl.ds(at, 128)]
            product = upper.astype(jnp.float32) * ctx[:, pl.ds(at, 128)].astype(jnp.float32)
            q_t, upper_t = q.T, upper.T
            grad_q = None
            grad_k, grad_v = [], []
            for half in range(2):
                weights = probs[p % 2, half]
                delta = jnp.sum(lane_half(product, half), -1, keepdims=True)
                scores = dot_nt(lane_half(upper, half), v)
                low = (weights.astype(jnp.float32) * (scores - delta)).astype(jnp.bfloat16)
                part = dot_nn(low, lane_half(k, half))
                grad_q = part if grad_q is None else grad_q + part
                here = slice(half * HEAD_DIM, (half + 1) * HEAD_DIM)
                grad_k.append(dot_nn(q_t[here], low))
                grad_v.append(dot_nn(upper_t[here], weights))
            back_q = (grad_q * 0.125).astype(jnp.bfloat16)
            back_v = jnp.concatenate(grad_v, 0).astype(jnp.bfloat16).T
            proj_grad[:, pl.ds(at, 128)] = back_q
            proj_grad[:, pl.ds(LANES + at, 128)] = jnp.concatenate(grad_k, 0).astype(jnp.bfloat16).T
            proj_grad[:, pl.ds(2 * LANES + at, 128)] = back_v
            layer_sums[layer, 0:1, pl.ds(at, 128)] = column_sum(back_q)
            layer_sums[layer, 1:2, pl.ds(at, 128)] = column_sum(back_v)

            @pl.when(p < 6)
            def _():
                start(fetch_probs(layer, p + 2))

            return 0

        lax.fori_loop(0, 8, one_pair, 0)
        prefetch(fetch_heads() + fetch_probs(0, 0) + fetch_probs(0, 1))
        fetched(fetch_qkv())

        def columns_of(n):
            block = m_qkv[n // TILE].reshape(TILE, 3 * LANES)
            columns = slice(n, n + TILE)
            grad[:, columns] = (acc[:, columns] + dot_nt(proj_grad[...], block)).astype(jnp.bfloat16)

        if with_links:

            @pl.when(s == 0)
            def _():
                for n in range(0, LANES, TILE):
                    columns_of(n)

            @pl.when(s == 1)
            def _():
                begin_sums()
                for k, n in enumerate(range(0, LANES, TILE)):
                    columns_of(n)
                    then_sums(k)

        else:
            for n in range(0, LANES, TILE):
                columns_of(n)
        prefetch(fetch_qkv())
        hand_start(2 + layer, grad, grad_out, layer)
        return 0

    lax.fori_loop(0, 2, one_layer, 0)
    hand_wait(1, x, y_out, 1)
    hand_wait(2, grad, grad_out, 0)
    if with_links:
        hand_arrived(sec, x, y_out)
        hand_arrived(2 + sec, grad, grad_out)
        end_links()
    else:
        sums[...] = layer_sums[...]


def both_layers(weights, tokens, cotangent, segments, lengths, vectors):
    with_links = len(weights) == 4
    low, wide_type = jnp.bfloat16, jnp.float32
    in_hbm = pl.BlockSpec(memory_space=pltpu.HBM)
    in_vmem = pl.BlockSpec(memory_space=pltpu.VMEM)
    in_smem = pl.BlockSpec(memory_space=pltpu.SMEM)
    shape = jax.ShapeDtypeStruct
    sums = (8, LANES) if with_links else (2, 8, LANES)
    outs = [shape((ITEMS, 4, 2, 2, BLOCK, LANES), low)] if with_links else []
    outs += [
        shape((2, SEQ, LANES), low),
        shape((2, SEQ, LANES), low),
        shape(sums, wide_type),
        shape((2, PAIRS, 2, SEQ, SEQ), low),
        shape((SEQ, 3 * LANES), low),
        shape((SEQ, LANES), low),
        shape((2, SEQ, 2 * LANES), low),
        shape((2, SEQ, LANES), low),
        shape((2, SEQ, 128), wide_type),
    ]
    out_specs = [in_hbm] * len(outs)
    out_specs[3 if with_links else 2] = in_vmem
    dma = pltpu.SemaphoreType.DMA
    scratch = [
        pltpu.VMEM((SEQ, LANES), low),
        pltpu.VMEM((2, 16, LANES), wide_type),
        pltpu.VMEM((4, 2, 2, BLOCK, 3 * LANES), low),
        pltpu.VMEM((4, 2, 2, BLOCK, LANES), low),
        pltpu.VMEM((4, 2, 2, BLOCK, 4 * LANES), low),
        pltpu.VMEM((2, 4, 2, 2, 2 * BLOCK, LANES), low),
        pltpu.VMEM((SEQ, 3 * LANES), low),
        pltpu.VMEM((SEQ, LANES), low),
        pltpu.VMEM((SEQ, LANES), low),
        pltpu.VMEM((2, SEQ, 2 * LANES), low),
        pltpu.VMEM((2, SEQ, 2 * LANES), low),
        pltpu.VMEM((SEQ, LANES), wide_type),
        pltpu.VMEM((SEQ, SEQ), wide_type),
        pltpu.VMEM((2, 2, SEQ, SEQ), low),
        pltpu.VMEM((2, SEQ, LANES), low),
        pltpu.VMEM((2, SEQ, 128), wide_type),
        pltpu.VMEM((SEQ, LANES), low),
        pltpu.VMEM((SEQ, 3 * LANES), low),
        pltpu.VMEM((2, 8, LANES), wide_type),
        dma((3,)),
        dma((PER_LAYER,)),
        dma((2,)),
        dma((7,)),
        dma((PER_LAYER,)),
        dma((8,)),
        dma((4,)),
    ]
    if with_links:
        specs = [in_hbm] * 6 + [in_vmem, in_smem] + [in_vmem] * 7
        scratch += [
            pltpu.VMEM((PER_LAYER, HALF, LANES), low),
            pltpu.VMEM((8, LANES), wide_type),
            pltpu.VMEM((3, 8, LANES), wide_type),
            pltpu.VMEM((3, 8, LANES), wide_type),
            pltpu.VMEM((8, LANES), wide_type),
            pltpu.VMEM((8, LANES), wide_type),
            dma((PER_LAYER,)),
            dma((PER_LAYER,)),
            dma((PER_LAYER,)),
            dma((PER_LAYER,)),
            dma((17,)),
            dma((17, ITEMS)),
            dma((2,)),
            dma((4,)),
            dma((4,)),
            dma((7,)),
            dma((7,)),
        ]
        params = pltpu.CompilerParams(collective_id=0, has_side_effects=True, vmem_limit_bytes=VMEM_LIMIT)
    else:
        specs = [in_hbm] * 3 + [in_vmem, in_smem, in_hbm]
        params = pltpu.CompilerParams(vmem_limit_bytes=VMEM_LIMIT)
    results = pl.pallas_call(
        partial(layers_kernel, with_links),
        out_shape=tuple(outs),
        in_specs=specs,
        out_specs=tuple(out_specs),
        scratch_shapes=scratch,
        compiler_params=params,
    )(*weights, tokens, cotangent, segments, lengths, *vectors)
    return results[1:4] if with_links else results[:3]


def gather(w_qkv, w_out, w_in, w_ffn_out):
    matrices = [lax.all_gather(w[0], "dp", axis=0, tiled=True) for w in (w_qkv, w_out, w_in, w_ffn_out)]
    qkv, attn, hidden, final = matrices
    blocks = [qkv[:, b * LANES : (b + 1) * LANES] for b in range(3)] + [attn]
    blocks += [hidden[:, b * LANES : (b + 1) * LANES] for b in range(4)]
    final = final.reshape(16, 4, BLOCK, LANES).transpose(1, 0, 2, 3).reshape(4, 1024, LANES)
    own = jnp.concatenate([jnp.stack(blocks), final])
    return lax.all_gather(own, "section", axis=0, tiled=True).reshape(24, 4, 2, 2, BLOCK, LANES)


def on_device(
    tokens,
    segment_ids,
    row_lengths,
    w_qkv,
    w_out,
    w_in,
    w_ffn_out,
    bias_q,
    bias_v,
    bias_out,
    bias_in,
    bias_ffn_out,
    ln_gain,
    ln_shift,
    out_cotangent,
):
    weights = (w_qkv, w_out, w_in, w_ffn_out)
    vectors = (bias_q, bias_v, bias_out, bias_in, bias_ffn_out, ln_gain, ln_shift)
    data = (tokens, out_cotangent, segment_ids, row_lengths)
    if w_qkv.shape[1] == BLOCK:
        tops, grads, sums = both_layers(weights, *data, vectors)
    else:
        sec = lax.axis_index("section")
        wide_in, gains, shifts = bias_in.reshape(4, LANES), ln_gain[0], ln_shift[0]
        vec = jnp.concatenate(
            [bias_q, bias_v, bias_out, wide_in, bias_ffn_out, gains, shifts, jnp.zeros((4, LANES))]
        )
        vec = lax.all_gather(vec, "section", axis=0)
        tops, grads, sums = both_layers((gather(*weights),), *data, (vec,))

        def swap(array):
            return lax.ppermute(array, "section", [(0, 1), (1, 0)])

        def placed(both):
            got = swap(jnp.where(sec == 0, both[1], both[0]))
            return jnp.where(sec == 0, jnp.stack([both[0], got]), jnp.stack([got, both[1]]))

        tops, grads = placed(tops), placed(grads)
        sums = jnp.where(sec == 0, sums[0], sums[1]) + swap(jnp.where(sec == 0, sums[1], sums[0]))
        sums = lax.psum(sums, "dp")
    totals = (sums[0:1], sums[1:2], sums[2:3], sums[3:7].reshape(1, 4 * LANES), sums[7:8])
    return (tops[None, :, None], grads[None, :, None]) + totals


def solution(mesh):
    placed = (
        P(None, "dp", None, None),
        P(None, "dp", None),
        P(None, "dp"),
        P("section", "dp", None),
        P("section", "dp", None),
        P("section", "dp", None),
        P("section", "dp", None),
        P("section", None),
        P("section", None),
        P("section", None),
        P("section", None),
        P("section", None),
        P("section", None, None),
        P("section", None, None),
        P(None, "dp", None, None),
    )
    return jax.shard_map(
        on_device,
        mesh=mesh,
        in_specs=placed,
        out_specs=(
            P("section", None, "dp", None, None),
            P("section", None, "dp", None, None),
            P("section", None),
            P("section", None),
            P("section", None),
            P("section", None),
            P("section", None),
        ),
        check_vma=False,
    )
```

```python
from functools import partial
import math

import jax
import jax.numpy as jnp
from jax import lax
from jax.experimental import pallas as pl
from jax.experimental.pallas import tpu as pltpu
from jax.sharding import PartitionSpec as P

HEAD_DIM = 64
SEQ = 512
GROUPS = 4
epsilon = 1e-06
VMEM_LIMIT = 60 * 2**20
MESH = pl.DeviceIdType.MESH
ITEMS = 24
PER_LAYER = ITEMS // 2
LANES = 1024
BLOCK = 64
HALF = BLOCK // 2
CUT = 384
STAGES = (1, 2, 3, 4, 6)
LOAD = 7
FRONT = 6
SETTLE = 3
TILE = 256


def link_plan(wq, wo, wi, wf, full, vec, stage, in_sem, place_sem, cross_send, cross_recv, send_sem, recv_sem, vec_sem):
    sec = lax.axis_index("section")
    chip = lax.axis_index("dp")
    per_layer, items = PER_LAYER, ITEMS
    z = chip // 4
    y = (chip // 2) % 2
    x = chip % 2
    dev_x = (sec, z * 4 + y * 2 + 1 - x)
    dev_y = (sec, z * 4 + (1 - y) * 2 + x)
    dev_xy = (sec, z * 4 + (1 - y) * 2 + 1 - x)
    dev_up = (sec, jnp.minimum(z + 1, 3) * 4 + y * 2 + x)
    dev_down = (sec, jnp.maximum(z - 1, 0) * 4 + y * 2 + x)
    dev_core = (1 - sec, chip)
    in_plane = (dev_x, dev_y, dev_xy)
    along_z = tuple((sec, ((z + k) % 4) * 4 + y * 2 + x) for k in (1, 2, 3))

    def own_block(b, row):
        if b < 3:
            return wq.at[0, pl.ds(row, HALF), b * LANES : (b + 1) * LANES]
        if b == 3:
            return wo.at[0, pl.ds(row, HALF), :]
        if b < 8:
            return wi.at[0, pl.ds(row, HALF), (b - 4) * LANES : (b - 3) * LANES]
        return wf.at[0, pl.ds((b - 8) * BLOCK + row, HALF), :]

    mine = pl.multiple_of(sec * HALF, HALF)
    other = pl.multiple_of((1 - sec) * HALF, HALF)

    def to_stage(b):
        return pltpu.make_async_copy(own_block(b, mine), stage.at[b], in_sem.at[b])

    def to_place(b):
        return pltpu.make_async_copy(
            stage.at[b], full.at[sec * per_layer + b, z, y, x, pl.ds(mine, HALF), :], place_sem.at[b]
        )

    def cross(b):
        return pltpu.make_async_remote_copy(
            src_ref=own_block(b, other),
            dst_ref=full.at[sec * per_layer + b, z, y, x, pl.ds(other, HALF), :],
            send_sem=cross_send.at[b],
            recv_sem=cross_recv.at[b],
            device_id=dev_core,
            device_id_type=MESH,
        )

    def give_vec(where):
        return pltpu.make_async_remote_copy(
            src_ref=where,
            dst_ref=where,
            send_sem=vec_sem.at[0],
            recv_sem=vec_sem.at[1],
            device_id=dev_core,
            device_id_type=MESH,
        )

    def begin():
        for b in range(per_layer):
            to_stage(b).start()
        barrier = pltpu.get_barrier_semaphore()
        for k in range(1, 32):
            device = ((sec + k // 16) % 2, (chip + k) % 16)
            pl.semaphore_signal(barrier, inc=1, device_id=device, device_id_type=MESH)
        pl.semaphore_wait(barrier, 31)
        for b in range(per_layer):
            cross(b).start()
        give_vec(vec.at[sec]).start()
        for b in range(per_layer):
            to_stage(b).wait()
            to_place(b).start()

    def vec_here():
        give_vec(vec.at[sec]).wait_send()
        give_vec(vec.at[1 - sec]).wait_recv()

    def copy(ref, kind, item, device):
        return pltpu.make_async_remote_copy(
            src_ref=ref,
            dst_ref=ref,
            send_sem=send_sem.at[kind],
            recv_sem=recv_sem.at[kind, item],
            device_id=device,
            device_id_type=MESH,
        )

    def views(core):
        rows = slice(core * HALF, (core + 1) * HALF)
        first, last = slice(0, CUT), slice(CUT, LANES)
        if core == 0:
            pair = lambda i, at: full.at[i, at, :, x, rows, last]
            eight_first = lambda i: full.at[i, :, y, :, rows, first]
            eight_last = lambda i: full.at[i, :, :, x, rows, last]
            towards = (dev_x, dev_y)
        else:
            pair = lambda i, at: full.at[i, at, y, :, rows, last]
            eight_first = lambda i: full.at[i, :, :, x, rows, first]
            eight_last = lambda i: full.at[i, :, y, :, rows, last]
            towards = (dev_y, dev_x)
        return (
            towards,
            lambda i, at: full.at[i, at, y, x, rows, first],
            lambda i: full.at[i, :, y, x, rows, first],
            eight_first,
            lambda i, at: full.at[i, at, y, x, rows, last],
            pair,
            eight_last,
            lambda i: full.at[i, :, :, :, rows, :],
        )

    def z_send(base, block, hop, item, at):
        if at < 3 and at - (hop - 1) >= 0:
            copy(block(item, at - (hop - 1)), base + hop - 1, item, dev_up).start()
        if at > 0 and at + (hop - 1) <= 3:
            copy(block(item, at + (hop - 1)), base + 2 + hop, item, dev_down).start()

    def z_recv(base, block, hop, item, at):
        if at - hop >= 0:
            copy(block(item, at - hop), base + hop - 1, item, dev_up).wait_recv()
        if at + hop <= 3:
            copy(block(item, at + hop), base + 2 + hop, item, dev_down).wait_recv()

    def step_at(t, at, core):
        (dev_u, dev_v), own_a, col_a, eight_a, own_d, pair_d, eight_d, whole = views(core)
        turns = [t - offset for offset in STAGES]

        def live(item):
            return (item >= 0) & (item < items)

        def first_move(item):
            @pl.when(live(item))
            def _():
                layer, b = item // per_layer, item % per_layer

                @pl.when(layer == core)
                def _():
                    pltpu.make_async_copy(
                        stage.at[b], full.at[item, z, y, x, pl.ds(core * HALF, HALF), :], place_sem.at[b]
                    ).wait()

                @pl.when(layer != core)
                def _():
                    mine_there = full.at[item, z, y, x, pl.ds(core * HALF, HALF), :]
                    pltpu.make_async_remote_copy(
                        src_ref=mine_there,
                        dst_ref=mine_there,
                        send_sem=cross_send.at[b],
                        recv_sem=cross_recv.at[b],
                        device_id=dev_core,
                        device_id_type=MESH,
                    ).wait_recv()

                copy(own_d(item, at), 8, item, dev_v).start()

        for lead in range(FRONT):
            first_move(t * FRONT + lead)

        @pl.when(live(t))
        def _():
            z_send(0, own_a, 1, t, at)

        item1 = turns[0]

        @pl.when(live(item1))
        def _():
            z_recv(0, own_a, 1, item1, at)
            z_send(0, own_a, 2, item1, at)
            copy(own_d(item1, at), 8, item1, dev_v).wait_recv()
            z_send(9, pair_d, 1, item1, at)

        item2 = turns[1]

        @pl.when(live(item2))
        def _():
            z_recv(0, own_a, 2, item2, at)
            z_send(0, own_a, 3, item2, at)
            z_recv(9, pair_d, 1, item2, at)
            z_send(9, pair_d, 2, item2, at)

        item3 = turns[2]

        @pl.when(live(item3))
        def _():
            z_recv(0, own_a, 3, item3, at)
            copy(col_a(item3), 6, item3, dev_u).start()
            z_recv(9, pair_d, 2, item3, at)
            z_send(9, pair_d, 3, item3, at)

        item4 = turns[3]

        @pl.when(live(item4))
        def _():
            copy(col_a(item4), 6, item4, dev_u).wait_recv()
            copy(eight_a(item4), 7, item4, dev_v).start()
            z_recv(9, pair_d, 3, item4, at)
            copy(eight_d(item4), 15, item4, dev_u).start()

        item5 = turns[4]

        @pl.when(live(item5))
        def _():
            copy(eight_a(item5), 7, item5, dev_v).wait_recv()
            copy(eight_d(item5), 15, item5, dev_u).wait_recv()
            copy(whole(item5), 16, item5, dev_core).start()

    def step(t):
        for at in range(4):
            for core in range(2):

                @pl.when((z == at) & (sec == core))
                def _():
                    step_at(t, at, core)

    def arrived(item):
        for core in range(2):

            @pl.when(sec == core)
            def _():
                copy(views(1 - core)[-1](item), 16, item, dev_core).wait_recv()

    def end():
        for b in range(per_layer):
            cross(b).wait_send()
        for core in range(2):

            @pl.when(sec == core)
            def _():
                _, own_a, col_a, eight_a, own_d, pair_d, eight_d, whole = views(core)
                every = slice(None)

                def sent(ref, kind):
                    copy(ref, kind, 0, dev_core).wait_send()

                sent(whole(every), 16)
                sent(col_a(every), 6)
                sent(eight_a(every), 7)
                sent(eight_d(every), 15)
                sent(own_d(every, 0), 8)
                for hop in (1, 2, 3):
                    for base, block in ((0, own_a), (9, pair_d)):

                        @pl.when((z < 3) & (z - (hop - 1) >= 0))
                        def _():
                            sent(block(every, 0), base + hop - 1)

                        @pl.when((z > 0) & (z + (hop - 1) <= 3))
                        def _():
                            sent(block(every, 0), base + 2 + hop)

    return begin, vec_here, step, arrived, end, dev_core, in_plane, along_z


def wide(ref, columns):
    block = ref[:, :, :, :, columns]
    return block.reshape(-1, block.shape[-1])


def dot_nt(left, right):
    return lax.dot_general(left, right, (((1,), (1,)), ((), ())), preferred_element_type=jnp.float32)


def dot_nn(left, right):
    return jnp.dot(left, right, preferred_element_type=jnp.float32)


def pair_bias(codes):
    down = jnp.broadcast_to(codes, (128, codes.shape[1])).T[:, :1]
    return jnp.where(down == codes, 0.0, -1000000000.0)


def lane_half(pair, half):
    lanes = lax.broadcasted_iota(jnp.int32, pair.shape, 1)
    return jnp.where((lanes < HEAD_DIM) == (half == 0), pair, jnp.zeros_like(pair))


def layers_kernel(with_links, *refs):
    if with_links:
        wq, wo, wi, wf, *refs = refs
    else:
        full, *refs = refs
    tokens, cotangent, segments, lengths, *refs = refs
    if with_links:
        parts, refs = refs[:7], refs[7:]
        full, *refs = refs
    else:
        given_vec, *refs = refs
    (y_out, grad_out, sums, prob_save, qkv_save, ctx_save, slope_save, norm_save, inv_save, *refs) = refs
    (x, vec, m_qkv, m_attn, m_hidden, m_final, qkv, ctx, hid, act, slope, acc, bias, probs, norms, invs, *refs) = refs
    (grad, proj_grad, layer_sums, head_sums, in_sem, load_sem, p_sem, save_sem, m_sem, sem, out_sem, *refs) = refs
    sec = lax.axis_index("section")
    if with_links:
        (stage, got_core, got_plane, got_z, got_late, part_core, part_plane, *link_sems) = refs
        *link_sems, ex_send, ex_recv, sum_send, sum_recv, late_sent, late_got = link_sems

    def start(copies):
        for copy in copies:
            copy.start()

    def wait(copies):
        for copy in copies:
            copy.wait()

    take_x = pltpu.make_async_copy(tokens.at[sec, 0], x, in_sem.at[0])
    take_grad = pltpu.make_async_copy(cotangent.at[sec, 0], grad, in_sem.at[1])
    take_x.start()
    take_grad.start()
    head_sums[...] = jnp.zeros_like(head_sums)
    if with_links:
        bias_q, bias_v, bias_out, bias_in, bias_ffn_out, ln_gain, ln_shift = parts
        for k, ref in enumerate((bias_q, bias_v, bias_out)):
            vec[sec, k : k + 1, :] = ref[...]
        for k in range(4):
            vec[sec, 3 + k : 4 + k, :] = bias_in[:, k * LANES : (k + 1) * LANES]
        vec[sec, 7:8, :] = bias_ffn_out[...]
        vec[sec, 8:10, :] = ln_gain[0]
        vec[sec, 10:12, :] = ln_shift[0]
        vec[sec, 12:16, :] = jnp.zeros((4, LANES), jnp.float32)
        begin_links, vec_here, step_links, arrived, end_links, dev_core, in_plane, along_z = link_plan(
            wq, wo, wi, wf, full, vec, stage, *link_sems
        )
        begin_links()
    else:
        take_vec = pltpu.make_async_copy(given_vec, vec, in_sem.at[2])
        take_vec.start()

    def settle():
        valid = lax.broadcasted_iota(jnp.int32, (1, SEQ), 1) < lengths[0, sec]
        bias[...] = pair_bias(segments[sec] * 2 + valid.astype(jnp.int32))
        take_x.wait()
        if with_links:
            vec_here()
        else:
            take_vec.wait()

    def row(layer, index):
        return vec[layer, index : index + 1, :]

    def hand_over(which, source, out, layer):
        local = pltpu.make_async_copy(source, out.at[sec], out_sem.at[which])
        if with_links:
            far = pltpu.make_async_remote_copy(
                src_ref=source,
                dst_ref=out.at[sec],
                send_sem=ex_send.at[which],
                recv_sem=ex_recv.at[which],
                device_id=dev_core,
                device_id_type=MESH,
            )
            return local, far
        return (pltpu.make_async_copy(source, out.at[layer], out_sem.at[which]),)

    def hand_start(which, source, out, layer):
        copies = hand_over(which, source, out, layer)
        if with_links:

            @pl.when(layer == sec)
            def _():
                copies[0].start()

            @pl.when(layer != sec)
            def _():
                copies[1].start()

        else:
            copies[0].start()

    def hand_wait(which, source, out, layer):
        copies = hand_over(which, source, out, layer)
        if with_links:

            @pl.when(layer == sec)
            def _():
                copies[0].wait()

            @pl.when(layer != sec)
            def _():
                copies[1].wait_send()

        else:
            copies[0].wait()

    def hand_arrived(which, source, out):
        pltpu.make_async_remote_copy(
            src_ref=source,
            dst_ref=out.at[1 - sec],
            send_sem=ex_send.at[which],
            recv_sem=ex_recv.at[which],
            device_id=dev_core,
            device_id_type=MESH,
        ).wait_recv()

    def load(item):
        b = item % PER_LAYER

        def into(b):
            if b < 3:
                return m_qkv.at[:, :, :, :, b * LANES : (b + 1) * LANES]
            if b == 3:
                return m_attn
            if b < 8:
                return m_hidden.at[:, :, :, :, (b - 4) * LANES : (b - 3) * LANES]
            return m_final.at[(b - 8) // 2, :, :, :, ((b - 8) % 2) * BLOCK : ((b - 8) % 2 + 1) * BLOCK, :]

        for k in range(PER_LAYER):

            @pl.when(b == k)
            def _():
                pltpu.make_async_copy(full.at[item], into(k), load_sem.at[k]).start()

    def loaded(b):
        pltpu.make_async_copy(full.at[0], m_attn, load_sem.at[b]).wait()

    def project(layer, b):
        scale = jnp.where(b == 0, 0.125, 1.0)
        shift = jnp.where(b == 0, row(layer, 0), jnp.where(b == 2, row(layer, 1), 0.0))
        at = pl.multiple_of(b * LANES, LANES)
        for n in range(0, LANES, TILE):
            columns = pl.ds(at + n, TILE)
            out = dot_nn(x[...], wide(m_qkv, columns)) + shift[:, n : n + TILE]
            qkv[:, columns] = (out.astype(jnp.bfloat16).astype(jnp.float32) * scale).astype(jnp.bfloat16)

    def save_p(layer, p):
        group, k = p // 2, p % 2
        return pltpu.make_async_copy(probs.at[group % 2, k], prob_save.at[layer, group, k], p_sem.at[p % 4])

    def attend(layer, first, last):
        def one(p, _):
            @pl.when(p >= 4)
            def _():
                save_p(layer, p - 4).wait()

            at = pl.multiple_of(p * 128, 128)
            q, k, v = (qkv[:, pl.ds(part * LANES + at, 128)] for part in range(3))
            total = None
            for half in range(2):
                scores = dot_nt(lane_half(q, half), k) + bias[...]
                exps = jnp.exp(scores - jnp.max(scores, -1, keepdims=True))
                share = (exps / jnp.sum(exps, -1, keepdims=True)).astype(jnp.bfloat16)
                probs[(p // 2) % 2, p % 2, half] = share
                out = dot_nn(share, lane_half(v, half))
                total = out if total is None else total + out
            ctx[:, pl.ds(at, 128)] = total.astype(jnp.bfloat16)
            save_p(layer, p).start()
            return 0

        lax.fori_loop(first, last, one, 0)

    def save(which):
        pairs = (
            (qkv, qkv_save),
            (ctx, ctx_save),
            (slope, slope_save),
            (norms.at[0], norm_save.at[0]),
            (invs.at[0], inv_save.at[0]),
            (norms.at[1], norm_save.at[1]),
            (invs.at[1], inv_save.at[1]),
        )
        return pltpu.make_async_copy(*pairs[which], save_sem.at[which])

    def normalize(layer, which, put):
        for r in range(0, SEQ, 128):
            rows = slice(r, r + 128)
            residual = acc[rows, :]
            centered = residual - jnp.mean(residual, -1, keepdims=True)
            inverse = lax.rsqrt(jnp.mean(centered * centered, -1, keepdims=True) + epsilon)
            normed = centered * inverse
            norms[which, rows, :] = normed.astype(jnp.bfloat16)
            invs[which, rows, :] = jnp.broadcast_to(inverse, (128, 128))
            put[rows, :] = (normed * row(layer, 8 + which) + row(layer, 10 + which)).astype(jnp.bfloat16)

    def attn_out(layer):
        for n in range(0, LANES, TILE):
            columns = slice(n, n + TILE)
            acc[:, columns] = x[:, columns].astype(jnp.float32) + (
                dot_nn(ctx[...], wide(m_attn, columns)) + row(layer, 2)[:, columns]
            )
        normalize(layer, 0, hid)

    def ffn_in(layer, j):
        shift = vec[layer, pl.ds(3 + j, 1), :]
        at = pl.multiple_of(j * LANES, LANES)
        for n in range(0, LANES, TILE):
            pre = dot_nn(hid[...], wide(m_hidden, pl.ds(at + n, TILE))) + shift[:, n : n + TILE]
            cdf = 0.5 * (1.0 + lax.erf(pre * math.sqrt(0.5)))
            pdf = jnp.exp(pre * pre * -0.5) * (1.0 / math.sqrt(2.0 * math.pi))
            value = (pre * cdf).astype(jnp.bfloat16)
            grade = (cdf + pre * pdf).astype(jnp.bfloat16)
            to = pl.ds(pl.multiple_of(j * 512 + n // 2, 128), 128)
            for half in range(2):
                act[half, :, to] = value[:, half * 128 : (half + 1) * 128]
                slope[half, :, to] = grade[:, half * 128 : (half + 1) * 128]

    def ffn_out(layer, half):
        for n in range(0, LANES, TILE):
            columns = slice(n, n + TILE)
            out = dot_nn(act[half], wide(m_final.at[half], columns))
            if half == 0:
                acc[:, columns] = hid[:, columns].astype(jnp.float32) + (out + row(layer, 7)[:, columns])
            else:
                acc[:, columns] += out

    def compute(c):
        layer, b = c // PER_LAYER, c % PER_LAYER

        def lower(then):
            pl.when(layer == 0)(then)

        @pl.when(b <= 2)
        def _():
            loaded(b)

            @pl.when((b == 0) & (layer == 1))
            def _():
                wait([save(5), save(6)])

            project(layer, b)

        @pl.when(b == 2)
        def _():
            lower(lambda: start([save(0)]))
            attend(layer, 0, 2)

        @pl.when(b == 3)
        def _():
            loaded(3)
            attend(layer, 2, 5)

        @pl.when(b == 4)
        def _():
            loaded(4)
            attend(layer, 5, 8)

        @pl.when(b == 5)
        def _():
            lower(lambda: start([save(1)]))
            loaded(5)
            attn_out(layer)
            lower(lambda: start([save(3), save(4)]))

        @pl.when((b >= 5) & (b <= 8))
        def _():
            ffn_in(layer, b - 5)

        @pl.when(b == 6)
        def _():
            loaded(6)
            wait([save_p(layer, p) for p in range(4, 8)])
            lower(lambda: wait([save(0), save(1)]))

        @pl.when(b == 7)
        def _():
            loaded(7)

        @pl.when(b == 8)
        def _():
            lower(lambda: start([save(2)]))
            loaded(8)

        @pl.when(b == 9)
        def _():
            loaded(9)

            @pl.when(layer == 1)
            def _():
                hand_wait(0, x, y_out, 0)

            ffn_out(layer, 0)
            lower(lambda: wait([save(3), save(4)]))

        @pl.when(b == 10)
        def _():
            loaded(10)
            lower(lambda: wait([save(2)]))

        @pl.when(b == 11)
        def _():
            loaded(11)
            ffn_out(layer, 1)
            normalize(layer, 1, x)
            lower(lambda: start([save(5), save(6)]))
            hand_start(layer, x, y_out, layer)

    def step(t, _):
        if with_links:
            step_links(t)

        @pl.when(t == SETTLE)
        def _():
            settle()

        first = t - LOAD

        @pl.when((first >= 0) & (first < ITEMS))
        def _():
            if with_links:
                arrived(first)
            load(first)

        second = t - LOAD - 1

        @pl.when((second >= 0) & (second < ITEMS))
        def _():
            compute(second)

        return 0

    lax.fori_loop(0, ITEMS + LOAD + 1, step, 0)
    def fetch_final(half):
        return [
            pltpu.make_async_copy(
                full.at[8 + 2 * half + g],
                m_final.at[half, :, :, :, g * BLOCK : (g + 1) * BLOCK, :],
                m_sem.at[2 * half + g],
            )
            for g in range(2)
        ]

    def fetch_hidden():
        return [
            pltpu.make_async_copy(
                full.at[4 + j], m_hidden.at[:, :, :, :, j * LANES : (j + 1) * LANES], m_sem.at[4 + j]
            )
            for j in range(4)
        ]

    def fetch_attn():
        return [pltpu.make_async_copy(full.at[3], m_attn, m_sem.at[8])]

    def fetch_qkv():
        return [
            pltpu.make_async_copy(full.at[j], m_qkv.at[:, :, :, :, j * LANES : (j + 1) * LANES], m_sem.at[9 + j])
            for j in range(3)
        ]

    def fetch_norm(which):
        return [
            pltpu.make_async_copy(norm_save.at[which], norms.at[which], sem.at[2 * which]),
            pltpu.make_async_copy(inv_save.at[which], invs.at[which], sem.at[2 * which + 1]),
        ]

    def fetch_slope(half):
        return [pltpu.make_async_copy(slope_save.at[half], slope.at[half], sem.at[4 + half])]

    def fetch_heads():
        return [
            pltpu.make_async_copy(qkv_save, qkv, sem.at[6]),
            pltpu.make_async_copy(ctx_save, ctx, sem.at[7]),
        ]

    def fetch_probs(layer, group):
        return [pltpu.make_async_copy(prob_save.at[layer, group], probs.at[group % 2], p_sem.at[group % 2])]

    start(fetch_probs(1, 0) + fetch_probs(1, 1))
    take_grad.wait()

    def column_sum(values):
        return jnp.sum(values.astype(jnp.float32), 0, keepdims=True)

    def norm_back(layer, which, upstream_of):
        gain = vec[layer, 8 + which : 9 + which, :]
        total = jnp.zeros((1, LANES), jnp.float32)
        for r in range(0, SEQ, 128):
            rows = slice(r, r + 128)
            upstream = upstream_of(rows) * gain
            normed = norms[which, rows, :].astype(jnp.float32)
            back = invs[which, rows, 0:1] * (
                upstream
                - jnp.mean(upstream, -1, keepdims=True)
                - normed * jnp.mean(upstream * normed, -1, keepdims=True)
            )
            acc[rows, :] = back
            low = back.astype(jnp.bfloat16)
            hid[rows, :] = low
            total = total + column_sum(low)
        return total

    def sum_copy(source, target, k, device):
        return pltpu.make_async_remote_copy(
            src_ref=source,
            dst_ref=target,
            send_sem=sum_send.at[k],
            recv_sem=sum_recv.at[k],
            device_id=device,
            device_id_type=MESH,
        )

    def spread_heads(target, where, group, heads):
        for row in range(2):
            for k in range(2):
                at = (2 * group + k) * 128
                target[where, row : row + 1, at : at + 128] = heads[2 * row + k : 2 * row + k + 1, :]

    def core_sums():
        return [sum_copy(layer_sums.at[1 - sec], got_core, 0, dev_core)]

    def plane_sums():
        return [sum_copy(part_core, got_plane.at[k], 1 + k, device) for k, device in enumerate(in_plane)]

    def z_sums():
        return [sum_copy(part_plane, got_z.at[k], 4 + k, device) for k, device in enumerate(along_z)]

    def begin_early():
        layer_sums[0, 0:2, :] = jnp.zeros((2, LANES), jnp.float32)
        for group in range(GROUPS):
            spread_heads(layer_sums, 1, group, head_sums[1, group])
        start(core_sums())

    def early_sums(k):
        @pl.when(k == 0)
        def _():
            wait(core_sums())
            part_core[...] = layer_sums[sec] + got_core[...]
            start(plane_sums())

        @pl.when(k == 2)
        def _():
            wait(plane_sums())
            part_plane[...] = part_core[...] + (got_plane[0] + got_plane[1]) + got_plane[2]
            start(z_sums())

    def end_early():
        wait(z_sums())
        sums[0] = part_plane[...] + (got_z[0] + got_z[1]) + got_z[2]

    def late_send(group):
        own = 16 * sec + lax.axis_index("dp")
        got_late[group, own] = head_sums[0, group]

        def one(k, _):
            sum_late(group, own, (0, (lax.axis_index("dp") + k) % 16)).start()
            return 0

        lax.fori_loop(1, 16, one, 0)

        @pl.when(sec == 1)
        def _():
            sum_late(group, own, dev_core).start()

    def sum_late(group, slot, device):
        return pltpu.make_async_remote_copy(
            src_ref=head_sums.at[0, group],
            dst_ref=got_late.at[group, slot],
            send_sem=late_sent.at[group],
            recv_sem=late_got.at[group],
            device_id=device,
            device_id_type=MESH,
        )

    def end_late():
        def many(group, count):
            several = got_late.at[group, pl.ds(0, count)]
            return pltpu.make_async_remote_copy(
                src_ref=several,
                dst_ref=several,
                send_sem=late_sent.at[group],
                recv_sem=late_got.at[group],
                device_id=dev_core,
                device_id_type=MESH,
            )

        for group in range(GROUPS):
            for core in range(2):

                @pl.when(sec == core)
                def _():
                    many(group, 15 + core).wait_send()
                    if core == 0:
                        many(group, 31).wait_recv()
                        spread_heads(sums, 0, group, jnp.sum(got_late[group], 0))

    def one_layer(s, _):
        layer = 1 - s

        def prefetch(copies):
            @pl.when(s == 0)
            def _():
                start(copies)

        def fetched(copies):
            @pl.when(s == 1)
            def _():
                wait(copies)

        fetched(fetch_norm(1))
        layer_sums[layer, 7:8, :] = norm_back(layer, 1, lambda rows: grad[rows, :].astype(jnp.float32))
        prefetch(fetch_norm(1))
        for half in range(2):
            fetched(fetch_final(half) + fetch_slope(half))
            for n in range(0, 2048, TILE):
                chip = n // 128
                block = m_final[half, chip // 4, (chip // 2) % 2].reshape(TILE, LANES)
                back = dot_nt(hid[...], block) * slope[half, :, n : n + TILE].astype(jnp.float32)
                low = back.astype(jnp.bfloat16)
                total = column_sum(low)
                for k in range(2):
                    at = (chip + k) * 256 + half * 128
                    part = slice(k * 128, (k + 1) * 128)
                    act[at // 2048, :, at % 2048 : at % 2048 + 128] = low[:, part]
                    layer_sums[layer, 3 + at // LANES : 4 + at // LANES, at % LANES : at % LANES + 128] = total[:, part]
            prefetch(fetch_final(half) + fetch_slope(half))
        fetched(fetch_hidden())
        for n in range(0, LANES, TILE):
            block = m_hidden[n // TILE].reshape(TILE, 4 * LANES)
            acc[:, n : n + TILE] += dot_nt(act[0], block[:, : 2 * LANES]) + dot_nt(act[1], block[:, 2 * LANES :])
        prefetch(fetch_hidden())
        fetched(fetch_norm(0))
        layer_sums[layer, 2:3, :] = norm_back(
            layer, 0, lambda rows: acc[rows, :].astype(jnp.bfloat16).astype(jnp.float32)
        )
        prefetch(fetch_norm(0))

        @pl.when(s == 1)
        def _():
            hand_wait(3, grad, grad_out, 1)

        fetched(fetch_attn())
        for n in range(0, LANES, TILE):
            block = m_attn[n // TILE].reshape(TILE, LANES)
            grad[:, n : n + TILE] = dot_nt(hid[...], block).astype(jnp.bfloat16)
        prefetch(fetch_attn())
        fetched(fetch_heads())

        def one_group(group, _):
            wait(fetch_probs(layer, group))
            for k in range(2):
                one_pair(2 * group + k, group, k, probs.at[group % 2, k])

            @pl.when(group < GROUPS - 2)
            def _():
                start(fetch_probs(layer, group + 2))

            if with_links:

                @pl.when(s == 1)
                def _():
                    late_send(group)
                    early_sums(group)

            return 0

        def one_pair(p, group, k, shares):
            at = pl.multiple_of(p * 128, 128)
            q, keys, v = (qkv[:, pl.ds(part * LANES + at, 128)] for part in range(3))
            upper = grad[:, pl.ds(at, 128)]
            product = upper.astype(jnp.float32) * ctx[:, pl.ds(at, 128)].astype(jnp.float32)
            q_t, k_t, upper_t = q.T, keys.T, upper.T
            grad_q, grad_k, grad_v = [], [], []
            for half in range(2):
                weights = shares[half]
                delta = jnp.sum(lane_half(product, half), -1, keepdims=True)
                scores = dot_nt(lane_half(upper, half), v)
                low = (weights.astype(jnp.float32) * (scores - delta)).astype(jnp.bfloat16)
                here = slice(half * HEAD_DIM, (half + 1) * HEAD_DIM)
                grad_q.append(dot_nt(k_t[here], low) * 0.125)
                grad_k.append(dot_nn(q_t[here], low))
                grad_v.append(dot_nn(upper_t[here], weights))
            for part, rows in enumerate((grad_q, grad_k, grad_v)):
                back = jnp.concatenate(rows, 0).astype(jnp.bfloat16).T
                proj_grad[:, pl.ds(part * LANES + at, 128)] = back
                if part != 1:
                    head_sums[layer, group, part + k : part + k + 1, :] = column_sum(back)

        if with_links:

            @pl.when(s == 1)
            def _():
                begin_early()

        lax.fori_loop(0, GROUPS, one_group, 0)
        prefetch(fetch_heads() + fetch_probs(0, 0) + fetch_probs(0, 1))
        fetched(fetch_qkv())

        def columns_of(n):
            block = m_qkv[n // TILE].reshape(TILE, 3 * LANES)
            columns = slice(n, n + TILE)
            grad[:, columns] = (acc[:, columns] + dot_nt(proj_grad[...], block)).astype(jnp.bfloat16)

        if with_links:

            @pl.when(s == 0)
            def _():
                for n in range(0, LANES, TILE):
                    columns_of(n)

            @pl.when(s == 1)
            def _():
                for n in range(0, LANES, TILE):
                    columns_of(n)
                    if n == TILE:
                        end_early()
                end_late()

        else:
            for n in range(0, LANES, TILE):
                columns_of(n)
        prefetch(fetch_qkv())
        hand_start(2 + layer, grad, grad_out, layer)
        return 0

    lax.fori_loop(0, 2, one_layer, 0)
    hand_wait(1, x, y_out, 1)
    hand_wait(2, grad, grad_out, 0)
    if with_links:
        hand_arrived(sec, x, y_out)
        hand_arrived(2 + sec, grad, grad_out)
        end_links()
    else:
        for layer in range(2):
            for group in range(GROUPS):
                spread_heads(layer_sums, layer, group, head_sums[layer, group])
        sums[...] = layer_sums[...]


def both_layers(weights, tokens, cotangent, segments, lengths, vectors):
    with_links = len(weights) == 4
    low, wide_type = jnp.bfloat16, jnp.float32
    in_hbm = pl.BlockSpec(memory_space=pltpu.HBM)
    in_vmem = pl.BlockSpec(memory_space=pltpu.VMEM)
    in_smem = pl.BlockSpec(memory_space=pltpu.SMEM)
    shape = jax.ShapeDtypeStruct
    sums = (1, 8, LANES) if with_links else (2, 8, LANES)
    outs = [shape((ITEMS, 4, 2, 2, BLOCK, LANES), low)] if with_links else []
    outs += [
        shape((2, SEQ, LANES), low),
        shape((2, SEQ, LANES), low),
        shape(sums, wide_type),
        shape((2, GROUPS, 2, 2, SEQ, SEQ), low),
        shape((SEQ, 3 * LANES), low),
        shape((SEQ, LANES), low),
        shape((2, SEQ, 2 * LANES), low),
        shape((2, SEQ, LANES), low),
        shape((2, SEQ, 128), wide_type),
    ]
    out_specs = [in_hbm] * len(outs)
    out_specs[3 if with_links else 2] = in_vmem
    dma = pltpu.SemaphoreType.DMA
    scratch = [
        pltpu.VMEM((SEQ, LANES), low),
        pltpu.VMEM((2, 16, LANES), wide_type),
        pltpu.VMEM((4, 2, 2, BLOCK, 3 * LANES), low),
        pltpu.VMEM((4, 2, 2, BLOCK, LANES), low),
        pltpu.VMEM((4, 2, 2, BLOCK, 4 * LANES), low),
        pltpu.VMEM((2, 4, 2, 2, 2 * BLOCK, LANES), low),
        pltpu.VMEM((SEQ, 3 * LANES), low),
        pltpu.VMEM((SEQ, LANES), low),
        pltpu.VMEM((SEQ, LANES), low),
        pltpu.VMEM((2, SEQ, 2 * LANES), low),
        pltpu.VMEM((2, SEQ, 2 * LANES), low),
        pltpu.VMEM((SEQ, LANES), wide_type),
        pltpu.VMEM((SEQ, SEQ), wide_type),
        pltpu.VMEM((2, 2, 2, SEQ, SEQ), low),
        pltpu.VMEM((2, SEQ, LANES), low),
        pltpu.VMEM((2, SEQ, 128), wide_type),
        pltpu.VMEM((SEQ, LANES), low),
        pltpu.VMEM((SEQ, 3 * LANES), low),
        pltpu.VMEM((2, 8, LANES), wide_type),
        pltpu.VMEM((2, GROUPS, 8, 128), wide_type),
        dma((3,)),
        dma((PER_LAYER,)),
        dma((4,)),
        dma((7,)),
        dma((PER_LAYER,)),
        dma((8,)),
        dma((4,)),
    ]
    if with_links:
        specs = [in_hbm] * 6 + [in_vmem, in_smem] + [in_vmem] * 7
        scratch += [
            pltpu.VMEM((PER_LAYER, HALF, LANES), low),
            pltpu.VMEM((8, LANES), wide_type),
            pltpu.VMEM((3, 8, LANES), wide_type),
            pltpu.VMEM((3, 8, LANES), wide_type),
            pltpu.VMEM((GROUPS, 32, 8, 128), wide_type),
            pltpu.VMEM((8, LANES), wide_type),
            pltpu.VMEM((8, LANES), wide_type),
            dma((PER_LAYER,)),
            dma((PER_LAYER,)),
            dma((PER_LAYER,)),
            dma((PER_LAYER,)),
            dma((17,)),
            dma((17, ITEMS)),
            dma((2,)),
            dma((4,)),
            dma((4,)),
            dma((7,)),
            dma((7,)),
            dma((GROUPS,)),
            dma((GROUPS,)),
        ]
        params = pltpu.CompilerParams(collective_id=0, has_side_effects=True, vmem_limit_bytes=VMEM_LIMIT)
    else:
        specs = [in_hbm] * 3 + [in_vmem, in_smem, in_hbm]
        params = pltpu.CompilerParams(vmem_limit_bytes=VMEM_LIMIT)
    results = pl.pallas_call(
        partial(layers_kernel, with_links),
        out_shape=tuple(outs),
        in_specs=specs,
        out_specs=tuple(out_specs),
        scratch_shapes=scratch,
        compiler_params=params,
    )(*weights, tokens, cotangent, segments, lengths, *vectors)
    return results[1:4] if with_links else results[:3]


def gather(w_qkv, w_out, w_in, w_ffn_out):
    matrices = [lax.all_gather(w[0], "dp", axis=0, tiled=True) for w in (w_qkv, w_out, w_in, w_ffn_out)]
    qkv, attn, hidden, final = matrices
    blocks = [qkv[:, b * LANES : (b + 1) * LANES] for b in range(3)] + [attn]
    blocks += [hidden[:, b * LANES : (b + 1) * LANES] for b in range(4)]
    final = final.reshape(16, 4, BLOCK, LANES).transpose(1, 0, 2, 3).reshape(4, 1024, LANES)
    own = jnp.concatenate([jnp.stack(blocks), final])
    return lax.all_gather(own, "section", axis=0, tiled=True).reshape(24, 4, 2, 2, BLOCK, LANES)


def on_device(
    tokens,
    segment_ids,
    row_lengths,
    w_qkv,
    w_out,
    w_in,
    w_ffn_out,
    bias_q,
    bias_v,
    bias_out,
    bias_in,
    bias_ffn_out,
    ln_gain,
    ln_shift,
    out_cotangent,
):
    weights = (w_qkv, w_out, w_in, w_ffn_out)
    vectors = (bias_q, bias_v, bias_out, bias_in, bias_ffn_out, ln_gain, ln_shift)
    data = (tokens, out_cotangent, segment_ids, row_lengths.T)
    if w_qkv.shape[1] == BLOCK:
        tops, grads, sums = both_layers(weights, *data, vectors)
        sums = sums[0]
    else:
        sec = lax.axis_index("section")
        wide_in, gains, shifts = bias_in.reshape(4, LANES), ln_gain[0], ln_shift[0]
        vec = jnp.concatenate(
            [bias_q, bias_v, bias_out, wide_in, bias_ffn_out, gains, shifts, jnp.zeros((4, LANES))]
        )
        vec = lax.all_gather(vec, "section", axis=0)
        tops, grads, sums = both_layers((gather(*weights),), *data, (vec,))

        def swap(array):
            return lax.ppermute(array, "section", [(0, 1), (1, 0)])

        def placed(both):
            got = swap(jnp.where(sec == 0, both[1], both[0]))
            return jnp.where(sec == 0, jnp.stack([both[0], got]), jnp.stack([got, both[1]]))

        tops, grads = placed(tops), placed(grads)
        sums = jnp.where(sec == 0, sums[0], sums[1]) + swap(jnp.where(sec == 0, sums[1], sums[0]))
        sums = lax.psum(sums, "dp")
    totals = (sums[0:1], sums[1:2], sums[2:3], sums[3:7].reshape(1, 4 * LANES), sums[7:8])
    return (tops[None, :, None], grads[None, :, None]) + totals


def solution(mesh):
    placed = (
        P(None, "dp", None, None),
        P(None, "dp", None),
        P(None, "dp"),
        P("section", "dp", None),
        P("section", "dp", None),
        P("section", "dp", None),
        P("section", "dp", None),
        P("section", None),
        P("section", None),
        P("section", None),
        P("section", None),
        P("section", None),
        P("section", None, None),
        P("section", None, None),
        P(None, "dp", None, None),
    )
    return jax.shard_map(
        on_device,
        mesh=mesh,
        in_specs=placed,
        out_specs=(
            P("section", None, "dp", None, None),
            P("section", None, "dp", None, None),
            P("section", None),
            P("section", None),
            P("section", None),
            P("section", None),
            P("section", None),
        ),
        check_vma=False,
    )
```

```python
from functools import partial
import math

import jax
import jax.numpy as jnp
from jax import lax
from jax.experimental import pallas as pl
from jax.experimental.pallas import tpu as pltpu
from jax.sharding import PartitionSpec as P

HEAD_DIM = 64
SEQ = 512
GROUPS = 4
epsilon = 1e-06
VMEM_LIMIT = 58 * 2**20
MESH = pl.DeviceIdType.MESH
ITEMS = 24
PER_LAYER = ITEMS // 2
LANES = 1024
BLOCK = 64
HALF = BLOCK // 2
CUT = 384
STAGES = (1, 2, 3, 4, 6)
LOAD = 7
FRONT = 6
SETTLE = 3
TILE = 256


def link_plan(wq, wo, wi, wf, full, vec, stage, in_sem, place_sem, cross_send, cross_recv, send_sem, recv_sem, vec_sem):
    sec = lax.axis_index("section")
    chip = lax.axis_index("dp")
    per_layer, items = PER_LAYER, ITEMS
    z = chip // 4
    y = (chip // 2) % 2
    x = chip % 2
    dev_x = (sec, z * 4 + y * 2 + 1 - x)
    dev_y = (sec, z * 4 + (1 - y) * 2 + x)
    dev_xy = (sec, z * 4 + (1 - y) * 2 + 1 - x)
    dev_up = (sec, jnp.minimum(z + 1, 3) * 4 + y * 2 + x)
    dev_down = (sec, jnp.maximum(z - 1, 0) * 4 + y * 2 + x)
    dev_core = (1 - sec, chip)
    in_plane = (dev_x, dev_y, dev_xy)
    along_z = tuple((sec, ((z + k) % 4) * 4 + y * 2 + x) for k in (1, 2, 3))

    def own_block(b, row):
        if b < 3:
            return wq.at[0, pl.ds(row, HALF), b * LANES : (b + 1) * LANES]
        if b == 3:
            return wo.at[0, pl.ds(row, HALF), :]
        if b < 8:
            return wi.at[0, pl.ds(row, HALF), (b - 4) * LANES : (b - 3) * LANES]
        pair, columns = (b - 8) // 2, slice((b % 2) * 512, (b % 2) * 512 + 512)
        return [wf.at[0, pl.ds((2 * pair + g) * BLOCK + row, HALF), columns] for g in range(2)]

    mine = pl.multiple_of(sec * HALF, HALF)
    other = pl.multiple_of((1 - sec) * HALF, HALF)

    def to_stage(b):
        return pltpu.make_async_copy(stage.at[b], stage.at[b], in_sem.at[b])

    def stage_start(b):
        block = own_block(b, mine)
        if b < 8:
            pltpu.make_async_copy(block, stage.at[b], in_sem.at[b]).start()
        else:
            for g in range(2):
                pltpu.make_async_copy(block[g], stage.at[b, :, g * 512 : (g + 1) * 512], in_sem.at[b]).start()

    def to_place(b):
        return pltpu.make_async_copy(
            stage.at[b], full.at[sec * per_layer + b, z, y, x, pl.ds(mine, HALF), :], place_sem.at[b]
        )

    def cross_copy(b, source, columns):
        return pltpu.make_async_remote_copy(
            src_ref=source,
            dst_ref=full.at[sec * per_layer + b, z, y, x, pl.ds(other, HALF), columns],
            send_sem=cross_send.at[b],
            recv_sem=cross_recv.at[b],
            device_id=dev_core,
            device_id_type=MESH,
        )

    def cross_start(b):
        block = own_block(b, other)
        if b < 8:
            cross_copy(b, block, slice(None)).start()
        else:
            for g in range(2):
                cross_copy(b, block[g], slice(g * 512, (g + 1) * 512)).start()

    def cross_sent(b):
        cross_copy(b, stage.at[b], slice(None)).wait_send()

    def give_vec(where):
        return pltpu.make_async_remote_copy(
            src_ref=where,
            dst_ref=where,
            send_sem=vec_sem.at[0],
            recv_sem=vec_sem.at[1],
            device_id=dev_core,
            device_id_type=MESH,
        )

    def begin():
        for b in range(per_layer):
            stage_start(b)
        barrier = pltpu.get_barrier_semaphore()
        for k in range(1, 32):
            device = ((sec + k // 16) % 2, (chip + k) % 16)
            pl.semaphore_signal(barrier, inc=1, device_id=device, device_id_type=MESH)
        pl.semaphore_wait(barrier, 31)
        for b in range(per_layer):
            cross_start(b)
        give_vec(vec.at[sec]).start()
        for b in range(per_layer):
            to_stage(b).wait()
            to_place(b).start()

    def vec_here():
        give_vec(vec.at[sec]).wait_send()
        give_vec(vec.at[1 - sec]).wait_recv()

    def copy(ref, kind, item, device):
        return pltpu.make_async_remote_copy(
            src_ref=ref,
            dst_ref=ref,
            send_sem=send_sem.at[kind],
            recv_sem=recv_sem.at[kind, item],
            device_id=device,
            device_id_type=MESH,
        )

    def views(core):
        rows = slice(core * HALF, (core + 1) * HALF)
        first, last = slice(0, CUT), slice(CUT, LANES)
        if core == 0:
            pair = lambda i, at: full.at[i, at, :, x, rows, last]
            eight_first = lambda i: full.at[i, :, y, :, rows, first]
            eight_last = lambda i: full.at[i, :, :, x, rows, last]
            towards = (dev_x, dev_y)
        else:
            pair = lambda i, at: full.at[i, at, y, :, rows, last]
            eight_first = lambda i: full.at[i, :, :, x, rows, first]
            eight_last = lambda i: full.at[i, :, y, :, rows, last]
            towards = (dev_y, dev_x)
        return (
            towards,
            lambda i, at: full.at[i, at, y, x, rows, first],
            lambda i: full.at[i, :, y, x, rows, first],
            eight_first,
            lambda i, at: full.at[i, at, y, x, rows, last],
            pair,
            eight_last,
            lambda i: full.at[i, :, :, :, rows, :],
        )

    def z_send(base, block, hop, item, at):
        if at < 3 and at - (hop - 1) >= 0:
            copy(block(item, at - (hop - 1)), base + hop - 1, item, dev_up).start()
        if at > 0 and at + (hop - 1) <= 3:
            copy(block(item, at + (hop - 1)), base + 2 + hop, item, dev_down).start()

    def z_recv(base, block, hop, item, at):
        if at - hop >= 0:
            copy(block(item, at - hop), base + hop - 1, item, dev_up).wait_recv()
        if at + hop <= 3:
            copy(block(item, at + hop), base + 2 + hop, item, dev_down).wait_recv()

    def step_at(t, at, core):
        (dev_u, dev_v), own_a, col_a, eight_a, own_d, pair_d, eight_d, whole = views(core)
        turns = [t - offset for offset in STAGES]

        def live(item):
            return (item >= 0) & (item < items)

        def first_move(item):
            @pl.when(live(item))
            def _():
                layer, b = item // per_layer, item % per_layer

                @pl.when(layer == core)
                def _():
                    pltpu.make_async_copy(
                        stage.at[b], full.at[item, z, y, x, pl.ds(core * HALF, HALF), :], place_sem.at[b]
                    ).wait()

                @pl.when(layer != core)
                def _():
                    mine_there = full.at[item, z, y, x, pl.ds(core * HALF, HALF), :]
                    pltpu.make_async_remote_copy(
                        src_ref=mine_there,
                        dst_ref=mine_there,
                        send_sem=cross_send.at[b],
                        recv_sem=cross_recv.at[b],
                        device_id=dev_core,
                        device_id_type=MESH,
                    ).wait_recv()

                copy(own_d(item, at), 8, item, dev_v).start()

        for lead in range(FRONT):
            first_move(t * FRONT + lead)

        @pl.when(live(t))
        def _():
            z_send(0, own_a, 1, t, at)

        item1 = turns[0]

        @pl.when(live(item1))
        def _():
            z_recv(0, own_a, 1, item1, at)
            z_send(0, own_a, 2, item1, at)
            copy(own_d(item1, at), 8, item1, dev_v).wait_recv()
            z_send(9, pair_d, 1, item1, at)

        item2 = turns[1]

        @pl.when(live(item2))
        def _():
            z_recv(0, own_a, 2, item2, at)
            z_send(0, own_a, 3, item2, at)
            z_recv(9, pair_d, 1, item2, at)
            z_send(9, pair_d, 2, item2, at)

        item3 = turns[2]

        @pl.when(live(item3))
        def _():
            z_recv(0, own_a, 3, item3, at)
            copy(col_a(item3), 6, item3, dev_u).start()
            z_recv(9, pair_d, 2, item3, at)
            z_send(9, pair_d, 3, item3, at)

        item4 = turns[3]

        @pl.when(live(item4))
        def _():
            copy(col_a(item4), 6, item4, dev_u).wait_recv()
            copy(eight_a(item4), 7, item4, dev_v).start()
            z_recv(9, pair_d, 3, item4, at)
            copy(eight_d(item4), 15, item4, dev_u).start()

        item5 = turns[4]

        @pl.when(live(item5))
        def _():
            copy(eight_a(item5), 7, item5, dev_v).wait_recv()
            copy(eight_d(item5), 15, item5, dev_u).wait_recv()
            copy(whole(item5), 16, item5, dev_core).start()

    def step(t):
        for at in range(4):
            for core in range(2):

                @pl.when((z == at) & (sec == core))
                def _():
                    step_at(t, at, core)

    def arrived(item):
        for core in range(2):

            @pl.when(sec == core)
            def _():
                copy(views(1 - core)[-1](item), 16, item, dev_core).wait_recv()

    def end():
        for b in range(per_layer):
            cross_sent(b)
        for core in range(2):

            @pl.when(sec == core)
            def _():
                _, own_a, col_a, eight_a, own_d, pair_d, eight_d, whole = views(core)
                every = slice(None)

                def sent(ref, kind):
                    copy(ref, kind, 0, dev_core).wait_send()

                sent(whole(every), 16)
                sent(col_a(every), 6)
                sent(eight_a(every), 7)
                sent(eight_d(every), 15)
                sent(own_d(every, 0), 8)
                for hop in (1, 2, 3):
                    for base, block in ((0, own_a), (9, pair_d)):

                        @pl.when((z < 3) & (z - (hop - 1) >= 0))
                        def _():
                            sent(block(every, 0), base + hop - 1)

                        @pl.when((z > 0) & (z + (hop - 1) <= 3))
                        def _():
                            sent(block(every, 0), base + 2 + hop)

    return begin, vec_here, step, arrived, end, dev_core, in_plane, along_z


def wide(ref, columns):
    block = ref[:, :, :, :, columns]
    return block.reshape(-1, block.shape[-1])


def dot_nt(left, right):
    return lax.dot_general(left, right, (((1,), (1,)), ((), ())), preferred_element_type=jnp.float32)


def dot_nn(left, right):
    return jnp.dot(left, right, preferred_element_type=jnp.float32)


def pair_bias(codes):
    down = jnp.broadcast_to(codes, (128, codes.shape[1])).T[:, :1]
    return jnp.where(down == codes, 0.0, -1000000000.0)


def lane_half(pair, half):
    lanes = lax.broadcasted_iota(jnp.int32, pair.shape, 1)
    return jnp.where((lanes < HEAD_DIM) == (half == 0), pair, jnp.zeros_like(pair))


def layers_kernel(with_links, *refs):
    if with_links:
        wq, wo, wi, wf, *refs = refs
    else:
        full, *refs = refs
    tokens, cotangent, segments, lengths, *refs = refs
    if with_links:
        parts, refs = refs[:7], refs[7:]
        full, *refs = refs
    else:
        given_vec, *refs = refs
    (y_out, grad_out, sums, prob_save, qkv_save, ctx_save, slope_save, norm_save, inv_save, *refs) = refs
    (x, vec, m_qkv, m_attn, m_hidden, m_final, qkv, ctx, hid, act, slope, acc, bias, probs, norms, invs, *refs) = refs
    (grad, layer_sums, head_sums, in_sem, load_sem, p_sem, save_sem, m_sem, sem, out_sem, *refs) = refs
    sec = lax.axis_index("section")
    if with_links:
        (stage, got_core, got_plane, got_z, got_late, part_core, part_plane, *link_sems) = refs
        *link_sems, ex_send, ex_recv, sum_send, sum_recv, late_sent, late_got = link_sems

    def start(copies):
        for copy in copies:
            copy.start()

    def wait(copies):
        for copy in copies:
            copy.wait()

    take_x = pltpu.make_async_copy(tokens.at[sec, 0], x, in_sem.at[0])
    take_grad = pltpu.make_async_copy(cotangent.at[sec, 0], grad, in_sem.at[1])
    take_x.start()
    take_grad.start()
    head_sums[...] = jnp.zeros_like(head_sums)
    if with_links:
        bias_q, bias_v, bias_out, bias_in, bias_ffn_out, ln_gain, ln_shift = parts
        for k, ref in enumerate((bias_q, bias_v, bias_out)):
            vec[sec, k : k + 1, :] = ref[...]
        for k in range(4):
            vec[sec, 3 + k : 4 + k, :] = bias_in[:, k * LANES : (k + 1) * LANES]
        vec[sec, 7:8, :] = bias_ffn_out[...]
        vec[sec, 8:10, :] = ln_gain[0]
        vec[sec, 10:12, :] = ln_shift[0]
        vec[sec, 12:16, :] = jnp.zeros((4, LANES), jnp.float32)
        begin_links, vec_here, step_links, arrived, end_links, dev_core, in_plane, along_z = link_plan(
            wq, wo, wi, wf, full, vec, stage, *link_sems
        )
        begin_links()
    else:
        take_vec = pltpu.make_async_copy(given_vec, vec, in_sem.at[2])
        take_vec.start()

    def settle():
        valid = lax.broadcasted_iota(jnp.int32, (1, SEQ), 1) < lengths[0, sec]
        bias[...] = pair_bias(segments[sec] * 2 + valid.astype(jnp.int32))
        take_x.wait()
        if with_links:
            vec_here()
        else:
            take_vec.wait()

    def row(layer, index):
        return vec[layer, index : index + 1, :]

    def hand_over(which, source, out, layer):
        local = pltpu.make_async_copy(source, out.at[sec], out_sem.at[which])
        if with_links:
            far = pltpu.make_async_remote_copy(
                src_ref=source,
                dst_ref=out.at[sec],
                send_sem=ex_send.at[which],
                recv_sem=ex_recv.at[which],
                device_id=dev_core,
                device_id_type=MESH,
            )
            return local, far
        return (pltpu.make_async_copy(source, out.at[layer], out_sem.at[which]),)

    def hand_start(which, source, out, layer):
        copies = hand_over(which, source, out, layer)
        if with_links:

            @pl.when(layer == sec)
            def _():
                copies[0].start()

            @pl.when(layer != sec)
            def _():
                copies[1].start()

        else:
            copies[0].start()

    def hand_wait(which, source, out, layer):
        copies = hand_over(which, source, out, layer)
        if with_links:

            @pl.when(layer == sec)
            def _():
                copies[0].wait()

            @pl.when(layer != sec)
            def _():
                copies[1].wait_send()

        else:
            copies[0].wait()

    def hand_arrived(which, source, out):
        pltpu.make_async_remote_copy(
            src_ref=source,
            dst_ref=out.at[1 - sec],
            send_sem=ex_send.at[which],
            recv_sem=ex_recv.at[which],
            device_id=dev_core,
            device_id_type=MESH,
        ).wait_recv()

    def load(item):
        b = item % PER_LAYER

        def into(b):
            if b < 3:
                return m_qkv.at[:, :, :, :, b * LANES : (b + 1) * LANES]
            if b == 3:
                return m_attn
            if b < 8:
                return m_hidden.at[:, :, :, :, (b - 4) * LANES : (b - 3) * LANES]
            return None

        for k in range(PER_LAYER):

            @pl.when(b == k)
            def _():
                if k < 8:
                    pltpu.make_async_copy(full.at[item], into(k), load_sem.at[k]).start()
                else:
                    for g in range(2):
                        final_part(item, k, g, load_sem.at[k]).start()

    def final_part(item, b, g, semaphore):
        columns = slice((b % 2) * 512, (b % 2) * 512 + 512)
        return pltpu.make_async_copy(
            full.at[item, :, :, :, :, g * 512 : (g + 1) * 512],
            m_final.at[(b - 8) // 2, :, :, :, g * BLOCK : (g + 1) * BLOCK, columns],
            semaphore,
        )

    def loaded(b):
        pltpu.make_async_copy(full.at[0], m_attn, load_sem.at[b]).wait()

    def project(layer, b):
        scale = jnp.where(b == 0, 0.125, 1.0)
        shift = jnp.where(b == 0, row(layer, 0), jnp.where(b == 2, row(layer, 1), 0.0))
        at = pl.multiple_of(b * LANES, LANES)
        for n in range(0, LANES, TILE):
            columns = pl.ds(at + n, TILE)
            out = dot_nn(x[...], wide(m_qkv, columns)) + shift[:, n : n + TILE]
            qkv[:, columns] = (out.astype(jnp.bfloat16).astype(jnp.float32) * scale).astype(jnp.bfloat16)

    def save_p(layer, p):
        group, k = p // 2, p % 2
        return pltpu.make_async_copy(probs.at[group % 2, k], prob_save.at[layer, group, k], p_sem.at[p % 4])

    def attend(layer, first, last):
        def one(p, _):
            @pl.when(p >= 4)
            def _():
                save_p(layer, p - 4).wait()

            at = pl.multiple_of(p * 128, 128)
            q, k, v = (qkv[:, pl.ds(part * LANES + at, 128)] for part in range(3))
            total = None
            for half in range(2):
                scores = dot_nt(lane_half(q, half), k) + bias[...]
                exps = jnp.exp(scores - jnp.max(scores, -1, keepdims=True))
                share = (exps / jnp.sum(exps, -1, keepdims=True)).astype(jnp.bfloat16)
                probs[(p // 2) % 2, p % 2, half] = share
                out = dot_nn(share, lane_half(v, half))
                total = out if total is None else total + out
            ctx[:, pl.ds(at, 128)] = total.astype(jnp.bfloat16)
            save_p(layer, p).start()
            return 0

        lax.fori_loop(first, last, one, 0)

    def save(which):
        pairs = (
            (qkv, qkv_save),
            (ctx, ctx_save),
            (slope, slope_save),
            (norms.at[0], norm_save.at[0]),
            (invs.at[0], inv_save.at[0]),
            (norms.at[1], norm_save.at[1]),
            (invs.at[1], inv_save.at[1]),
        )
        return pltpu.make_async_copy(*pairs[which], save_sem.at[which])

    def normalize(layer, which, put):
        for r in range(0, SEQ, 128):
            rows = slice(r, r + 128)
            residual = acc[rows, :]
            centered = residual - jnp.mean(residual, -1, keepdims=True)
            inverse = lax.rsqrt(jnp.mean(centered * centered, -1, keepdims=True) + epsilon)
            normed = centered * inverse
            norms[which, rows, :] = normed.astype(jnp.bfloat16)
            invs[which, rows, :] = jnp.broadcast_to(inverse, (128, 128))
            put[rows, :] = (normed * row(layer, 8 + which) + row(layer, 10 + which)).astype(jnp.bfloat16)

    def attn_out(layer):
        for n in range(0, LANES, TILE):
            columns = slice(n, n + TILE)
            acc[:, columns] = x[:, columns].astype(jnp.float32) + (
                dot_nn(ctx[...], wide(m_attn, columns)) + row(layer, 2)[:, columns]
            )
        normalize(layer, 0, hid)

    def ffn_in(layer, j):
        shift = vec[layer, pl.ds(3 + j, 1), :]
        at = pl.multiple_of(j * LANES, LANES)
        for n in range(0, LANES, TILE):
            pre = dot_nn(hid[...], wide(m_hidden, pl.ds(at + n, TILE))) + shift[:, n : n + TILE]
            cdf = 0.5 * (1.0 + lax.erf(pre * math.sqrt(0.5)))
            pdf = jnp.exp(pre * pre * -0.5) * (1.0 / math.sqrt(2.0 * math.pi))
            value = (pre * cdf).astype(jnp.bfloat16)
            grade = (cdf + pre * pdf).astype(jnp.bfloat16)
            to = pl.ds(pl.multiple_of(j * 512 + n // 2, 128), 128)
            for half in range(2):
                act[half, :, to] = value[:, half * 128 : (half + 1) * 128]
                slope[half, :, to] = grade[:, half * 128 : (half + 1) * 128]

    def ffn_out(layer, half, part):
        for n in range(part * 512, part * 512 + 512, TILE):
            columns = slice(n, n + TILE)
            out = dot_nn(act[half], wide(m_final.at[half], columns))
            if half == 0:
                acc[:, columns] = hid[:, columns].astype(jnp.float32) + (out + row(layer, 7)[:, columns])
            else:
                acc[:, columns] += out

    def compute(c):
        layer, b = c // PER_LAYER, c % PER_LAYER

        def lower(then):
            pl.when(layer == 0)(then)

        @pl.when(b <= 2)
        def _():
            loaded(b)

            @pl.when((b == 0) & (layer == 1))
            def _():
                wait([save(5), save(6)])

            project(layer, b)

        @pl.when(b == 2)
        def _():
            lower(lambda: start([save(0)]))
            attend(layer, 0, 2)

        @pl.when(b == 3)
        def _():
            loaded(3)
            attend(layer, 2, 5)

        @pl.when(b == 4)
        def _():
            loaded(4)
            attend(layer, 5, 8)

        @pl.when(b == 5)
        def _():
            lower(lambda: start([save(1)]))
            loaded(5)
            attn_out(layer)
            lower(lambda: start([save(3), save(4)]))

        @pl.when((b >= 5) & (b <= 8))
        def _():
            ffn_in(layer, b - 5)

        @pl.when(b == 6)
        def _():
            loaded(6)
            wait([save_p(layer, p) for p in range(4, 8)])
            lower(lambda: wait([save(0), save(1)]))

        @pl.when(b == 7)
        def _():
            loaded(7)

        @pl.when(b == 8)
        def _():
            lower(lambda: start([save(2)]))
            loaded(8)

        @pl.when(b == 9)
        def _():
            loaded(9)

            @pl.when(layer == 1)
            def _():
                hand_wait(0, x, y_out, 0)

            ffn_out(layer, 0, 0)
            ffn_out(layer, 0, 1)
            lower(lambda: wait([save(3), save(4)]))

        @pl.when(b == 10)
        def _():
            loaded(10)
            ffn_out(layer, 1, 0)
            lower(lambda: wait([save(2)]))

        @pl.when(b == 11)
        def _():
            loaded(11)
            ffn_out(layer, 1, 1)
            normalize(layer, 1, x)
            lower(lambda: start([save(5), save(6)]))
            hand_start(layer, x, y_out, layer)

    def step(t, _):
        if with_links:
            step_links(t)

        @pl.when(t == SETTLE)
        def _():
            settle()

        first = t - LOAD

        @pl.when((first >= 0) & (first < ITEMS))
        def _():
            if with_links:
                arrived(first)
            load(first)

        second = t - LOAD - 1

        @pl.when((second >= 0) & (second < ITEMS))
        def _():
            compute(second)

        return 0

    lax.fori_loop(0, ITEMS + LOAD + 1, step, 0)
    def fetch_final(half):
        return [
            final_part(8 + 2 * half + k, 8 + 2 * half + k, g, m_sem.at[(0, 12)[half] + 2 * k + g])
            for k in range(2)
            for g in range(2)
        ]

    def fetch_hidden():
        return [
            pltpu.make_async_copy(
                full.at[4 + j], m_hidden.at[:, :, :, :, j * LANES : (j + 1) * LANES], m_sem.at[4 + j]
            )
            for j in range(4)
        ]

    def fetch_attn():
        return [pltpu.make_async_copy(full.at[3], m_attn, m_sem.at[8])]

    def fetch_qkv():
        return [
            pltpu.make_async_copy(full.at[j], m_qkv.at[:, :, :, :, j * LANES : (j + 1) * LANES], m_sem.at[9 + j])
            for j in range(3)
        ]

    def fetch_norm(which):
        return [
            pltpu.make_async_copy(norm_save.at[which], norms.at[which], sem.at[2 * which]),
            pltpu.make_async_copy(inv_save.at[which], invs.at[which], sem.at[2 * which + 1]),
        ]

    def fetch_slope(half):
        return [pltpu.make_async_copy(slope_save.at[half], slope.at[half], sem.at[4 + half])]

    def fetch_heads():
        return [
            pltpu.make_async_copy(qkv_save, qkv, sem.at[6]),
            pltpu.make_async_copy(ctx_save, ctx, sem.at[7]),
        ]

    def fetch_probs(layer, group):
        return [pltpu.make_async_copy(prob_save.at[layer, group], probs.at[group % 2], p_sem.at[group % 2])]

    start(fetch_probs(1, 0) + fetch_probs(1, 1))
    take_grad.wait()

    def column_sum(values):
        return jnp.sum(values.astype(jnp.float32), 0, keepdims=True)

    def norm_back(layer, which, upstream_of):
        gain = vec[layer, 8 + which : 9 + which, :]
        total = jnp.zeros((1, LANES), jnp.float32)
        for r in range(0, SEQ, 128):
            rows = slice(r, r + 128)
            upstream = upstream_of(rows) * gain
            normed = norms[which, rows, :].astype(jnp.float32)
            back = invs[which, rows, 0:1] * (
                upstream
                - jnp.mean(upstream, -1, keepdims=True)
                - normed * jnp.mean(upstream * normed, -1, keepdims=True)
            )
            acc[rows, :] = back
            low = back.astype(jnp.bfloat16)
            hid[rows, :] = low
            total = total + column_sum(low)
        return total

    def sum_copy(source, target, k, device):
        return pltpu.make_async_remote_copy(
            src_ref=source,
            dst_ref=target,
            send_sem=sum_send.at[k],
            recv_sem=sum_recv.at[k],
            device_id=device,
            device_id_type=MESH,
        )

    def spread_heads(target, where, group, heads):
        for row in range(2):
            for k in range(2):
                at = (2 * group + k) * 128
                target[where, row : row + 1, at : at + 128] = heads[2 * row + k : 2 * row + k + 1, :]

    def core_sums():
        return [sum_copy(layer_sums.at[1 - sec], got_core, 0, dev_core)]

    def plane_sums():
        return [sum_copy(part_core, got_plane.at[k], 1 + k, device) for k, device in enumerate(in_plane)]

    def z_sums():
        return [sum_copy(part_plane, got_z.at[k], 4 + k, device) for k, device in enumerate(along_z)]

    def begin_early():
        layer_sums[0, 0:2, :] = jnp.zeros((2, LANES), jnp.float32)
        for group in range(GROUPS):
            spread_heads(layer_sums, 1, group, head_sums[1, group])
        start(core_sums())

    def early_sums(k):
        @pl.when(k == 0)
        def _():
            wait(core_sums())
            part_core[...] = layer_sums[sec] + got_core[...]
            start(plane_sums())

        @pl.when(k == 2)
        def _():
            wait(plane_sums())
            part_plane[...] = part_core[...] + (got_plane[0] + got_plane[1]) + got_plane[2]
            start(z_sums())

    def end_early():
        wait(z_sums())
        sums[0] = part_plane[...] + (got_z[0] + got_z[1]) + got_z[2]

    def late_send(group):
        own = 16 * sec + lax.axis_index("dp")
        got_late[group, own] = head_sums[0, group]

        def one(k, _):
            sum_late(group, own, (0, (lax.axis_index("dp") + k) % 16)).start()
            return 0

        lax.fori_loop(1, 16, one, 0)

        @pl.when(sec == 1)
        def _():
            sum_late(group, own, dev_core).start()

    def sum_late(group, slot, device):
        return pltpu.make_async_remote_copy(
            src_ref=head_sums.at[0, group],
            dst_ref=got_late.at[group, slot],
            send_sem=late_sent.at[group],
            recv_sem=late_got.at[group],
            device_id=device,
            device_id_type=MESH,
        )

    def end_late():
        def many(group, count):
            several = got_late.at[group, pl.ds(0, count)]
            return pltpu.make_async_remote_copy(
                src_ref=several,
                dst_ref=several,
                send_sem=late_sent.at[group],
                recv_sem=late_got.at[group],
                device_id=dev_core,
                device_id_type=MESH,
            )

        for group in range(GROUPS):
            for core in range(2):

                @pl.when(sec == core)
                def _():
                    many(group, 15 + core).wait_send()
                    if core == 0:
                        many(group, 31).wait_recv()
                        spread_heads(sums, 0, group, jnp.sum(got_late[group], 0))

    def one_layer(s, _):
        layer = 1 - s

        def prefetch(copies):
            @pl.when(s == 0)
            def _():
                start(copies)

        def fetched(copies):
            @pl.when(s == 1)
            def _():
                wait(copies)

        fetched(fetch_norm(1))
        layer_sums[layer, 7:8, :] = norm_back(layer, 1, lambda rows: grad[rows, :].astype(jnp.float32))
        prefetch(fetch_norm(1))
        for half in range(2):
            fetched(fetch_final(half) + fetch_slope(half))
            for n in range(0, 2048, TILE):
                chip = n // 128
                block = m_final[half, chip // 4, (chip // 2) % 2].reshape(TILE, LANES)
                back = dot_nt(hid[...], block) * slope[half, :, n : n + TILE].astype(jnp.float32)
                low = back.astype(jnp.bfloat16)
                total = column_sum(low)
                for k in range(2):
                    at = (chip + k) * 256 + half * 128
                    part = slice(k * 128, (k + 1) * 128)
                    act[at // 2048, :, at % 2048 : at % 2048 + 128] = low[:, part]
                    layer_sums[layer, 3 + at // LANES : 4 + at // LANES, at % LANES : at % LANES + 128] = total[:, part]
            prefetch(fetch_final(half) + fetch_slope(half))
        fetched(fetch_hidden())
        for n in range(0, LANES, TILE):
            block = m_hidden[n // TILE].reshape(TILE, 4 * LANES)
            acc[:, n : n + TILE] += dot_nt(act[0], block[:, : 2 * LANES]) + dot_nt(act[1], block[:, 2 * LANES :])
        prefetch(fetch_hidden())
        fetched(fetch_norm(0))
        layer_sums[layer, 2:3, :] = norm_back(
            layer, 0, lambda rows: acc[rows, :].astype(jnp.bfloat16).astype(jnp.float32)
        )
        prefetch(fetch_norm(0))

        @pl.when(s == 1)
        def _():
            hand_wait(3, grad, grad_out, 1)

        fetched(fetch_attn())
        for n in range(0, LANES, TILE):
            block = m_attn[n // TILE].reshape(TILE, LANES)
            grad[:, n : n + TILE] = dot_nt(hid[...], block).astype(jnp.bfloat16)
        prefetch(fetch_attn())
        fetched(fetch_heads())

        def one_group(group, _):
            wait(fetch_probs(layer, group))
            for k in range(2):
                one_pair(2 * group + k, group, k, probs.at[group % 2, k])

            @pl.when(group < GROUPS - 2)
            def _():
                start(fetch_probs(layer, group + 2))

            if with_links:

                @pl.when(s == 1)
                def _():
                    late_send(group)
                    early_sums(group)

            return 0

        def one_pair(p, group, k, shares):
            at = pl.multiple_of(p * 128, 128)
            q, keys, v = (qkv[:, pl.ds(part * LANES + at, 128)] for part in range(3))
            upper = grad[:, pl.ds(at, 128)]
            product = upper.astype(jnp.float32) * ctx[:, pl.ds(at, 128)].astype(jnp.float32)
            q_t, k_t, upper_t = q.T, keys.T, upper.T
            grad_q, grad_k, grad_v = [], [], []
            for half in range(2):
                weights = shares[half]
                delta = jnp.sum(lane_half(product, half), -1, keepdims=True)
                scores = dot_nt(lane_half(upper, half), v)
                low = (weights.astype(jnp.float32) * (scores - delta)).astype(jnp.bfloat16)
                here = slice(half * HEAD_DIM, (half + 1) * HEAD_DIM)
                grad_q.append(dot_nt(k_t[here], low) * 0.125)
                grad_k.append(dot_nn(q_t[here], low))
                grad_v.append(dot_nn(upper_t[here], weights))
            for part, rows in enumerate((grad_q, grad_k, grad_v)):
                back = jnp.concatenate(rows, 0).astype(jnp.bfloat16).T
                act[part // 2, :, pl.ds((part % 2) * LANES + at, 128)] = back
                if part != 1:
                    head_sums[layer, group, part + k : part + k + 1, :] = column_sum(back)

        if with_links:

            @pl.when(s == 1)
            def _():
                begin_early()

        lax.fori_loop(0, GROUPS, one_group, 0)
        prefetch(fetch_heads() + fetch_probs(0, 0) + fetch_probs(0, 1))
        fetched(fetch_qkv())

        def columns_of(n):
            block = m_qkv[n // TILE].reshape(TILE, 3 * LANES)
            columns = slice(n, n + TILE)
            total = dot_nt(act[0], block[:, : 2 * LANES]) + dot_nt(act[1, :, :LANES], block[:, 2 * LANES :])
            grad[:, columns] = (acc[:, columns] + total).astype(jnp.bfloat16)

        if with_links:

            @pl.when(s == 0)
            def _():
                for n in range(0, LANES, TILE):
                    columns_of(n)

            @pl.when(s == 1)
            def _():
                for n in range(0, LANES, TILE):
                    columns_of(n)
                    if n == TILE:
                        end_early()
                end_late()

        else:
            for n in range(0, LANES, TILE):
                columns_of(n)
        prefetch(fetch_qkv())
        hand_start(2 + layer, grad, grad_out, layer)
        return 0

    lax.fori_loop(0, 2, one_layer, 0)
    hand_wait(1, x, y_out, 1)
    hand_wait(2, grad, grad_out, 0)
    if with_links:
        hand_arrived(sec, x, y_out)
        hand_arrived(2 + sec, grad, grad_out)
        end_links()
    else:
        for layer in range(2):
            for group in range(GROUPS):
                spread_heads(layer_sums, layer, group, head_sums[layer, group])
        sums[...] = layer_sums[...]


def both_layers(weights, tokens, cotangent, segments, lengths, vectors):
    with_links = len(weights) == 4
    low, wide_type = jnp.bfloat16, jnp.float32
    in_hbm = pl.BlockSpec(memory_space=pltpu.HBM)
    in_vmem = pl.BlockSpec(memory_space=pltpu.VMEM)
    in_smem = pl.BlockSpec(memory_space=pltpu.SMEM)
    shape = jax.ShapeDtypeStruct
    sums = (1, 8, LANES) if with_links else (2, 8, LANES)
    outs = [shape((ITEMS, 4, 2, 2, BLOCK, LANES), low)] if with_links else []
    outs += [
        pltpu.VMEM((2, SEQ, LANES), low),
        pltpu.VMEM((2, SEQ, LANES), low),
        shape(sums, wide_type),
        shape((2, GROUPS, 2, 2, SEQ, SEQ), low),
        shape((SEQ, 3 * LANES), low),
        shape((SEQ, LANES), low),
        shape((2, SEQ, 2 * LANES), low),
        shape((2, SEQ, LANES), low),
        shape((2, SEQ, 128), wide_type),
    ]
    out_specs = [in_hbm] * len(outs)
    for k in range(3):
        out_specs[k + with_links] = in_vmem
    dma = pltpu.SemaphoreType.DMA
    scratch = [
        pltpu.VMEM((SEQ, LANES), low),
        pltpu.VMEM((2, 16, LANES), wide_type),
        pltpu.VMEM((4, 2, 2, BLOCK, 3 * LANES), low),
        pltpu.VMEM((4, 2, 2, BLOCK, LANES), low),
        pltpu.VMEM((4, 2, 2, BLOCK, 4 * LANES), low),
        pltpu.VMEM((2, 4, 2, 2, 2 * BLOCK, LANES), low),
        pltpu.VMEM((SEQ, 3 * LANES), low),
        pltpu.VMEM((SEQ, LANES), low),
        pltpu.VMEM((SEQ, LANES), low),
        pltpu.VMEM((2, SEQ, 2 * LANES), low),
        pltpu.VMEM((2, SEQ, 2 * LANES), low),
        pltpu.VMEM((SEQ, LANES), wide_type),
        pltpu.VMEM((SEQ, SEQ), wide_type),
        pltpu.VMEM((2, 2, 2, SEQ, SEQ), low),
        pltpu.VMEM((2, SEQ, LANES), low),
        pltpu.VMEM((2, SEQ, 128), wide_type),
        pltpu.VMEM((SEQ, LANES), low),
        pltpu.VMEM((2, 8, LANES), wide_type),
        pltpu.VMEM((2, GROUPS, 8, 128), wide_type),
        dma((3,)),
        dma((PER_LAYER,)),
        dma((4,)),
        dma((7,)),
        dma((16,)),
        dma((8,)),
        dma((4,)),
    ]
    if with_links:
        specs = [in_hbm] * 6 + [in_vmem, in_smem] + [in_vmem] * 7
        scratch += [
            pltpu.VMEM((PER_LAYER, HALF, LANES), low),
            pltpu.VMEM((8, LANES), wide_type),
            pltpu.VMEM((3, 8, LANES), wide_type),
            pltpu.VMEM((3, 8, LANES), wide_type),
            pltpu.VMEM((GROUPS, 32, 8, 128), wide_type),
            pltpu.VMEM((8, LANES), wide_type),
            pltpu.VMEM((8, LANES), wide_type),
            dma((PER_LAYER,)),
            dma((PER_LAYER,)),
            dma((PER_LAYER,)),
            dma((PER_LAYER,)),
            dma((17,)),
            dma((17, ITEMS)),
            dma((2,)),
            dma((4,)),
            dma((4,)),
            dma((7,)),
            dma((7,)),
            dma((GROUPS,)),
            dma((GROUPS,)),
        ]
        params = pltpu.CompilerParams(collective_id=0, has_side_effects=True, vmem_limit_bytes=VMEM_LIMIT)
    else:
        specs = [in_hbm] * 3 + [in_vmem, in_smem, in_hbm]
        params = pltpu.CompilerParams(vmem_limit_bytes=VMEM_LIMIT)
    results = pl.pallas_call(
        partial(layers_kernel, with_links),
        out_shape=tuple(outs),
        in_specs=specs,
        out_specs=tuple(out_specs),
        scratch_shapes=scratch,
        compiler_params=params,
    )(*weights, tokens, cotangent, segments, lengths, *vectors)
    return results[1:4] if with_links else results[:3]


def gather(w_qkv, w_out, w_in, w_ffn_out):
    matrices = [lax.all_gather(w[0], "dp", axis=0, tiled=True) for w in (w_qkv, w_out, w_in, w_ffn_out)]
    qkv, attn, hidden, final = matrices
    blocks = [qkv[:, b * LANES : (b + 1) * LANES] for b in range(3)] + [attn]
    blocks += [hidden[:, b * LANES : (b + 1) * LANES] for b in range(4)]
    final = final.reshape(16, 2, 2, BLOCK, 2, 512).transpose(1, 4, 0, 3, 2, 5).reshape(4, 1024, LANES)
    own = jnp.concatenate([jnp.stack(blocks), final])
    return lax.all_gather(own, "section", axis=0, tiled=True).reshape(24, 4, 2, 2, BLOCK, LANES)


def on_device(
    tokens,
    segment_ids,
    row_lengths,
    w_qkv,
    w_out,
    w_in,
    w_ffn_out,
    bias_q,
    bias_v,
    bias_out,
    bias_in,
    bias_ffn_out,
    ln_gain,
    ln_shift,
    out_cotangent,
):
    weights = (w_qkv, w_out, w_in, w_ffn_out)
    vectors = (bias_q, bias_v, bias_out, bias_in, bias_ffn_out, ln_gain, ln_shift)
    data = (tokens, out_cotangent, segment_ids, row_lengths.T)
    if w_qkv.shape[1] == BLOCK:
        tops, grads, sums = both_layers(weights, *data, vectors)
        sums = sums[0]
    else:
        sec = lax.axis_index("section")
        wide_in, gains, shifts = bias_in.reshape(4, LANES), ln_gain[0], ln_shift[0]
        vec = jnp.concatenate(
            [bias_q, bias_v, bias_out, wide_in, bias_ffn_out, gains, shifts, jnp.zeros((4, LANES))]
        )
        vec = lax.all_gather(vec, "section", axis=0)
        tops, grads, sums = both_layers((gather(*weights),), *data, (vec,))

        def swap(array):
            return lax.ppermute(array, "section", [(0, 1), (1, 0)])

        def placed(both):
            got = swap(jnp.where(sec == 0, both[1], both[0]))
            return jnp.where(sec == 0, jnp.stack([both[0], got]), jnp.stack([got, both[1]]))

        tops, grads = placed(tops), placed(grads)
        sums = jnp.where(sec == 0, sums[0], sums[1]) + swap(jnp.where(sec == 0, sums[1], sums[0]))
        sums = lax.psum(sums, "dp")
    totals = (sums[0:1], sums[1:2], sums[2:3], sums[3:7].reshape(1, 4 * LANES), sums[7:8])
    return (tops[None, :, None], grads[None, :, None]) + totals


def solution(mesh):
    placed = (
        P(None, "dp", None, None),
        P(None, "dp", None),
        P(None, "dp"),
        P("section", "dp", None),
        P("section", "dp", None),
        P("section", "dp", None),
        P("section", "dp", None),
        P("section", None),
        P("section", None),
        P("section", None),
        P("section", None),
        P("section", None),
        P("section", None, None),
        P("section", None, None),
        P(None, "dp", None, None),
    )
    return jax.shard_map(
        on_device,
        mesh=mesh,
        in_specs=placed,
        out_specs=(
            P("section", None, "dp", None, None),
            P("section", None, "dp", None, None),
            P("section", None),
            P("section", None),
            P("section", None),
            P("section", None),
            P("section", None),
        ),
        check_vma=False,
    )
```

```python
from functools import partial
import math

import jax
import jax.numpy as jnp
from jax import lax
from jax.experimental import pallas as pl
from jax.experimental.pallas import tpu as pltpu
from jax.sharding import PartitionSpec as P

HEAD_DIM = 64
SEQ = 512
GROUPS = 4
epsilon = 1e-06
VMEM_LIMIT = 58 * 2**20
MESH = pl.DeviceIdType.MESH
ITEMS = 24
PER_LAYER = ITEMS // 2
LANES = 1024
BLOCK = 64
HALF = BLOCK // 2
CUT = 384
STAGES = (1, 2, 3, 4, 6)
LOAD = 7
FRONT = 6
SETTLE = 3
TILE = 256


def link_plan(wq, wo, wi, wf, full, vec, stage, in_sem, place_sem, cross_send, cross_recv, send_sem, recv_sem, vec_sem):
    sec = lax.axis_index("section")
    chip = lax.axis_index("dp")
    per_layer, items = PER_LAYER, ITEMS
    z = chip // 4
    y = (chip // 2) % 2
    x = chip % 2
    dev_x = (sec, z * 4 + y * 2 + 1 - x)
    dev_y = (sec, z * 4 + (1 - y) * 2 + x)
    dev_xy = (sec, z * 4 + (1 - y) * 2 + 1 - x)
    dev_up = (sec, jnp.minimum(z + 1, 3) * 4 + y * 2 + x)
    dev_down = (sec, jnp.maximum(z - 1, 0) * 4 + y * 2 + x)
    dev_core = (1 - sec, chip)
    in_plane = (dev_x, dev_y, dev_xy)
    along_z = tuple((sec, ((z + k) % 4) * 4 + y * 2 + x) for k in (1, 2, 3))

    def own_block(b, row):
        if b < 3:
            return wq.at[0, pl.ds(row, HALF), b * LANES : (b + 1) * LANES]
        if b == 3:
            return wo.at[0, pl.ds(row, HALF), :]
        if b < 8:
            return wi.at[0, pl.ds(row, HALF), (b - 4) * LANES : (b - 3) * LANES]
        pair, columns = (b - 8) // 2, slice((b % 2) * 512, (b % 2) * 512 + 512)
        return [wf.at[0, pl.ds((2 * pair + g) * BLOCK + row, HALF), columns] for g in range(2)]

    mine = pl.multiple_of(sec * HALF, HALF)
    other = pl.multiple_of((1 - sec) * HALF, HALF)

    def to_stage(b):
        return pltpu.make_async_copy(stage.at[b], stage.at[b], in_sem.at[b])

    def stage_start(b):
        block = own_block(b, mine)
        if b < 8:
            pltpu.make_async_copy(block, stage.at[b], in_sem.at[b]).start()
        else:
            for g in range(2):
                pltpu.make_async_copy(block[g], stage.at[b, :, g * 512 : (g + 1) * 512], in_sem.at[b]).start()

    def to_place(b):
        return pltpu.make_async_copy(
            stage.at[b], full.at[sec * per_layer + b, z, y, x, pl.ds(mine, HALF), :], place_sem.at[b]
        )

    def cross_copy(b, source, columns):
        return pltpu.make_async_remote_copy(
            src_ref=source,
            dst_ref=full.at[sec * per_layer + b, z, y, x, pl.ds(other, HALF), columns],
            send_sem=cross_send.at[b],
            recv_sem=cross_recv.at[b],
            device_id=dev_core,
            device_id_type=MESH,
        )

    def cross_start(b):
        block = own_block(b, other)
        if b < 8:
            cross_copy(b, block, slice(None)).start()
        else:
            for g in range(2):
                cross_copy(b, block[g], slice(g * 512, (g + 1) * 512)).start()

    def cross_sent(b):
        cross_copy(b, stage.at[b], slice(None)).wait_send()

    def give_vec(where):
        return pltpu.make_async_remote_copy(
            src_ref=where,
            dst_ref=where,
            send_sem=vec_sem.at[0],
            recv_sem=vec_sem.at[1],
            device_id=dev_core,
            device_id_type=MESH,
        )

    def begin():
        for b in range(per_layer):
            stage_start(b)
        barrier = pltpu.get_barrier_semaphore()
        for k in range(1, 32):
            device = ((sec + k // 16) % 2, (chip + k) % 16)
            pl.semaphore_signal(barrier, inc=1, device_id=device, device_id_type=MESH)
        pl.semaphore_wait(barrier, 31)
        for b in range(per_layer):
            cross_start(b)
        give_vec(vec.at[sec]).start()
        for b in range(per_layer):
            to_stage(b).wait()
            to_place(b).start()

    def vec_here():
        give_vec(vec.at[sec]).wait_send()
        give_vec(vec.at[1 - sec]).wait_recv()

    def copy(ref, kind, item, device):
        return pltpu.make_async_remote_copy(
            src_ref=ref,
            dst_ref=ref,
            send_sem=send_sem.at[kind],
            recv_sem=recv_sem.at[kind, item],
            device_id=device,
            device_id_type=MESH,
        )

    def views(core):
        rows = slice(core * HALF, (core + 1) * HALF)
        first, last = slice(0, CUT), slice(CUT, LANES)
        if core == 0:
            pair = lambda i, at: full.at[i, at, :, x, rows, last]
            eight_first = lambda i: full.at[i, :, y, :, rows, first]
            eight_last = lambda i: full.at[i, :, :, x, rows, last]
            towards = (dev_x, dev_y)
        else:
            pair = lambda i, at: full.at[i, at, y, :, rows, last]
            eight_first = lambda i: full.at[i, :, :, x, rows, first]
            eight_last = lambda i: full.at[i, :, y, :, rows, last]
            towards = (dev_y, dev_x)
        return (
            towards,
            lambda i, at: full.at[i, at, y, x, rows, first],
            lambda i: full.at[i, :, y, x, rows, first],
            eight_first,
            lambda i, at: full.at[i, at, y, x, rows, last],
            pair,
            eight_last,
            lambda i: full.at[i, :, :, :, rows, :],
        )

    def z_send(base, block, hop, item, at):
        if at < 3 and at - (hop - 1) >= 0:
            copy(block(item, at - (hop - 1)), base + hop - 1, item, dev_up).start()
        if at > 0 and at + (hop - 1) <= 3:
            copy(block(item, at + (hop - 1)), base + 2 + hop, item, dev_down).start()

    def z_recv(base, block, hop, item, at):
        if at - hop >= 0:
            copy(block(item, at - hop), base + hop - 1, item, dev_up).wait_recv()
        if at + hop <= 3:
            copy(block(item, at + hop), base + 2 + hop, item, dev_down).wait_recv()

    def step_at(t, at, core):
        (dev_u, dev_v), own_a, col_a, eight_a, own_d, pair_d, eight_d, whole = views(core)
        turns = [t - offset for offset in STAGES]

        def live(item):
            return (item >= 0) & (item < items)

        def first_move(item):
            @pl.when(live(item))
            def _():
                layer, b = item // per_layer, item % per_layer

                @pl.when(layer == core)
                def _():
                    pltpu.make_async_copy(
                        stage.at[b], full.at[item, z, y, x, pl.ds(core * HALF, HALF), :], place_sem.at[b]
                    ).wait()

                @pl.when(layer != core)
                def _():
                    mine_there = full.at[item, z, y, x, pl.ds(core * HALF, HALF), :]
                    pltpu.make_async_remote_copy(
                        src_ref=mine_there,
                        dst_ref=mine_there,
                        send_sem=cross_send.at[b],
                        recv_sem=cross_recv.at[b],
                        device_id=dev_core,
                        device_id_type=MESH,
                    ).wait_recv()

                copy(own_d(item, at), 8, item, dev_v).start()

        for lead in range(FRONT):
            first_move(t * FRONT + lead)

        @pl.when(live(t))
        def _():
            z_send(0, own_a, 1, t, at)

        item1 = turns[0]

        @pl.when(live(item1))
        def _():
            z_recv(0, own_a, 1, item1, at)
            z_send(0, own_a, 2, item1, at)
            copy(own_d(item1, at), 8, item1, dev_v).wait_recv()
            z_send(9, pair_d, 1, item1, at)

        item2 = turns[1]

        @pl.when(live(item2))
        def _():
            z_recv(0, own_a, 2, item2, at)
            z_send(0, own_a, 3, item2, at)
            z_recv(9, pair_d, 1, item2, at)
            z_send(9, pair_d, 2, item2, at)

        item3 = turns[2]

        @pl.when(live(item3))
        def _():
            z_recv(0, own_a, 3, item3, at)
            copy(col_a(item3), 6, item3, dev_u).start()
            z_recv(9, pair_d, 2, item3, at)
            z_send(9, pair_d, 3, item3, at)

        item4 = turns[3]

        @pl.when(live(item4))
        def _():
            copy(col_a(item4), 6, item4, dev_u).wait_recv()
            copy(eight_a(item4), 7, item4, dev_v).start()
            z_recv(9, pair_d, 3, item4, at)
            copy(eight_d(item4), 15, item4, dev_u).start()

        item5 = turns[4]

        @pl.when(live(item5))
        def _():
            copy(eight_a(item5), 7, item5, dev_v).wait_recv()
            copy(eight_d(item5), 15, item5, dev_u).wait_recv()
            copy(whole(item5), 16, item5, dev_core).start()

    def step(t):
        for at in range(4):
            for core in range(2):

                @pl.when((z == at) & (sec == core))
                def _():
                    step_at(t, at, core)

    def arrived(item):
        for core in range(2):

            @pl.when(sec == core)
            def _():
                copy(views(1 - core)[-1](item), 16, item, dev_core).wait_recv()

    def end():
        for b in range(per_layer):
            cross_sent(b)
        for core in range(2):

            @pl.when(sec == core)
            def _():
                _, own_a, col_a, eight_a, own_d, pair_d, eight_d, whole = views(core)
                every = slice(None)

                def sent(ref, kind):
                    copy(ref, kind, 0, dev_core).wait_send()

                sent(whole(every), 16)
                sent(col_a(every), 6)
                sent(eight_a(every), 7)
                sent(eight_d(every), 15)
                sent(own_d(every, 0), 8)
                for hop in (1, 2, 3):
                    for base, block in ((0, own_a), (9, pair_d)):

                        @pl.when((z < 3) & (z - (hop - 1) >= 0))
                        def _():
                            sent(block(every, 0), base + hop - 1)

                        @pl.when((z > 0) & (z + (hop - 1) <= 3))
                        def _():
                            sent(block(every, 0), base + 2 + hop)

    return begin, vec_here, step, arrived, end, dev_core, in_plane, along_z


def wide(ref, columns):
    block = ref[:, :, :, :, columns]
    return block.reshape(-1, block.shape[-1])


def dot_nt(left, right):
    return lax.dot_general(left, right, (((1,), (1,)), ((), ())), preferred_element_type=jnp.float32)


def dot_nn(left, right):
    return jnp.dot(left, right, preferred_element_type=jnp.float32)


def pair_bias(codes):
    down = jnp.broadcast_to(codes, (128, codes.shape[1])).T[:, :1]
    return jnp.where(down == codes, 0.0, -1000000000.0)


def lane_half(pair, half):
    lanes = lax.broadcasted_iota(jnp.int32, pair.shape, 1)
    return jnp.where((lanes < HEAD_DIM) == (half == 0), pair, jnp.zeros_like(pair))


def layers_kernel(with_links, *refs):
    if with_links:
        wq, wo, wi, wf, *refs = refs
    else:
        full, *refs = refs
    tokens, cotangent, segments, lengths, *refs = refs
    if with_links:
        parts, refs = refs[:7], refs[7:]
        full, *refs = refs
    else:
        given_vec, *refs = refs
    (y_out, grad_out, sums, prob_save, qkv_save, ctx_save, slope_save, norm_save, inv_save, *refs) = refs
    (x, vec, m_qkv, m_attn, m_hidden, m_final, qkv, ctx, hid, act, slope, acc, bias, probs, norms, invs, *refs) = refs
    (grad, layer_sums, head_sums, in_sem, load_sem, p_sem, save_sem, m_sem, sem, out_sem, *refs) = refs
    sec = lax.axis_index("section")
    if with_links:
        (stage, got_core, got_plane, got_z, got_late, part_core, part_plane, *link_sems) = refs
        *link_sems, ex_send, ex_recv, sum_send, sum_recv, late_sent, late_got = link_sems

    def start(copies):
        for copy in copies:
            copy.start()

    def wait(copies):
        for copy in copies:
            copy.wait()

    take_x = pltpu.make_async_copy(tokens.at[sec, 0], x, in_sem.at[0])
    take_grad = pltpu.make_async_copy(cotangent.at[sec, 0], grad, in_sem.at[1])
    take_x.start()
    take_grad.start()
    head_sums[...] = jnp.zeros_like(head_sums)
    if with_links:
        bias_q, bias_v, bias_out, bias_in, bias_ffn_out, ln_gain, ln_shift = parts
        for k, ref in enumerate((bias_q, bias_v, bias_out)):
            vec[sec, k : k + 1, :] = ref[...]
        for k in range(4):
            vec[sec, 3 + k : 4 + k, :] = bias_in[:, k * LANES : (k + 1) * LANES]
        vec[sec, 7:8, :] = bias_ffn_out[...]
        vec[sec, 8:10, :] = ln_gain[0]
        vec[sec, 10:12, :] = ln_shift[0]
        vec[sec, 12:16, :] = jnp.zeros((4, LANES), jnp.float32)
        begin_links, vec_here, step_links, arrived, end_links, dev_core, in_plane, along_z = link_plan(
            wq, wo, wi, wf, full, vec, stage, *link_sems
        )
        begin_links()
    else:
        take_vec = pltpu.make_async_copy(given_vec, vec, in_sem.at[2])
        take_vec.start()

    def settle():
        valid = lax.broadcasted_iota(jnp.int32, (1, SEQ), 1) < lengths[0, sec]
        bias[...] = pair_bias(segments[sec] * 2 + valid.astype(jnp.int32))
        take_x.wait()
        if with_links:
            vec_here()
        else:
            take_vec.wait()

    def row(layer, index):
        return vec[layer, index : index + 1, :]

    def hand_over(which, source, out, layer):
        local = pltpu.make_async_copy(source, out.at[sec], out_sem.at[which])
        if with_links:
            far = pltpu.make_async_remote_copy(
                src_ref=source,
                dst_ref=out.at[sec],
                send_sem=ex_send.at[which],
                recv_sem=ex_recv.at[which],
                device_id=dev_core,
                device_id_type=MESH,
            )
            return local, far
        return (pltpu.make_async_copy(source, out.at[layer], out_sem.at[which]),)

    def hand_start(which, source, out, layer):
        copies = hand_over(which, source, out, layer)
        if with_links:

            @pl.when(layer == sec)
            def _():
                copies[0].start()

            @pl.when(layer != sec)
            def _():
                copies[1].start()

        else:
            copies[0].start()

    def hand_wait(which, source, out, layer):
        copies = hand_over(which, source, out, layer)
        if with_links:

            @pl.when(layer == sec)
            def _():
                copies[0].wait()

            @pl.when(layer != sec)
            def _():
                copies[1].wait_send()

        else:
            copies[0].wait()

    def hand_arrived(which, source, out):
        pltpu.make_async_remote_copy(
            src_ref=source,
            dst_ref=out.at[1 - sec],
            send_sem=ex_send.at[which],
            recv_sem=ex_recv.at[which],
            device_id=dev_core,
            device_id_type=MESH,
        ).wait_recv()

    def load(item):
        b = item % PER_LAYER

        def into(b):
            if b < 3:
                return m_qkv.at[:, :, :, :, b * LANES : (b + 1) * LANES]
            if b == 3:
                return m_attn
            if b < 8:
                return m_hidden.at[:, :, :, :, (b - 4) * LANES : (b - 3) * LANES]
            return None

        for k in range(PER_LAYER):

            @pl.when(b == k)
            def _():
                if k < 8:
                    pltpu.make_async_copy(full.at[item], into(k), load_sem.at[k]).start()
                else:
                    for g in range(2):
                        final_part(item, k, g, load_sem.at[k]).start()

    def final_part(item, b, g, semaphore):
        columns = slice((b % 2) * 512, (b % 2) * 512 + 512)
        return pltpu.make_async_copy(
            full.at[item, :, :, :, :, g * 512 : (g + 1) * 512],
            m_final.at[(b - 8) // 2, :, :, :, g * BLOCK : (g + 1) * BLOCK, columns],
            semaphore,
        )

    def loaded(b):
        pltpu.make_async_copy(full.at[0], m_attn, load_sem.at[b]).wait()

    def project(layer, b):
        scale = jnp.where(b == 0, 0.125, 1.0)
        shift = jnp.where(b == 0, row(layer, 0), jnp.where(b == 2, row(layer, 1), 0.0))
        at = pl.multiple_of(b * LANES, LANES)
        for n in range(0, LANES, TILE):
            columns = pl.ds(at + n, TILE)
            out = dot_nn(x[...], wide(m_qkv, columns)) + shift[:, n : n + TILE]
            qkv[:, columns] = (out.astype(jnp.bfloat16).astype(jnp.float32) * scale).astype(jnp.bfloat16)

    def save_p(layer, p):
        group, k = p // 2, p % 2
        return pltpu.make_async_copy(probs.at[group % 2, k], prob_save.at[layer, group, k], p_sem.at[p % 4])

    def attend(layer, first, last):
        def one(p, _):
            @pl.when(p >= 4)
            def _():
                save_p(layer, p - 4).wait()

            at = pl.multiple_of(p * 128, 128)
            q, k, v = (qkv[:, pl.ds(part * LANES + at, 128)] for part in range(3))
            total = None
            for half in range(2):
                scores = dot_nt(lane_half(q, half), k) + bias[...]
                exps = jnp.exp(scores - jnp.max(scores, -1, keepdims=True))
                share = (exps / jnp.sum(exps, -1, keepdims=True)).astype(jnp.bfloat16)
                probs[(p // 2) % 2, p % 2, half] = share
                out = dot_nn(share, lane_half(v, half))
                total = out if total is None else total + out
            ctx[:, pl.ds(at, 128)] = total.astype(jnp.bfloat16)
            save_p(layer, p).start()
            return 0

        lax.fori_loop(first, last, one, 0)

    def save(which):
        pairs = (
            (qkv, qkv_save),
            (ctx, ctx_save),
            (slope, slope_save),
            (norms.at[0], norm_save.at[0]),
            (invs.at[0], inv_save.at[0]),
            (norms.at[1], norm_save.at[1]),
            (invs.at[1], inv_save.at[1]),
        )
        return pltpu.make_async_copy(*pairs[which], save_sem.at[which])

    def normalize(layer, which, put, first=0, last=SEQ):
        for r in range(first, last, 128):
            rows = slice(r, r + 128)
            residual = acc[rows, :]
            centered = residual - jnp.mean(residual, -1, keepdims=True)
            inverse = lax.rsqrt(jnp.mean(centered * centered, -1, keepdims=True) + epsilon)
            normed = centered * inverse
            norms[which, rows, :] = normed.astype(jnp.bfloat16)
            invs[which, rows, :] = jnp.broadcast_to(inverse, (128, 128))
            put[rows, :] = (normed * row(layer, 8 + which) + row(layer, 10 + which)).astype(jnp.bfloat16)

    def attn_out(layer):
        for n in range(0, LANES, TILE):
            columns = slice(n, n + TILE)
            acc[:, columns] = x[:, columns].astype(jnp.float32) + (
                dot_nn(ctx[...], wide(m_attn, columns)) + row(layer, 2)[:, columns]
            )
        normalize(layer, 0, hid)

    def ffn_in(layer, j):
        shift = vec[layer, pl.ds(3 + j, 1), :]
        at = pl.multiple_of(j * LANES, LANES)
        for n in range(0, LANES, TILE):
            pre = dot_nn(hid[...], wide(m_hidden, pl.ds(at + n, TILE))) + shift[:, n : n + TILE]
            cdf = 0.5 * (1.0 + lax.erf(pre * math.sqrt(0.5)))
            pdf = jnp.exp(pre * pre * -0.5) * (1.0 / math.sqrt(2.0 * math.pi))
            value = (pre * cdf).astype(jnp.bfloat16)
            grade = (cdf + pre * pdf).astype(jnp.bfloat16)
            to = pl.ds(pl.multiple_of(j * 512 + n // 2, 128), 128)
            for half in range(2):
                act[half, :, to] = value[:, half * 128 : (half + 1) * 128]
                slope[half, :, to] = grade[:, half * 128 : (half + 1) * 128]

    def ffn_out(layer, half, part, rows=slice(0, SEQ)):
        for n in range(part * 512, part * 512 + 512, TILE):
            columns = slice(n, n + TILE)
            out = dot_nn(act[half, rows], wide(m_final.at[half], columns))
            if half == 0:
                acc[rows, columns] = hid[rows, columns].astype(jnp.float32) + (out + row(layer, 7)[:, columns])
            else:
                acc[rows, columns] += out

    def compute(c):
        layer, b = c // PER_LAYER, c % PER_LAYER

        def lower(then):
            pl.when(layer == 0)(then)

        @pl.when(b <= 2)
        def _():
            loaded(b)

            @pl.when((b == 0) & (layer == 1))
            def _():
                wait([save(5), save(6)])

            project(layer, b)

        @pl.when(b == 2)
        def _():
            lower(lambda: start([save(0)]))
            attend(layer, 0, 2)

        @pl.when(b == 3)
        def _():
            loaded(3)
            attend(layer, 2, 5)

        @pl.when(b == 4)
        def _():
            loaded(4)
            attend(layer, 5, 8)

        @pl.when(b == 5)
        def _():
            lower(lambda: start([save(1)]))
            loaded(5)
            attn_out(layer)
            lower(lambda: start([save(3), save(4)]))

        @pl.when((b >= 5) & (b <= 8))
        def _():
            ffn_in(layer, b - 5)

        @pl.when(b == 6)
        def _():
            loaded(6)
            wait([save_p(layer, p) for p in range(4, 8)])
            lower(lambda: wait([save(0), save(1)]))

        @pl.when(b == 7)
        def _():
            loaded(7)

        @pl.when(b == 8)
        def _():
            lower(lambda: start([save(2)]))
            loaded(8)

        @pl.when(b == 9)
        def _():
            loaded(9)

            @pl.when(layer == 1)
            def _():
                hand_wait(0, x, y_out, 0)

            ffn_out(layer, 0, 0)
            ffn_out(layer, 0, 1)
            lower(lambda: wait([save(3), save(4)]))

        @pl.when(b == 10)
        def _():
            loaded(10)
            ffn_out(layer, 1, 0)
            lower(lambda: wait([save(2)]))

        @pl.when(b == 11)
        def _():
            loaded(11)
            for top in (0, SEQ // 2):
                ffn_out(layer, 1, 1, slice(top, top + SEQ // 2))
                normalize(layer, 1, x, top, top + SEQ // 2)
            lower(lambda: start([save(5), save(6)]))
            hand_start(layer, x, y_out, layer)

    def step(t, _):
        if with_links:
            step_links(t)

        @pl.when(t == SETTLE)
        def _():
            settle()

        first = t - LOAD

        @pl.when((first >= 0) & (first < ITEMS))
        def _():
            if with_links:
                arrived(first)
            load(first)

        second = t - LOAD - 1

        @pl.when((second >= 0) & (second < ITEMS))
        def _():
            compute(second)

        return 0

    lax.fori_loop(0, ITEMS + LOAD + 1, step, 0)
    def fetch_final(half):
        return [
            final_part(8 + 2 * half + k, 8 + 2 * half + k, g, m_sem.at[(0, 12)[half] + 2 * k + g])
            for k in range(2)
            for g in range(2)
        ]

    def fetch_hidden():
        return [
            pltpu.make_async_copy(
                full.at[4 + j], m_hidden.at[:, :, :, :, j * LANES : (j + 1) * LANES], m_sem.at[4 + j]
            )
            for j in range(4)
        ]

    def fetch_attn():
        return [pltpu.make_async_copy(full.at[3], m_attn, m_sem.at[8])]

    def fetch_qkv():
        return [
            pltpu.make_async_copy(full.at[j], m_qkv.at[:, :, :, :, j * LANES : (j + 1) * LANES], m_sem.at[9 + j])
            for j in range(3)
        ]

    def fetch_norm(which):
        return [
            pltpu.make_async_copy(norm_save.at[which], norms.at[which], sem.at[2 * which]),
            pltpu.make_async_copy(inv_save.at[which], invs.at[which], sem.at[2 * which + 1]),
        ]

    def fetch_slope(half):
        return [pltpu.make_async_copy(slope_save.at[half], slope.at[half], sem.at[4 + half])]

    def fetch_heads():
        return [
            pltpu.make_async_copy(qkv_save, qkv, sem.at[6]),
            pltpu.make_async_copy(ctx_save, ctx, sem.at[7]),
        ]

    def fetch_probs(layer, group):
        return [pltpu.make_async_copy(prob_save.at[layer, group], probs.at[group % 2], p_sem.at[group % 2])]

    start(fetch_probs(1, 0) + fetch_probs(1, 1))
    take_grad.wait()

    def column_sum(values):
        return jnp.sum(values.astype(jnp.float32), 0, keepdims=True)

    def norm_back(layer, which, upstream_of, first=0, last=SEQ):
        gain = vec[layer, 8 + which : 9 + which, :]
        total = jnp.zeros((1, LANES), jnp.float32)
        for r in range(first, last, 128):
            rows = slice(r, r + 128)
            upstream = upstream_of(rows) * gain
            normed = norms[which, rows, :].astype(jnp.float32)
            back = invs[which, rows, 0:1] * (
                upstream
                - jnp.mean(upstream, -1, keepdims=True)
                - normed * jnp.mean(upstream * normed, -1, keepdims=True)
            )
            acc[rows, :] = back
            low = back.astype(jnp.bfloat16)
            hid[rows, :] = low
            total = total + column_sum(low)
        return total

    def sum_copy(source, target, k, device):
        return pltpu.make_async_remote_copy(
            src_ref=source,
            dst_ref=target,
            send_sem=sum_send.at[k],
            recv_sem=sum_recv.at[k],
            device_id=device,
            device_id_type=MESH,
        )

    def spread_heads(target, where, group, heads):
        for row in range(2):
            for k in range(2):
                at = (2 * group + k) * 128
                target[where, row : row + 1, at : at + 128] = heads[2 * row + k : 2 * row + k + 1, :]

    def core_sums():
        return [sum_copy(layer_sums.at[1 - sec], got_core, 0, dev_core)]

    def plane_sums():
        return [sum_copy(part_core, got_plane.at[k], 1 + k, device) for k, device in enumerate(in_plane)]

    def z_sums():
        return [sum_copy(part_plane, got_z.at[k], 4 + k, device) for k, device in enumerate(along_z)]

    def begin_early():
        layer_sums[0, 0:2, :] = jnp.zeros((2, LANES), jnp.float32)
        for group in range(GROUPS):
            spread_heads(layer_sums, 1, group, head_sums[1, group])
        start(core_sums())

    def early_sums(k):
        @pl.when(k == 0)
        def _():
            wait(core_sums())
            part_core[...] = layer_sums[sec] + got_core[...]
            start(plane_sums())

        @pl.when(k == 2)
        def _():
            wait(plane_sums())
            part_plane[...] = part_core[...] + (got_plane[0] + got_plane[1]) + got_plane[2]
            start(z_sums())

    def end_early():
        wait(z_sums())
        sums[0] = part_plane[...] + (got_z[0] + got_z[1]) + got_z[2]

    def late_send(group):
        own = 16 * sec + lax.axis_index("dp")
        got_late[group, own] = head_sums[0, group]

        def one(k, _):
            sum_late(group, own, (0, (lax.axis_index("dp") + k) % 16)).start()
            return 0

        lax.fori_loop(1, 16, one, 0)

        @pl.when(sec == 1)
        def _():
            sum_late(group, own, dev_core).start()

    def sum_late(group, slot, device):
        return pltpu.make_async_remote_copy(
            src_ref=head_sums.at[0, group],
            dst_ref=got_late.at[group, slot],
            send_sem=late_sent.at[group],
            recv_sem=late_got.at[group],
            device_id=device,
            device_id_type=MESH,
        )

    def end_late():
        def many(group, count):
            several = got_late.at[group, pl.ds(0, count)]
            return pltpu.make_async_remote_copy(
                src_ref=several,
                dst_ref=several,
                send_sem=late_sent.at[group],
                recv_sem=late_got.at[group],
                device_id=dev_core,
                device_id_type=MESH,
            )

        for group in range(GROUPS):
            for core in range(2):

                @pl.when(sec == core)
                def _():
                    many(group, 15 + core).wait_send()
                    if core == 0:
                        many(group, 31).wait_recv()
                        spread_heads(sums, 0, group, jnp.sum(got_late[group], 0))

    def one_layer(s, _):
        layer = 1 - s

        def prefetch(copies):
            @pl.when(s == 0)
            def _():
                start(copies)

        def fetched(copies):
            @pl.when(s == 1)
            def _():
                wait(copies)

        fetched(fetch_norm(1) + fetch_final(0) + fetch_slope(0) + fetch_final(1) + fetch_slope(1))
        fetched(fetch_hidden() + fetch_norm(0) + fetch_attn())
        layer_sums[layer, 7:8, :] = norm_back(layer, 1, lambda rows: grad[rows, :].astype(jnp.float32))
        for half in range(2):
            for n in range(0, 2048, TILE):
                chip = n // 128
                block = m_final[half, chip // 4, (chip // 2) % 2].reshape(TILE, LANES)
                back = dot_nt(hid[...], block) * slope[half, :, n : n + TILE].astype(jnp.float32)
                low = back.astype(jnp.bfloat16)
                total = column_sum(low)
                for k in range(2):
                    at = (chip + k) * 256 + half * 128
                    part = slice(k * 128, (k + 1) * 128)
                    act[at // 2048, :, at % 2048 : at % 2048 + 128] = low[:, part]
                    layer_sums[layer, 3 + at // LANES : 4 + at // LANES, at % LANES : at % LANES + 128] = total[:, part]
        prefetch(fetch_norm(1) + fetch_final(0) + fetch_slope(0) + fetch_final(1) + fetch_slope(1))

        @pl.when(s == 1)
        def _():
            hand_wait(3, grad, grad_out, 1)

        total = jnp.zeros((1, LANES), jnp.float32)
        for top in (0, SEQ // 2):
            rows = slice(top, top + SEQ // 2)
            for n in range(0, LANES, TILE):
                block = m_hidden[n // TILE].reshape(TILE, 4 * LANES)
                acc[rows, n : n + TILE] += dot_nt(act[0, rows], block[:, : 2 * LANES]) + dot_nt(
                    act[1, rows], block[:, 2 * LANES :]
                )
            total = total + norm_back(
                layer, 0, lambda at: acc[at, :].astype(jnp.bfloat16).astype(jnp.float32), top, top + SEQ // 2
            )
        layer_sums[layer, 2:3, :] = total
        for n in range(0, LANES, TILE):
            block = m_attn[n // TILE].reshape(TILE, LANES)
            grad[:, n : n + TILE] = dot_nt(hid[...], block).astype(jnp.bfloat16)
        prefetch(fetch_hidden() + fetch_norm(0) + fetch_attn())
        fetched(fetch_heads())

        def one_group(group, _):
            wait(fetch_probs(layer, group))
            for k in range(2):
                one_pair(2 * group + k, group, k, probs.at[group % 2, k])

            @pl.when(group < GROUPS - 2)
            def _():
                start(fetch_probs(layer, group + 2))

            if with_links:

                @pl.when(s == 1)
                def _():
                    late_send(group)
                    early_sums(group)

            return 0

        def one_pair(p, group, k, shares):
            at = pl.multiple_of(p * 128, 128)
            q, keys, v = (qkv[:, pl.ds(part * LANES + at, 128)] for part in range(3))
            upper = grad[:, pl.ds(at, 128)]
            product = upper.astype(jnp.float32) * ctx[:, pl.ds(at, 128)].astype(jnp.float32)
            q_t, k_t, upper_t = q.T, keys.T, upper.T
            grad_q, grad_k, grad_v = [], [], []
            for half in range(2):
                weights = shares[half]
                delta = jnp.sum(lane_half(product, half), -1, keepdims=True)
                scores = dot_nt(lane_half(upper, half), v)
                low = (weights.astype(jnp.float32) * (scores - delta)).astype(jnp.bfloat16)
                here = slice(half * HEAD_DIM, (half + 1) * HEAD_DIM)
                grad_q.append(dot_nt(k_t[here], low) * 0.125)
                grad_k.append(dot_nn(q_t[here], low))
                grad_v.append(dot_nn(upper_t[here], weights))
            for part, rows in enumerate((grad_q, grad_k, grad_v)):
                back = jnp.concatenate(rows, 0).astype(jnp.bfloat16).T
                act[part // 2, :, pl.ds((part % 2) * LANES + at, 128)] = back
                if part != 1:
                    head_sums[layer, group, part + k : part + k + 1, :] = column_sum(back)

        if with_links:

            @pl.when(s == 1)
            def _():
                begin_early()

        lax.fori_loop(0, GROUPS, one_group, 0)
        prefetch(fetch_heads() + fetch_probs(0, 0) + fetch_probs(0, 1))
        fetched(fetch_qkv())

        def columns_of(n):
            block = m_qkv[n // TILE].reshape(TILE, 3 * LANES)
            columns = slice(n, n + TILE)
            total = dot_nt(act[0], block[:, : 2 * LANES]) + dot_nt(act[1, :, :LANES], block[:, 2 * LANES :])
            grad[:, columns] = (acc[:, columns] + total).astype(jnp.bfloat16)

        if with_links:

            @pl.when(s == 0)
            def _():
                for n in range(0, LANES, TILE):
                    columns_of(n)

            @pl.when(s == 1)
            def _():
                for n in range(0, LANES, TILE):
                    columns_of(n)
                    if n == TILE:
                        end_early()
                end_late()

        else:
            for n in range(0, LANES, TILE):
                columns_of(n)
        prefetch(fetch_qkv())
        hand_start(2 + layer, grad, grad_out, layer)
        return 0

    lax.fori_loop(0, 2, one_layer, 0)
    hand_wait(1, x, y_out, 1)
    hand_wait(2, grad, grad_out, 0)
    if with_links:
        hand_arrived(sec, x, y_out)
        hand_arrived(2 + sec, grad, grad_out)
        end_links()
    else:
        for layer in range(2):
            for group in range(GROUPS):
                spread_heads(layer_sums, layer, group, head_sums[layer, group])
        sums[...] = layer_sums[...]


def both_layers(weights, tokens, cotangent, segments, lengths, vectors):
    with_links = len(weights) == 4
    low, wide_type = jnp.bfloat16, jnp.float32
    in_hbm = pl.BlockSpec(memory_space=pltpu.HBM)
    in_vmem = pl.BlockSpec(memory_space=pltpu.VMEM)
    in_smem = pl.BlockSpec(memory_space=pltpu.SMEM)
    shape = jax.ShapeDtypeStruct
    sums = (1, 8, LANES) if with_links else (2, 8, LANES)
    outs = [shape((ITEMS, 4, 2, 2, BLOCK, LANES), low)] if with_links else []
    outs += [
        pltpu.VMEM((2, SEQ, LANES), low),
        pltpu.VMEM((2, SEQ, LANES), low),
        shape(sums, wide_type),
        shape((2, GROUPS, 2, 2, SEQ, SEQ), low),
        shape((SEQ, 3 * LANES), low),
        shape((SEQ, LANES), low),
        shape((2, SEQ, 2 * LANES), low),
        shape((2, SEQ, LANES), low),
        shape((2, SEQ, 128), wide_type),
    ]
    out_specs = [in_hbm] * len(outs)
    for k in range(3):
        out_specs[k + with_links] = in_vmem
    dma = pltpu.SemaphoreType.DMA
    scratch = [
        pltpu.VMEM((SEQ, LANES), low),
        pltpu.VMEM((2, 16, LANES), wide_type),
        pltpu.VMEM((4, 2, 2, BLOCK, 3 * LANES), low),
        pltpu.VMEM((4, 2, 2, BLOCK, LANES), low),
        pltpu.VMEM((4, 2, 2, BLOCK, 4 * LANES), low),
        pltpu.VMEM((2, 4, 2, 2, 2 * BLOCK, LANES), low),
        pltpu.VMEM((SEQ, 3 * LANES), low),
        pltpu.VMEM((SEQ, LANES), low),
        pltpu.VMEM((SEQ, LANES), low),
        pltpu.VMEM((2, SEQ, 2 * LANES), low),
        pltpu.VMEM((2, SEQ, 2 * LANES), low),
        pltpu.VMEM((SEQ, LANES), wide_type),
        pltpu.VMEM((SEQ, SEQ), wide_type),
        pltpu.VMEM((2, 2, 2, SEQ, SEQ), low),
        pltpu.VMEM((2, SEQ, LANES), low),
        pltpu.VMEM((2, SEQ, 128), wide_type),
        pltpu.VMEM((SEQ, LANES), low),
        pltpu.VMEM((2, 8, LANES), wide_type),
        pltpu.VMEM((2, GROUPS, 8, 128), wide_type),
        dma((3,)),
        dma((PER_LAYER,)),
        dma((4,)),
        dma((7,)),
        dma((16,)),
        dma((8,)),
        dma((4,)),
    ]
    if with_links:
        specs = [in_hbm] * 6 + [in_vmem, in_smem] + [in_vmem] * 7
        scratch += [
            pltpu.VMEM((PER_LAYER, HALF, LANES), low),
            pltpu.VMEM((8, LANES), wide_type),
            pltpu.VMEM((3, 8, LANES), wide_type),
            pltpu.VMEM((3, 8, LANES), wide_type),
            pltpu.VMEM((GROUPS, 32, 8, 128), wide_type),
            pltpu.VMEM((8, LANES), wide_type),
            pltpu.VMEM((8, LANES), wide_type),
            dma((PER_LAYER,)),
            dma((PER_LAYER,)),
            dma((PER_LAYER,)),
            dma((PER_LAYER,)),
            dma((17,)),
            dma((17, ITEMS)),
            dma((2,)),
            dma((4,)),
            dma((4,)),
            dma((7,)),
            dma((7,)),
            dma((GROUPS,)),
            dma((GROUPS,)),
        ]
        params = pltpu.CompilerParams(collective_id=0, has_side_effects=True, vmem_limit_bytes=VMEM_LIMIT)
    else:
        specs = [in_hbm] * 3 + [in_vmem, in_smem, in_hbm]
        params = pltpu.CompilerParams(vmem_limit_bytes=VMEM_LIMIT)
    results = pl.pallas_call(
        partial(layers_kernel, with_links),
        out_shape=tuple(outs),
        in_specs=specs,
        out_specs=tuple(out_specs),
        scratch_shapes=scratch,
        compiler_params=params,
    )(*weights, tokens, cotangent, segments, lengths, *vectors)
    return results[1:4] if with_links else results[:3]


def gather(w_qkv, w_out, w_in, w_ffn_out):
    matrices = [lax.all_gather(w[0], "dp", axis=0, tiled=True) for w in (w_qkv, w_out, w_in, w_ffn_out)]
    qkv, attn, hidden, final = matrices
    blocks = [qkv[:, b * LANES : (b + 1) * LANES] for b in range(3)] + [attn]
    blocks += [hidden[:, b * LANES : (b + 1) * LANES] for b in range(4)]
    final = final.reshape(16, 2, 2, BLOCK, 2, 512).transpose(1, 4, 0, 3, 2, 5).reshape(4, 1024, LANES)
    own = jnp.concatenate([jnp.stack(blocks), final])
    return lax.all_gather(own, "section", axis=0, tiled=True).reshape(24, 4, 2, 2, BLOCK, LANES)


def on_device(
    tokens,
    segment_ids,
    row_lengths,
    w_qkv,
    w_out,
    w_in,
    w_ffn_out,
    bias_q,
    bias_v,
    bias_out,
    bias_in,
    bias_ffn_out,
    ln_gain,
    ln_shift,
    out_cotangent,
):
    weights = (w_qkv, w_out, w_in, w_ffn_out)
    vectors = (bias_q, bias_v, bias_out, bias_in, bias_ffn_out, ln_gain, ln_shift)
    data = (tokens, out_cotangent, segment_ids, row_lengths.T)
    if w_qkv.shape[1] == BLOCK:
        tops, grads, sums = both_layers(weights, *data, vectors)
        sums = sums[0]
    else:
        sec = lax.axis_index("section")
        wide_in, gains, shifts = bias_in.reshape(4, LANES), ln_gain[0], ln_shift[0]
        vec = jnp.concatenate(
            [bias_q, bias_v, bias_out, wide_in, bias_ffn_out, gains, shifts, jnp.zeros((4, LANES))]
        )
        vec = lax.all_gather(vec, "section", axis=0)
        tops, grads, sums = both_layers((gather(*weights),), *data, (vec,))

        def swap(array):
            return lax.ppermute(array, "section", [(0, 1), (1, 0)])

        def placed(both):
            got = swap(jnp.where(sec == 0, both[1], both[0]))
            return jnp.where(sec == 0, jnp.stack([both[0], got]), jnp.stack([got, both[1]]))

        tops, grads = placed(tops), placed(grads)
        sums = jnp.where(sec == 0, sums[0], sums[1]) + swap(jnp.where(sec == 0, sums[1], sums[0]))
        sums = lax.psum(sums, "dp")
    totals = (sums[0:1], sums[1:2], sums[2:3], sums[3:7].reshape(1, 4 * LANES), sums[7:8])
    return (tops[None, :, None], grads[None, :, None]) + totals


def solution(mesh):
    placed = (
        P(None, "dp", None, None),
        P(None, "dp", None),
        P(None, "dp"),
        P("section", "dp", None),
        P("section", "dp", None),
        P("section", "dp", None),
        P("section", "dp", None),
        P("section", None),
        P("section", None),
        P("section", None),
        P("section", None),
        P("section", None),
        P("section", None, None),
        P("section", None, None),
        P(None, "dp", None, None),
    )
    return jax.shard_map(
        on_device,
        mesh=mesh,
        in_specs=placed,
        out_specs=(
            P("section", None, "dp", None, None),
            P("section", None, "dp", None, None),
            P("section", None),
            P("section", None),
            P("section", None),
            P("section", None),
            P("section", None),
        ),
        check_vma=False,
    )
```

```python
from functools import partial
import math

import jax
import jax.numpy as jnp
from jax import lax
from jax.experimental import pallas as pl
from jax.experimental.pallas import tpu as pltpu
from jax.sharding import PartitionSpec as P

HEAD_DIM = 64
SEQ = 512
GROUPS = 4
epsilon = 1e-06
VMEM_LIMIT = 58 * 2**20
MESH = pl.DeviceIdType.MESH
ITEMS = 24
PER_LAYER = ITEMS // 2
LANES = 1024
BLOCK = 64
HALF = BLOCK // 2
CUT = 384
STAGES = (1, 2, 3, 4, 5)
LOAD = 6
FRONT = 6
SETTLE = 3
TILE = 256


def link_plan(wq, wo, wi, wf, full, vec, stage, in_sem, place_sem, cross_send, cross_recv, send_sem, recv_sem, vec_sem):
    sec = lax.axis_index("section")
    chip = lax.axis_index("dp")
    per_layer, items = PER_LAYER, ITEMS
    z = chip // 4
    y = (chip // 2) % 2
    x = chip % 2
    dev_x = (sec, z * 4 + y * 2 + 1 - x)
    dev_y = (sec, z * 4 + (1 - y) * 2 + x)
    dev_xy = (sec, z * 4 + (1 - y) * 2 + 1 - x)
    dev_up = (sec, jnp.minimum(z + 1, 3) * 4 + y * 2 + x)
    dev_down = (sec, jnp.maximum(z - 1, 0) * 4 + y * 2 + x)
    dev_core = (1 - sec, chip)
    in_plane = (dev_x, dev_y, dev_xy)
    along_z = tuple((sec, ((z + k) % 4) * 4 + y * 2 + x) for k in (1, 2, 3))

    def own_block(b, row):
        if b < 3:
            return wq.at[0, pl.ds(row, HALF), b * LANES : (b + 1) * LANES]
        if b == 3:
            return wo.at[0, pl.ds(row, HALF), :]
        if b < 8:
            return wi.at[0, pl.ds(row, HALF), (b - 4) * LANES : (b - 3) * LANES]
        pair, columns = (b - 8) // 2, slice((b % 2) * 512, (b % 2) * 512 + 512)
        return [wf.at[0, pl.ds((2 * pair + g) * BLOCK + row, HALF), columns] for g in range(2)]

    mine = pl.multiple_of(sec * HALF, HALF)
    other = pl.multiple_of((1 - sec) * HALF, HALF)

    def to_stage(b):
        return pltpu.make_async_copy(stage.at[b], stage.at[b], in_sem.at[b])

    def stage_start(b):
        block = own_block(b, mine)
        if b < 8:
            pltpu.make_async_copy(block, stage.at[b], in_sem.at[b]).start()
        else:
            for g in range(2):
                pltpu.make_async_copy(block[g], stage.at[b, :, g * 512 : (g + 1) * 512], in_sem.at[b]).start()

    def to_place(b):
        return pltpu.make_async_copy(
            stage.at[b], full.at[sec * per_layer + b, z, y, x, pl.ds(mine, HALF), :], place_sem.at[b]
        )

    def cross_copy(b, source, columns):
        return pltpu.make_async_remote_copy(
            src_ref=source,
            dst_ref=full.at[sec * per_layer + b, z, y, x, pl.ds(other, HALF), columns],
            send_sem=cross_send.at[b],
            recv_sem=cross_recv.at[b],
            device_id=dev_core,
            device_id_type=MESH,
        )

    def cross_start(b):
        block = own_block(b, other)
        if b < 8:
            cross_copy(b, block, slice(None)).start()
        else:
            for g in range(2):
                cross_copy(b, block[g], slice(g * 512, (g + 1) * 512)).start()

    def cross_sent(b):
        cross_copy(b, stage.at[b], slice(None)).wait_send()

    def give_vec(where):
        return pltpu.make_async_remote_copy(
            src_ref=where,
            dst_ref=where,
            send_sem=vec_sem.at[0],
            recv_sem=vec_sem.at[1],
            device_id=dev_core,
            device_id_type=MESH,
        )

    def begin():
        for b in range(per_layer):
            stage_start(b)
        barrier = pltpu.get_barrier_semaphore()
        for k in range(1, 32):
            device = ((sec + k // 16) % 2, (chip + k) % 16)
            pl.semaphore_signal(barrier, inc=1, device_id=device, device_id_type=MESH)
        pl.semaphore_wait(barrier, 31)
        for b in range(per_layer):
            cross_start(b)
        give_vec(vec.at[sec]).start()
        for b in range(per_layer):
            to_stage(b).wait()
            to_place(b).start()

    def vec_here():
        give_vec(vec.at[sec]).wait_send()
        give_vec(vec.at[1 - sec]).wait_recv()

    def copy(ref, kind, item, device):
        return pltpu.make_async_remote_copy(
            src_ref=ref,
            dst_ref=ref,
            send_sem=send_sem.at[kind],
            recv_sem=recv_sem.at[kind, item],
            device_id=device,
            device_id_type=MESH,
        )

    def views(core):
        rows = slice(core * HALF, (core + 1) * HALF)
        first, last = slice(0, CUT), slice(CUT, LANES)
        if core == 0:
            pair = lambda i, at: full.at[i, at, :, x, rows, last]
            eight_first = lambda i: full.at[i, :, y, :, rows, first]
            eight_last = lambda i: full.at[i, :, :, x, rows, last]
            towards = (dev_x, dev_y)
        else:
            pair = lambda i, at: full.at[i, at, y, :, rows, last]
            eight_first = lambda i: full.at[i, :, :, x, rows, first]
            eight_last = lambda i: full.at[i, :, y, :, rows, last]
            towards = (dev_y, dev_x)
        return (
            towards,
            lambda i, at: full.at[i, at, y, x, rows, first],
            lambda i: full.at[i, :, y, x, rows, first],
            eight_first,
            lambda i, at: full.at[i, at, y, x, rows, last],
            pair,
            eight_last,
            lambda i: full.at[i, :, :, :, rows, :],
        )

    def z_send(base, block, hop, item, at):
        if at < 3 and at - (hop - 1) >= 0:
            copy(block(item, at - (hop - 1)), base + hop - 1, item, dev_up).start()
        if at > 0 and at + (hop - 1) <= 3:
            copy(block(item, at + (hop - 1)), base + 2 + hop, item, dev_down).start()

    def z_recv(base, block, hop, item, at):
        if at - hop >= 0:
            copy(block(item, at - hop), base + hop - 1, item, dev_up).wait_recv()
        if at + hop <= 3:
            copy(block(item, at + hop), base + 2 + hop, item, dev_down).wait_recv()

    def step_at(t, at, core):
        (dev_u, dev_v), own_a, col_a, eight_a, own_d, pair_d, eight_d, whole = views(core)
        turns = [t - offset for offset in STAGES]

        def live(item):
            return (item >= 0) & (item < items)

        def first_move(item):
            @pl.when(live(item))
            def _():
                layer, b = item // per_layer, item % per_layer

                @pl.when(layer == core)
                def _():
                    pltpu.make_async_copy(
                        stage.at[b], full.at[item, z, y, x, pl.ds(core * HALF, HALF), :], place_sem.at[b]
                    ).wait()

                @pl.when(layer != core)
                def _():
                    mine_there = full.at[item, z, y, x, pl.ds(core * HALF, HALF), :]
                    pltpu.make_async_remote_copy(
                        src_ref=mine_there,
                        dst_ref=mine_there,
                        send_sem=cross_send.at[b],
                        recv_sem=cross_recv.at[b],
                        device_id=dev_core,
                        device_id_type=MESH,
                    ).wait_recv()

                copy(own_d(item, at), 8, item, dev_v).start()

        for lead in range(FRONT):
            first_move(t * FRONT + lead)

        @pl.when(live(t))
        def _():
            z_send(0, own_a, 1, t, at)

        item1 = turns[0]

        @pl.when(live(item1))
        def _():
            z_recv(0, own_a, 1, item1, at)
            z_send(0, own_a, 2, item1, at)
            copy(own_d(item1, at), 8, item1, dev_v).wait_recv()
            z_send(9, pair_d, 1, item1, at)

        item2 = turns[1]

        @pl.when(live(item2))
        def _():
            z_recv(0, own_a, 2, item2, at)
            z_send(0, own_a, 3, item2, at)
            z_recv(9, pair_d, 1, item2, at)
            z_send(9, pair_d, 2, item2, at)

        item3 = turns[2]

        @pl.when(live(item3))
        def _():
            z_recv(0, own_a, 3, item3, at)
            copy(col_a(item3), 6, item3, dev_u).start()
            z_recv(9, pair_d, 2, item3, at)
            z_send(9, pair_d, 3, item3, at)

        item4 = turns[3]

        @pl.when(live(item4))
        def _():
            copy(col_a(item4), 6, item4, dev_u).wait_recv()
            copy(eight_a(item4), 7, item4, dev_v).start()
            z_recv(9, pair_d, 3, item4, at)
            copy(eight_d(item4), 15, item4, dev_u).start()

        item5 = turns[4]

        @pl.when(live(item5))
        def _():
            copy(eight_a(item5), 7, item5, dev_v).wait_recv()
            copy(eight_d(item5), 15, item5, dev_u).wait_recv()
            copy(whole(item5), 16, item5, dev_core).start()

    def step(t):
        for at in range(4):
            for core in range(2):

                @pl.when((z == at) & (sec == core))
                def _():
                    step_at(t, at, core)

    def arrived(item):
        for core in range(2):

            @pl.when(sec == core)
            def _():
                copy(views(1 - core)[-1](item), 16, item, dev_core).wait_recv()

    def end():
        for b in range(per_layer):
            cross_sent(b)
        for core in range(2):

            @pl.when(sec == core)
            def _():
                _, own_a, col_a, eight_a, own_d, pair_d, eight_d, whole = views(core)
                every = slice(None)

                def sent(ref, kind):
                    copy(ref, kind, 0, dev_core).wait_send()

                sent(whole(every), 16)
                sent(col_a(every), 6)
                sent(eight_a(every), 7)
                sent(eight_d(every), 15)
                sent(own_d(every, 0), 8)
                for hop in (1, 2, 3):
                    for base, block in ((0, own_a), (9, pair_d)):

                        @pl.when((z < 3) & (z - (hop - 1) >= 0))
                        def _():
                            sent(block(every, 0), base + hop - 1)

                        @pl.when((z > 0) & (z + (hop - 1) <= 3))
                        def _():
                            sent(block(every, 0), base + 2 + hop)

    return begin, vec_here, step, arrived, end, dev_core, in_plane, along_z


def wide(ref, columns):
    block = ref[:, :, :, :, columns]
    return block.reshape(-1, block.shape[-1])


def dot_nt(left, right):
    return lax.dot_general(left, right, (((1,), (1,)), ((), ())), preferred_element_type=jnp.float32)


def dot_nn(left, right):
    return jnp.dot(left, right, preferred_element_type=jnp.float32)


def pair_bias(codes):
    down = jnp.broadcast_to(codes, (128, codes.shape[1])).T[:, :1]
    return jnp.where(down == codes, 0.0, -1000000000.0)


def lane_half(pair, half):
    lanes = lax.broadcasted_iota(jnp.int32, pair.shape, 1)
    return jnp.where((lanes < HEAD_DIM) == (half == 0), pair, jnp.zeros_like(pair))


def layers_kernel(with_links, *refs):
    if with_links:
        wq, wo, wi, wf, *refs = refs
    else:
        full, *refs = refs
    tokens, cotangent, segments, lengths, *refs = refs
    if with_links:
        parts, refs = refs[:7], refs[7:]
        full, *refs = refs
    else:
        given_vec, *refs = refs
    (y_out, grad_out, sums, prob_save, qkv_save, ctx_save, slope_save, norm_save, inv_save, *refs) = refs
    (x, vec, m_qkv, m_attn, m_hidden, m_final, qkv, ctx, hid, act, slope, acc, bias, probs, norms, invs, *refs) = refs
    (grad, layer_sums, head_sums, in_sem, load_sem, p_sem, save_sem, m_sem, sem, out_sem, *refs) = refs
    sec = lax.axis_index("section")
    if with_links:
        (stage, got_core, got_plane, got_z, got_late, part_core, part_plane, *link_sems) = refs
        *link_sems, ex_send, ex_recv, sum_send, sum_recv, late_sent, late_got = link_sems

    def start(copies):
        for copy in copies:
            copy.start()

    def wait(copies):
        for copy in copies:
            copy.wait()

    take_x = pltpu.make_async_copy(tokens.at[sec, 0], x, in_sem.at[0])
    take_grad = pltpu.make_async_copy(cotangent.at[sec, 0], grad, in_sem.at[1])
    take_x.start()
    take_grad.start()
    head_sums[...] = jnp.zeros_like(head_sums)
    if with_links:
        bias_q, bias_v, bias_out, bias_in, bias_ffn_out, ln_gain, ln_shift = parts
        for k, ref in enumerate((bias_q, bias_v, bias_out)):
            vec[sec, k : k + 1, :] = ref[...]
        for k in range(4):
            vec[sec, 3 + k : 4 + k, :] = bias_in[:, k * LANES : (k + 1) * LANES]
        vec[sec, 7:8, :] = bias_ffn_out[...]
        vec[sec, 8:10, :] = ln_gain[0]
        vec[sec, 10:12, :] = ln_shift[0]
        vec[sec, 12:16, :] = jnp.zeros((4, LANES), jnp.float32)
        begin_links, vec_here, step_links, arrived, end_links, dev_core, in_plane, along_z = link_plan(
            wq, wo, wi, wf, full, vec, stage, *link_sems
        )
        begin_links()
    else:
        take_vec = pltpu.make_async_copy(given_vec, vec, in_sem.at[2])
        take_vec.start()

    def settle():
        valid = lax.broadcasted_iota(jnp.int32, (1, SEQ), 1) < lengths[0, sec]
        bias[...] = pair_bias(segments[sec] * 2 + valid.astype(jnp.int32))
        take_x.wait()
        if with_links:
            vec_here()
        else:
            take_vec.wait()

    def row(layer, index):
        return vec[layer, index : index + 1, :]

    def hand_over(which, source, out, layer):
        local = pltpu.make_async_copy(source, out.at[sec], out_sem.at[which])
        if with_links:
            far = pltpu.make_async_remote_copy(
                src_ref=source,
                dst_ref=out.at[sec],
                send_sem=ex_send.at[which],
                recv_sem=ex_recv.at[which],
                device_id=dev_core,
                device_id_type=MESH,
            )
            return local, far
        return (pltpu.make_async_copy(source, out.at[layer], out_sem.at[which]),)

    def hand_start(which, source, out, layer):
        copies = hand_over(which, source, out, layer)
        if with_links:

            @pl.when(layer == sec)
            def _():
                copies[0].start()

            @pl.when(layer != sec)
            def _():
                copies[1].start()

        else:
            copies[0].start()

    def hand_wait(which, source, out, layer):
        copies = hand_over(which, source, out, layer)
        if with_links:

            @pl.when(layer == sec)
            def _():
                copies[0].wait()

            @pl.when(layer != sec)
            def _():
                copies[1].wait_send()

        else:
            copies[0].wait()

    def hand_arrived(which, source, out):
        pltpu.make_async_remote_copy(
            src_ref=source,
            dst_ref=out.at[1 - sec],
            send_sem=ex_send.at[which],
            recv_sem=ex_recv.at[which],
            device_id=dev_core,
            device_id_type=MESH,
        ).wait_recv()

    def load(item):
        b = item % PER_LAYER

        def into(b):
            if b < 3:
                return m_qkv.at[:, :, :, :, b * LANES : (b + 1) * LANES]
            if b == 3:
                return m_attn
            if b < 8:
                return m_hidden.at[:, :, :, :, (b - 4) * LANES : (b - 3) * LANES]
            return None

        for k in range(PER_LAYER):

            @pl.when(b == k)
            def _():
                if k < 8:
                    pltpu.make_async_copy(full.at[item], into(k), load_sem.at[k]).start()
                else:
                    for g in range(2):
                        final_part(item, k, g, load_sem.at[k]).start()

    def final_part(item, b, g, semaphore):
        columns = slice((b % 2) * 512, (b % 2) * 512 + 512)
        return pltpu.make_async_copy(
            full.at[item, :, :, :, :, g * 512 : (g + 1) * 512],
            m_final.at[(b - 8) // 2, :, :, :, g * BLOCK : (g + 1) * BLOCK, columns],
            semaphore,
        )

    def loaded(b):
        pltpu.make_async_copy(full.at[0], m_attn, load_sem.at[b]).wait()

    def project(layer, b):
        scale = jnp.where(b == 0, 0.125, 1.0)
        shift = jnp.where(b == 0, row(layer, 0), jnp.where(b == 2, row(layer, 1), 0.0))
        at = pl.multiple_of(b * LANES, LANES)
        for n in range(0, LANES, TILE):
            columns = pl.ds(at + n, TILE)
            out = dot_nn(x[...], wide(m_qkv, columns)) + shift[:, n : n + TILE]
            qkv[:, columns] = (out.astype(jnp.bfloat16).astype(jnp.float32) * scale).astype(jnp.bfloat16)

    def save_p(layer, p):
        group, k = p // 2, p % 2
        return pltpu.make_async_copy(probs.at[group % 2, k], prob_save.at[layer, group, k], p_sem.at[p % 4])

    def attend(layer, first, last):
        def one(p, _):
            @pl.when(p >= 4)
            def _():
                save_p(layer, p - 4).wait()

            at = pl.multiple_of(p * 128, 128)
            q, k, v = (qkv[:, pl.ds(part * LANES + at, 128)] for part in range(3))
            total = None
            for half in range(2):
                scores = dot_nt(lane_half(q, half), k) + bias[...]
                exps = jnp.exp(scores - jnp.max(scores, -1, keepdims=True))
                share = (exps / jnp.sum(exps, -1, keepdims=True)).astype(jnp.bfloat16)
                probs[(p // 2) % 2, p % 2, half] = share
                out = dot_nn(share, lane_half(v, half))
                total = out if total is None else total + out
            ctx[:, pl.ds(at, 128)] = total.astype(jnp.bfloat16)
            save_p(layer, p).start()
            return 0

        lax.fori_loop(first, last, one, 0)

    def save(which):
        pairs = (
            (qkv, qkv_save),
            (ctx, ctx_save),
            (slope, slope_save),
            (norms.at[0], norm_save.at[0]),
            (invs.at[0], inv_save.at[0]),
            (norms.at[1], norm_save.at[1]),
            (invs.at[1], inv_save.at[1]),
        )
        return pltpu.make_async_copy(*pairs[which], save_sem.at[which])

    def normalize(layer, which, put, first=0, last=SEQ):
        for r in range(first, last, 128):
            rows = slice(r, r + 128)
            residual = acc[rows, :]
            centered = residual - jnp.mean(residual, -1, keepdims=True)
            inverse = lax.rsqrt(jnp.mean(centered * centered, -1, keepdims=True) + epsilon)
            normed = centered * inverse
            norms[which, rows, :] = normed.astype(jnp.bfloat16)
            invs[which, rows, :] = jnp.broadcast_to(inverse, (128, 128))
            put[rows, :] = (normed * row(layer, 8 + which) + row(layer, 10 + which)).astype(jnp.bfloat16)

    def attn_out(layer):
        for n in range(0, LANES, TILE):
            columns = slice(n, n + TILE)
            acc[:, columns] = x[:, columns].astype(jnp.float32) + (
                dot_nn(ctx[...], wide(m_attn, columns)) + row(layer, 2)[:, columns]
            )
        normalize(layer, 0, hid)

    def ffn_in(layer, j):
        shift = vec[layer, pl.ds(3 + j, 1), :]
        at = pl.multiple_of(j * LANES, LANES)
        for n in range(0, LANES, TILE):
            pre = dot_nn(hid[...], wide(m_hidden, pl.ds(at + n, TILE))) + shift[:, n : n + TILE]
            cdf = 0.5 * (1.0 + lax.erf(pre * math.sqrt(0.5)))
            pdf = jnp.exp(pre * pre * -0.5) * (1.0 / math.sqrt(2.0 * math.pi))
            value = (pre * cdf).astype(jnp.bfloat16)
            grade = (cdf + pre * pdf).astype(jnp.bfloat16)
            to = pl.ds(pl.multiple_of(j * 512 + n // 2, 128), 128)
            for half in range(2):
                act[half, :, to] = value[:, half * 128 : (half + 1) * 128]
                slope[half, :, to] = grade[:, half * 128 : (half + 1) * 128]

    def ffn_out(layer, half, part, rows=slice(0, SEQ)):
        for n in range(part * 512, part * 512 + 512, TILE):
            columns = slice(n, n + TILE)
            out = dot_nn(act[half, rows], wide(m_final.at[half], columns))
            if half == 0:
                acc[rows, columns] = hid[rows, columns].astype(jnp.float32) + (out + row(layer, 7)[:, columns])
            else:
                acc[rows, columns] += out

    def compute(c):
        layer, b = c // PER_LAYER, c % PER_LAYER

        def lower(then):
            pl.when(layer == 0)(then)

        @pl.when(b <= 2)
        def _():
            loaded(b)

            @pl.when((b == 0) & (layer == 1))
            def _():
                wait([save(5), save(6)])

            project(layer, b)

        @pl.when(b == 2)
        def _():
            lower(lambda: start([save(0)]))
            attend(layer, 0, 2)

        @pl.when(b == 3)
        def _():
            loaded(3)
            attend(layer, 2, 5)

        @pl.when(b == 4)
        def _():
            loaded(4)
            attend(layer, 5, 8)

        @pl.when(b == 5)
        def _():
            lower(lambda: start([save(1)]))
            loaded(5)
            attn_out(layer)
            lower(lambda: start([save(3), save(4)]))

        @pl.when((b >= 5) & (b <= 8))
        def _():
            ffn_in(layer, b - 5)

        @pl.when(b == 6)
        def _():
            loaded(6)
            wait([save_p(layer, p) for p in range(4, 8)])
            lower(lambda: wait([save(0), save(1)]))

        @pl.when(b == 7)
        def _():
            loaded(7)

        @pl.when(b == 8)
        def _():
            lower(lambda: start([save(2)]))
            loaded(8)

        @pl.when(b == 9)
        def _():
            loaded(9)

            @pl.when(layer == 1)
            def _():
                hand_wait(0, x, y_out, 0)

            ffn_out(layer, 0, 0)
            ffn_out(layer, 0, 1)
            lower(lambda: wait([save(3), save(4)]))

        @pl.when(b == 10)
        def _():
            loaded(10)
            ffn_out(layer, 1, 0)
            lower(lambda: wait([save(2)]))

        @pl.when(b == 11)
        def _():
            loaded(11)
            for top in (0, SEQ // 2):
                ffn_out(layer, 1, 1, slice(top, top + SEQ // 2))
                normalize(layer, 1, x, top, top + SEQ // 2)
            lower(lambda: start([save(5), save(6)]))
            hand_start(layer, x, y_out, layer)

    def step(t, _):
        if with_links:
            step_links(t)

        @pl.when(t == SETTLE)
        def _():
            settle()

        first = t - LOAD

        @pl.when((first >= 0) & (first < ITEMS))
        def _():
            if with_links:
                arrived(first)
            load(first)

        second = t - LOAD - 1

        @pl.when((second >= 0) & (second < ITEMS))
        def _():
            compute(second)

        return 0

    lax.fori_loop(0, ITEMS + LOAD + 1, step, 0)
    def fetch_final(half):
        return [
            final_part(8 + 2 * half + k, 8 + 2 * half + k, g, m_sem.at[(0, 12)[half] + 2 * k + g])
            for k in range(2)
            for g in range(2)
        ]

    def fetch_hidden():
        return [
            pltpu.make_async_copy(
                full.at[4 + j], m_hidden.at[:, :, :, :, j * LANES : (j + 1) * LANES], m_sem.at[4 + j]
            )
            for j in range(4)
        ]

    def fetch_attn():
        return [pltpu.make_async_copy(full.at[3], m_attn, m_sem.at[8])]

    def fetch_qkv():
        return [
            pltpu.make_async_copy(full.at[j], m_qkv.at[:, :, :, :, j * LANES : (j + 1) * LANES], m_sem.at[9 + j])
            for j in range(3)
        ]

    def fetch_norm(which):
        return [
            pltpu.make_async_copy(norm_save.at[which], norms.at[which], sem.at[2 * which]),
            pltpu.make_async_copy(inv_save.at[which], invs.at[which], sem.at[2 * which + 1]),
        ]

    def fetch_slope(half):
        return [pltpu.make_async_copy(slope_save.at[half], slope.at[half], sem.at[4 + half])]

    def fetch_heads():
        return [
            pltpu.make_async_copy(qkv_save, qkv, sem.at[6]),
            pltpu.make_async_copy(ctx_save, ctx, sem.at[7]),
        ]

    def fetch_probs(layer, group):
        return [pltpu.make_async_copy(prob_save.at[layer, group], probs.at[group % 2], p_sem.at[group % 2])]

    start(fetch_probs(1, 0) + fetch_probs(1, 1))
    take_grad.wait()

    def column_sum(values):
        return jnp.sum(values.astype(jnp.float32), 0, keepdims=True)

    def norm_back(layer, which, upstream_of, first=0, last=SEQ):
        gain = vec[layer, 8 + which : 9 + which, :]
        total = jnp.zeros((1, LANES), jnp.float32)
        for r in range(first, last, 128):
            rows = slice(r, r + 128)
            upstream = upstream_of(rows) * gain
            normed = norms[which, rows, :].astype(jnp.float32)
            back = invs[which, rows, 0:1] * (
                upstream
                - jnp.mean(upstream, -1, keepdims=True)
                - normed * jnp.mean(upstream * normed, -1, keepdims=True)
            )
            acc[rows, :] = back
            low = back.astype(jnp.bfloat16)
            hid[rows, :] = low
            total = total + column_sum(low)
        return total

    def sum_copy(source, target, k, device):
        return pltpu.make_async_remote_copy(
            src_ref=source,
            dst_ref=target,
            send_sem=sum_send.at[k],
            recv_sem=sum_recv.at[k],
            device_id=device,
            device_id_type=MESH,
        )

    def spread_heads(target, where, group, heads):
        for row in range(2):
            for k in range(2):
                at = (2 * group + k) * 128
                target[where, row : row + 1, at : at + 128] = heads[2 * row + k : 2 * row + k + 1, :]

    def core_sums():
        return [sum_copy(layer_sums.at[1 - sec], got_core, 0, dev_core)]

    def plane_sums():
        return [sum_copy(part_core, got_plane.at[k], 1 + k, device) for k, device in enumerate(in_plane)]

    def z_sums():
        return [sum_copy(part_plane, got_z.at[k], 4 + k, device) for k, device in enumerate(along_z)]

    def begin_early():
        layer_sums[0, 0:2, :] = jnp.zeros((2, LANES), jnp.float32)
        for group in range(GROUPS):
            spread_heads(layer_sums, 1, group, head_sums[1, group])
        start(core_sums())

    def early_sums(k):
        @pl.when(k == 0)
        def _():
            wait(core_sums())
            part_core[...] = layer_sums[sec] + got_core[...]
            start(plane_sums())

        @pl.when(k == 2)
        def _():
            wait(plane_sums())
            part_plane[...] = part_core[...] + (got_plane[0] + got_plane[1]) + got_plane[2]
            start(z_sums())

    def end_early():
        wait(z_sums())
        sums[0] = part_plane[...] + (got_z[0] + got_z[1]) + got_z[2]

    def late_send(group):
        own = 16 * sec + lax.axis_index("dp")
        got_late[group, own] = head_sums[0, group]

        def one(k, _):
            sum_late(group, own, (0, (lax.axis_index("dp") + k) % 16)).start()
            return 0

        lax.fori_loop(1, 16, one, 0)

        @pl.when(sec == 1)
        def _():
            sum_late(group, own, dev_core).start()

    def sum_late(group, slot, device):
        return pltpu.make_async_remote_copy(
            src_ref=head_sums.at[0, group],
            dst_ref=got_late.at[group, slot],
            send_sem=late_sent.at[group],
            recv_sem=late_got.at[group],
            device_id=device,
            device_id_type=MESH,
        )

    def end_late():
        def many(group, count):
            several = got_late.at[group, pl.ds(0, count)]
            return pltpu.make_async_remote_copy(
                src_ref=several,
                dst_ref=several,
                send_sem=late_sent.at[group],
                recv_sem=late_got.at[group],
                device_id=dev_core,
                device_id_type=MESH,
            )

        for group in range(GROUPS):
            for core in range(2):

                @pl.when(sec == core)
                def _():
                    many(group, 15 + core).wait_send()
                    if core == 0:
                        many(group, 31).wait_recv()
                        spread_heads(sums, 0, group, jnp.sum(got_late[group], 0))

    def one_layer(s, _):
        layer = 1 - s

        def prefetch(copies):
            @pl.when(s == 0)
            def _():
                start(copies)

        def fetched(copies):
            @pl.when(s == 1)
            def _():
                wait(copies)

        fetched(fetch_norm(1) + fetch_final(0) + fetch_slope(0) + fetch_final(1) + fetch_slope(1))
        fetched(fetch_hidden() + fetch_norm(0) + fetch_attn())
        layer_sums[layer, 7:8, :] = norm_back(layer, 1, lambda rows: grad[rows, :].astype(jnp.float32))
        for half in range(2):
            for n in range(0, 2048, TILE):
                chip = n // 128
                block = m_final[half, chip // 4, (chip // 2) % 2].reshape(TILE, LANES)
                back = dot_nt(hid[...], block) * slope[half, :, n : n + TILE].astype(jnp.float32)
                low = back.astype(jnp.bfloat16)
                total = column_sum(low)
                for k in range(2):
                    at = (chip + k) * 256 + half * 128
                    part = slice(k * 128, (k + 1) * 128)
                    act[at // 2048, :, at % 2048 : at % 2048 + 128] = low[:, part]
                    layer_sums[layer, 3 + at // LANES : 4 + at // LANES, at % LANES : at % LANES + 128] = total[:, part]
        prefetch(fetch_norm(1) + fetch_final(0) + fetch_slope(0) + fetch_final(1) + fetch_slope(1))

        @pl.when(s == 1)
        def _():
            hand_wait(3, grad, grad_out, 1)

        total = jnp.zeros((1, LANES), jnp.float32)
        for top in (0, SEQ // 2):
            rows = slice(top, top + SEQ // 2)
            for n in range(0, LANES, TILE):
                block = m_hidden[n // TILE].reshape(TILE, 4 * LANES)
                acc[rows, n : n + TILE] += dot_nt(act[0, rows], block[:, : 2 * LANES]) + dot_nt(
                    act[1, rows], block[:, 2 * LANES :]
                )
            total = total + norm_back(
                layer, 0, lambda at: acc[at, :].astype(jnp.bfloat16).astype(jnp.float32), top, top + SEQ // 2
            )
        layer_sums[layer, 2:3, :] = total
        for n in range(0, LANES, TILE):
            block = m_attn[n // TILE].reshape(TILE, LANES)
            grad[:, n : n + TILE] = dot_nt(hid[...], block).astype(jnp.bfloat16)
        prefetch(fetch_hidden() + fetch_norm(0) + fetch_attn())
        fetched(fetch_heads())

        def one_group(group, _):
            wait(fetch_probs(layer, group))
            for k in range(2):
                one_pair(2 * group + k, group, k, probs.at[group % 2, k])

            @pl.when(group < GROUPS - 2)
            def _():
                start(fetch_probs(layer, group + 2))

            if with_links:

                @pl.when(s == 1)
                def _():
                    late_send(group)
                    early_sums(group)

            return 0

        def one_pair(p, group, k, shares):
            at = pl.multiple_of(p * 128, 128)
            q, keys, v = (qkv[:, pl.ds(part * LANES + at, 128)] for part in range(3))
            upper = grad[:, pl.ds(at, 128)]
            product = upper.astype(jnp.float32) * ctx[:, pl.ds(at, 128)].astype(jnp.float32)
            q_t, k_t, upper_t = q.T, keys.T, upper.T
            grad_q, grad_k, grad_v = [], [], []
            for half in range(2):
                weights = shares[half]
                delta = jnp.sum(lane_half(product, half), -1, keepdims=True)
                scores = dot_nt(lane_half(upper, half), v)
                low = (weights.astype(jnp.float32) * (scores - delta)).astype(jnp.bfloat16)
                here = slice(half * HEAD_DIM, (half + 1) * HEAD_DIM)
                grad_q.append(dot_nt(k_t[here], low) * 0.125)
                grad_k.append(dot_nn(q_t[here], low))
                grad_v.append(dot_nn(upper_t[here], weights))
            for part, rows in enumerate((grad_q, grad_k, grad_v)):
                back = jnp.concatenate(rows, 0).astype(jnp.bfloat16).T
                act[part // 2, :, pl.ds((part % 2) * LANES + at, 128)] = back
                if part != 1:
                    head_sums[layer, group, part + k : part + k + 1, :] = column_sum(back)

        if with_links:

            @pl.when(s == 1)
            def _():
                begin_early()

        lax.fori_loop(0, GROUPS, one_group, 0)
        prefetch(fetch_heads() + fetch_probs(0, 0) + fetch_probs(0, 1))
        fetched(fetch_qkv())

        def columns_of(n):
            block = m_qkv[n // TILE].reshape(TILE, 3 * LANES)
            columns = slice(n, n + TILE)
            total = dot_nt(act[0], block[:, : 2 * LANES]) + dot_nt(act[1, :, :LANES], block[:, 2 * LANES :])
            grad[:, columns] = (acc[:, columns] + total).astype(jnp.bfloat16)

        if with_links:

            @pl.when(s == 0)
            def _():
                for n in range(0, LANES, TILE):
                    columns_of(n)

            @pl.when(s == 1)
            def _():
                for n in range(0, LANES, TILE):
                    columns_of(n)
                    if n == TILE:
                        end_early()
                end_late()

        else:
            for n in range(0, LANES, TILE):
                columns_of(n)
        prefetch(fetch_qkv())
        hand_start(2 + layer, grad, grad_out, layer)
        return 0

    lax.fori_loop(0, 2, one_layer, 0)
    hand_wait(1, x, y_out, 1)
    hand_wait(2, grad, grad_out, 0)
    if with_links:
        hand_arrived(sec, x, y_out)
        hand_arrived(2 + sec, grad, grad_out)
        end_links()
    else:
        for layer in range(2):
            for group in range(GROUPS):
                spread_heads(layer_sums, layer, group, head_sums[layer, group])
        sums[...] = layer_sums[...]


def both_layers(weights, tokens, cotangent, segments, lengths, vectors):
    with_links = len(weights) == 4
    low, wide_type = jnp.bfloat16, jnp.float32
    in_hbm = pl.BlockSpec(memory_space=pltpu.HBM)
    in_vmem = pl.BlockSpec(memory_space=pltpu.VMEM)
    in_smem = pl.BlockSpec(memory_space=pltpu.SMEM)
    shape = jax.ShapeDtypeStruct
    sums = (1, 8, LANES) if with_links else (2, 8, LANES)
    outs = [shape((ITEMS, 4, 2, 2, BLOCK, LANES), low)] if with_links else []
    outs += [
        pltpu.VMEM((2, SEQ, LANES), low),
        pltpu.VMEM((2, SEQ, LANES), low),
        shape(sums, wide_type),
        shape((2, GROUPS, 2, 2, SEQ, SEQ), low),
        shape((SEQ, 3 * LANES), low),
        shape((SEQ, LANES), low),
        shape((2, SEQ, 2 * LANES), low),
        shape((2, SEQ, LANES), low),
        shape((2, SEQ, 128), wide_type),
    ]
    out_specs = [in_hbm] * len(outs)
    for k in range(3):
        out_specs[k + with_links] = in_vmem
    dma = pltpu.SemaphoreType.DMA
    scratch = [
        pltpu.VMEM((SEQ, LANES), low),
        pltpu.VMEM((2, 16, LANES), wide_type),
        pltpu.VMEM((4, 2, 2, BLOCK, 3 * LANES), low),
        pltpu.VMEM((4, 2, 2, BLOCK, LANES), low),
        pltpu.VMEM((4, 2, 2, BLOCK, 4 * LANES), low),
        pltpu.VMEM((2, 4, 2, 2, 2 * BLOCK, LANES), low),
        pltpu.VMEM((SEQ, 3 * LANES), low),
        pltpu.VMEM((SEQ, LANES), low),
        pltpu.VMEM((SEQ, LANES), low),
        pltpu.VMEM((2, SEQ, 2 * LANES), low),
        pltpu.VMEM((2, SEQ, 2 * LANES), low),
        pltpu.VMEM((SEQ, LANES), wide_type),
        pltpu.VMEM((SEQ, SEQ), wide_type),
        pltpu.VMEM((2, 2, 2, SEQ, SEQ), low),
        pltpu.VMEM((2, SEQ, LANES), low),
        pltpu.VMEM((2, SEQ, 128), wide_type),
        pltpu.VMEM((SEQ, LANES), low),
        pltpu.VMEM((2, 8, LANES), wide_type),
        pltpu.VMEM((2, GROUPS, 8, 128), wide_type),
        dma((3,)),
        dma((PER_LAYER,)),
        dma((4,)),
        dma((7,)),
        dma((16,)),
        dma((8,)),
        dma((4,)),
    ]
    if with_links:
        specs = [in_hbm] * 6 + [in_vmem, in_smem] + [in_vmem] * 7
        scratch += [
            pltpu.VMEM((PER_LAYER, HALF, LANES), low),
            pltpu.VMEM((8, LANES), wide_type),
            pltpu.VMEM((3, 8, LANES), wide_type),
            pltpu.VMEM((3, 8, LANES), wide_type),
            pltpu.VMEM((GROUPS, 32, 8, 128), wide_type),
            pltpu.VMEM((8, LANES), wide_type),
            pltpu.VMEM((8, LANES), wide_type),
            dma((PER_LAYER,)),
            dma((PER_LAYER,)),
            dma((PER_LAYER,)),
            dma((PER_LAYER,)),
            dma((17,)),
            dma((17, ITEMS)),
            dma((2,)),
            dma((4,)),
            dma((4,)),
            dma((7,)),
            dma((7,)),
            dma((GROUPS,)),
            dma((GROUPS,)),
        ]
        params = pltpu.CompilerParams(collective_id=0, has_side_effects=True, vmem_limit_bytes=VMEM_LIMIT)
    else:
        specs = [in_hbm] * 3 + [in_vmem, in_smem, in_hbm]
        params = pltpu.CompilerParams(vmem_limit_bytes=VMEM_LIMIT)
    results = pl.pallas_call(
        partial(layers_kernel, with_links),
        out_shape=tuple(outs),
        in_specs=specs,
        out_specs=tuple(out_specs),
        scratch_shapes=scratch,
        compiler_params=params,
    )(*weights, tokens, cotangent, segments, lengths, *vectors)
    return results[1:4] if with_links else results[:3]


def gather(w_qkv, w_out, w_in, w_ffn_out):
    matrices = [lax.all_gather(w[0], "dp", axis=0, tiled=True) for w in (w_qkv, w_out, w_in, w_ffn_out)]
    qkv, attn, hidden, final = matrices
    blocks = [qkv[:, b * LANES : (b + 1) * LANES] for b in range(3)] + [attn]
    blocks += [hidden[:, b * LANES : (b + 1) * LANES] for b in range(4)]
    final = final.reshape(16, 2, 2, BLOCK, 2, 512).transpose(1, 4, 0, 3, 2, 5).reshape(4, 1024, LANES)
    own = jnp.concatenate([jnp.stack(blocks), final])
    return lax.all_gather(own, "section", axis=0, tiled=True).reshape(24, 4, 2, 2, BLOCK, LANES)


def on_device(
    tokens,
    segment_ids,
    row_lengths,
    w_qkv,
    w_out,
    w_in,
    w_ffn_out,
    bias_q,
    bias_v,
    bias_out,
    bias_in,
    bias_ffn_out,
    ln_gain,
    ln_shift,
    out_cotangent,
):
    weights = (w_qkv, w_out, w_in, w_ffn_out)
    vectors = (bias_q, bias_v, bias_out, bias_in, bias_ffn_out, ln_gain, ln_shift)
    data = (tokens, out_cotangent, segment_ids, row_lengths.T)
    if w_qkv.shape[1] == BLOCK:
        tops, grads, sums = both_layers(weights, *data, vectors)
        sums = sums[0]
    else:
        sec = lax.axis_index("section")
        wide_in, gains, shifts = bias_in.reshape(4, LANES), ln_gain[0], ln_shift[0]
        vec = jnp.concatenate(
            [bias_q, bias_v, bias_out, wide_in, bias_ffn_out, gains, shifts, jnp.zeros((4, LANES))]
        )
        vec = lax.all_gather(vec, "section", axis=0)
        tops, grads, sums = both_layers((gather(*weights),), *data, (vec,))

        def swap(array):
            return lax.ppermute(array, "section", [(0, 1), (1, 0)])

        def placed(both):
            got = swap(jnp.where(sec == 0, both[1], both[0]))
            return jnp.where(sec == 0, jnp.stack([both[0], got]), jnp.stack([got, both[1]]))

        tops, grads = placed(tops), placed(grads)
        sums = jnp.where(sec == 0, sums[0], sums[1]) + swap(jnp.where(sec == 0, sums[1], sums[0]))
        sums = lax.psum(sums, "dp")
    totals = (sums[0:1], sums[1:2], sums[2:3], sums[3:7].reshape(1, 4 * LANES), sums[7:8])
    return (tops[None, :, None], grads[None, :, None]) + totals


def solution(mesh):
    placed = (
        P(None, "dp", None, None),
        P(None, "dp", None),
        P(None, "dp"),
        P("section", "dp", None),
        P("section", "dp", None),
        P("section", "dp", None),
        P("section", "dp", None),
        P("section", None),
        P("section", None),
        P("section", None),
        P("section", None),
        P("section", None),
        P("section", None, None),
        P("section", None, None),
        P(None, "dp", None, None),
    )
    return jax.shard_map(
        on_device,
        mesh=mesh,
        in_specs=placed,
        out_specs=(
            P("section", None, "dp", None, None),
            P("section", None, "dp", None, None),
            P("section", None),
            P("section", None),
            P("section", None),
            P("section", None),
            P("section", None),
        ),
        check_vma=False,
    )
```
